128 devices in a mesh: rep: 2 (over core), exp: 64 (over y, x, z).
Axes of the slice: x: 4, y: 4, z: 4, core: 2. Of those that a mesh axis runs over, the one named last changes fastest.
Arguments:
- tokens: bfloat16 [16384, 1024], P(('rep', 'exp')), may hold values from -6 to 6
- hash_ids: int32 [16384, 1], P(('rep', 'exp')), may hold values from 0 to 63; in each aligned block of 128 rows (0 to 127, 128 to 255, ...) at most 8 rows name the same one
- doc_lengths: int32 [128, 4], P(('rep', 'exp')), may hold values from 1 to 64, 128 in all within a row
- w_query: bfloat16 [1024, 1024], P(('rep', 'exp')), may hold values from -0.1875 to 0.1875
- w_key: bfloat16 [1024, 1024], P(('rep', 'exp')), may hold values from -0.1875 to 0.1875
- w_value: bfloat16 [1024, 1024], P(('rep', 'exp')), may hold values from -0.1875 to 0.1875
- w_output: bfloat16 [1024, 1024], P(('rep', 'exp')), may hold values from -0.5 to 0.5
- norm1_gain: bfloat16 [1024], P(('rep', 'exp')), may hold values from 0.5 to 1.5
- norm1_bias: bfloat16 [1024], P(('rep', 'exp')), may hold values from -1 to 1
- norm2_gain: bfloat16 [1024], P(('rep', 'exp')), may hold values from 0.5 to 1.5
- norm2_bias: bfloat16 [1024], P(('rep', 'exp')), may hold values from -1 to 1
- expert_in: bfloat16 [64, 1024, 4096], P('exp', None, 'rep'), may hold values from -0.1875 to 0.1875
- expert_out: bfloat16 [64, 4096, 1024], P('exp', 'rep'), may hold values from -0.09375 to 0.09375
- load_average: float32 [64], replicated, may hold values from 64 to 1024
- out_grad: bfloat16 [16384, 1024], P(('rep', 'exp')), may hold values from -6 to 6
Outputs:
- output: bfloat16 [16384, 1024], P(('rep', 'exp'))
- input_grad: float32 [16384, 1024], P(('rep', 'exp'))
- w_query_grad: float32 [1024, 1024], P(('rep', 'exp'))
- w_key_grad: float32 [1024, 1024], P(('rep', 'exp'))
- w_value_grad: float32 [1024, 1024], P(('rep', 'exp'))
- w_output_grad: float32 [1024, 1024], P(('rep', 'exp'))
- norm1_gain_grad: float32 [1024], P(('rep', 'exp'))
- norm1_bias_grad: float32 [1024], P(('rep', 'exp'))
- norm2_gain_grad: float32 [1024], P(('rep', 'exp'))
- norm2_bias_grad: float32 [1024], P(('rep', 'exp'))
- expert_in_grad: float32 [64, 1024, 4096], P('exp', None, 'rep')
- expert_out_grad: float32 [64, 4096, 1024], P('exp', 'rep')
- counts: int32 [64], replicated
- new_average: float32 [64], replicated
The draws below stay inside these ranges and needn't reach their ends.
Inputs may be any that keep to these rules, and one draw needn't show every extreme that they name: `hash_ids`: in each aligned block of 128 rows (one device's tokens) no expert is named by more than 8 rows, a bound that some block reaches. `doc_lengths`: each row sums to 128; its largest entry is exactly 64.
All inputs are finite; a program needn't handle non-finite values.
Results may differ from the reference program's by a relative error of at most 0.012.
Values may be sent and summed in bfloat16 or wider, within the bound.
No kernel may reach another device: no remote copies, remote signals or barrier semaphores. Data moves between devices by JAX's collectives and lax.ppermute only.
A program may use at most 192 MiB of HBM per device.

```python
import math
import jax
import jax.numpy as jnp
import numpy as np
from jax import lax

D = 1024
HEADS = 16
HEAD_DIM = 64
FF = 4096
TOK_DEV = 128
DOCS = 4
EXPERTS = 64
CAP = 8
TOKENS = 16384
DEVICES = 128


def levels(rng, shape, cuts, low, top_value):
    def one(axis_at, blocks):
        steps = jax.random.uniform(jax.random.fold_in(jax.random.fold_in(rng, 6), axis_at), (blocks,), jnp.float32, low / len(cuts), top_value / len(cuts))
        return jnp.repeat(jnp.exp(steps), shape[axis_at] // blocks).reshape((-1,) + (1,) * (len(shape) - axis_at - 1))

    loudness = one(*cuts[0])
    for cut in cuts[1:]:
        loudness = loudness * one(*cut)
    return loudness


def length_profile(number_of, total, reach, lean):
    portions = [(1 << 20) // math.isqrt(standing ** lean) + 1 for standing in range(2, number_of + 1)]
    spare, given = total - reach - (number_of - 1), [1] * (number_of - 1)
    while spare > 0:
        movable = [i for i in range(number_of - 1) if given[i] < reach]
        pool, budget = sum([portions[i] for i in movable]), spare
        for i in movable:
            extra = min(reach - given[i], max(1, budget * portions[i] // pool), spare)
            given[i] = given[i] + extra
            spare = spare - extra
    return np.array([reach] + given)


def uneven(rng, amount, total, bound, skew):
    if amount == 2:
        one = jax.random.randint(rng, (), max(1, total - bound), min(bound, total - 1) + 1)
        return jnp.stack([one, total - one])
    sizes = jnp.asarray(length_profile(amount, total, bound, skew), jnp.int32)
    couples = (amount - 1) // 2
    giver, sink = sizes[1:1 + 2 * couples:2], sizes[2:2 + 2 * couples:2]
    slack = jnp.minimum(giver - 1, bound - sink)
    moved = jax.random.randint(jax.random.fold_in(rng, 1), (couples,), 0, 1 << 20) % (slack + 1)
    sizes = sizes.at[1:1 + 2 * couples:2].set(giver - moved).at[2:2 + 2 * couples:2].set(sink + moved)
    return sizes[jax.random.permutation(jax.random.fold_in(rng, 2), amount)]


def assign_block(key, own, number, rows, count, top, limit, lean):
    sequence = jax.random.permutation(key, count)
    packed, common = portions_of(count, rows * top, limit, lean, True), portions_of(count, rows * top, limit, lean, False)
    places = jnp.arange(count)

    def named(lengths, turn):
        used = int((lengths > 0).sum())
        fixed = max(1, used // 4)
        shifted = fixed + (places - fixed + turn * (used - fixed)) % max(1, count - fixed)
        return jnp.zeros((count,), jnp.int32).at[sequence[jnp.where(places < fixed, places, shifted)]].set(jnp.asarray(lengths, jnp.int32))

    lengths = jnp.where(number % 4 == 0, named(packed, number // 4), named(common, number - number // 4 - 1))
    mixed = jax.random.permutation(jax.random.fold_in(own, 3), count)
    source_of, sink = mixed[0:count // 2 * 2:2], mixed[1:count // 2 * 2:2]
    margin = jnp.minimum(lengths[source_of] - 1, limit - lengths[sink]) // 2
    margin = jnp.where((source_of == sequence[0]) | (sink == sequence[0]) | (lengths[sink] == 0), 0, jnp.maximum(margin, 0))
    shifted = jax.random.randint(jax.random.fold_in(own, 4), (count // 2,), 0, 1 << 20) % (margin + 1)
    lengths = lengths.at[source_of].add(-shifted).at[sink].add(shifted)
    members = jnp.searchsorted(jnp.cumsum(lengths), jnp.arange(rows * top), side="right").astype(jnp.int32)
    listing = members.reshape(top, rows).T
    listing = listing[jax.random.permutation(jax.random.fold_in(own, 1), rows)]
    turn = jax.random.randint(jax.random.fold_in(own, 2), (rows, 1), 0, top)
    return jnp.take_along_axis(listing, (jnp.arange(top)[None, :] + turn) % top, axis=1)


def portions_of(amount, total, most, lean, full):
    portions = [(1 << 20) // math.isqrt(grade ** lean) + 1 for grade in range(1, amount + 1)]
    largest = most if full else min(most, max(-(-total // amount), total * portions[0] // sum(portions)))
    least = 1 if total - largest >= amount - 1 else 0
    given, spare = [largest] + [least] * (amount - 1), total - largest - least * (amount - 1)
    while spare > 0:
        movable = [i for i in range(1, amount) if given[i] < largest] or [i for i in range(1, amount) if given[i] < most]
        whole, remaining = sum([portions[i] for i in movable]), spare
        for i in movable:
            extra = min(most - given[i], max(1, remaining * portions[i] // whole), spare)
            given[i] = given[i] + extra
            spare = spare - extra
    return np.array(given)


def noise(own_key, extent, width, bound, split=(), held_as=jnp.bfloat16):
    level = levels(own_key, extent, split, -0.22, 0.18) if split else 1.0
    values = jax.random.normal(own_key, extent, jnp.float32) * width * level
    return jnp.minimum(jnp.maximum(values, -bound), bound).astype(held_as)


def setup_inputs(seed: int = 0) -> dict:
    key_of = jax.random.split(jax.random.key(seed), 16)
    tokens = noise(key_of[0], (TOKENS, D), 1.0, 6.0, ((0, 128),))
    hash_ids_keys = jax.random.split(jax.random.fold_in(key_of[1], 1), TOKENS // TOK_DEV)
    hash_ids_turns = jax.random.permutation(jax.random.fold_in(key_of[1], 3), TOKENS // TOK_DEV)
    hash_ids = jax.vmap(lambda own, number: assign_block(jax.random.fold_in(key_of[1], 2), own, number, TOK_DEV, EXPERTS, 1, CAP, 2))(hash_ids_keys, hash_ids_turns).reshape((TOKENS, 1))
    doc_lengths = jax.vmap(lambda own: uneven(own, DOCS, TOK_DEV, TOK_DEV // 2, 2))(jax.random.split(key_of[2], DEVICES)).reshape((DEVICES, DOCS)).astype(jnp.int32)
    w_query = noise(key_of[3], (D, D), D ** -0.5, 0.1875, ((0, 128),))
    w_key = noise(key_of[4], (D, D), D ** -0.5, 0.1875, ((0, 128),))
    w_value = noise(key_of[5], (D, D), D ** -0.5, 0.1875, ((0, 128),))
    w_output = noise(key_of[6], (D, D), (D // 8) ** -0.5, 0.5, ((0, 128),))
    norm1_gain = jnp.clip(1.0 + 0.1 * jax.random.normal(key_of[7], (D,), jnp.float32), 0.5, 1.5).astype(jnp.bfloat16)
    norm1_bias = noise(key_of[8], (D,), 0.2, 1.0, ((0, 128),))
    norm2_gain = jnp.clip(1.0 + 0.1 * jax.random.normal(key_of[9], (D,), jnp.float32), 0.5, 1.5).astype(jnp.bfloat16)
    norm2_bias = noise(key_of[10], (D,), 0.2, 1.0, ((0, 128),))
    expert_in = noise(key_of[11], (EXPERTS, D, FF), D ** -0.5, 0.1875, ((0, 64), (2, 2)))
    expert_out = noise(key_of[12], (EXPERTS, FF, D), FF ** -0.5, 0.09375, ((0, 64), (1, 2)))
    load_average = jnp.clip(jnp.exp(jax.random.uniform(key_of[13], (EXPERTS,), jnp.float32, math.log(64.0), math.log(1024.0))), 64.0, 1024.0)
    out_grad = noise(key_of[14], (TOKENS, D), 1.0, 6.0, ((0, 128),))
    return dict(tokens=tokens, hash_ids=hash_ids, doc_lengths=doc_lengths, w_query=w_query, w_key=w_key, w_value=w_value, w_output=w_output, norm1_gain=norm1_gain, norm1_bias=norm1_bias, norm2_gain=norm2_gain, norm2_bias=norm2_bias, expert_in=expert_in, expert_out=expert_out, load_average=load_average, out_grad=out_grad)


HIGH = lax.Precision.HIGHEST
EPSILON = 1e-05
ROW_BLOCK = 128

@jax.custom_vjp
def low(v):
    return lax.optimization_barrier(v.astype(jnp.bfloat16)).astype(jnp.float32)

@jax.custom_vjp
def low_back(v):
    return v

def low_keep(v):
    return (low(v), None)

def low_pass(kept, grad):
    return (grad,)

def back_keep(v):
    return (v, None)

def back_low(kept, grad):
    return (low(grad),)
low.defvjp(low_keep, low_pass)
low_back.defvjp(back_keep, back_low)

def layer_norm(values, gain, shift):
    center = values - lax.optimization_barrier(jnp.mean(values, axis=-1, keepdims=True))
    spread = lax.optimization_barrier(jnp.mean(center * center, axis=-1, keepdims=True))
    return center * lax.rsqrt(spread + EPSILON) * gain + shift

def expert_block(block, weight_in, weight_out):
    pre = low_back(jnp.dot(block, weight_in, precision=HIGH))
    act = low(jax.nn.gelu(pre))
    return low(low_back(jnp.dot(act, weight_out, precision=HIGH)))

def skip_block(block, weight_in, weight_out):
    return jnp.zeros_like(block)

def forward(inputs, w_query, w_key, w_value, w_output, gain_one, bias_one, gain_two, bias_two, expert_in, expert_out, allowed, expert_ids, rank, block_count):
    group = 16
    scale = HEAD_DIM ** (-0.5)
    normed_low = low(layer_norm(inputs, gain_one, bias_one))

    def project(weight):
        made = low(low_back(jnp.dot(normed_low, weight, precision=HIGH)))
        return made.reshape(DEVICES // group, group, TOK_DEV, HEADS, HEAD_DIM)
    queries, keys, values = (project(w_query), project(w_key), project(w_value))

    def attend(pieces):
        query_block, key_block, value_block, mask_block = pieces
        raw = jnp.einsum('gqhd,gkhd->ghqk', query_block, key_block, precision=HIGH)
        scores = low_back(raw * scale)
        scores = jnp.where(mask_block[:, None], scores, -1e+30)
        probs = low(jax.nn.softmax(scores, axis=-1))
        return jnp.einsum('ghqk,gkhd->gqhd', probs, value_block, precision=HIGH)
    attended = lax.map(jax.checkpoint(attend), (queries, keys, values, allowed))
    attended = low(low_back(attended.reshape(TOKENS, D)))
    branch = low_back(jnp.dot(attended, w_output, precision=HIGH))
    hidden_one = inputs + branch
    normed_two = low(low_back(layer_norm(hidden_one, gain_two, bias_two)))
    block_total = -(-(DEVICES * CAP) // ROW_BLOCK)
    buffer = jnp.zeros((EXPERTS, block_total * ROW_BLOCK, D), jnp.float32)
    buffer = buffer.at[expert_ids, rank].set(normed_two)

    def expert_work(rows_all, weight_in, weight_out, used):
        results = []
        for index in range(block_total):
            block = rows_all[index * ROW_BLOCK:(index + 1) * ROW_BLOCK]
            results.append(lax.cond(index < used, expert_block, skip_block, block, weight_in, weight_out))
        return jnp.concatenate(results, axis=0)
    checked = jax.checkpoint(expert_work)

    def expert_step(carry, pieces):
        rows_all, weight_in, weight_out, used = pieces
        return (carry, checked(rows_all, weight_in, weight_out, used))
    _, expert_results = lax.scan(expert_step, jnp.zeros((), jnp.float32), (buffer, expert_in, expert_out, block_count))
    return hidden_one + expert_results[expert_ids, rank]

def reference(tokens, hash_ids, doc_lengths, w_query, w_key, w_value, w_output, norm1_gain, norm1_bias, norm2_gain, norm2_bias, expert_in, expert_out, load_average, out_grad):
    group = 16
    position = jnp.arange(TOK_DEV).astype(jnp.int32)
    ends = jnp.cumsum(doc_lengths, axis=1).astype(jnp.int32)
    segment = lax.optimization_barrier(jnp.sum((position[None, :, None] >= ends[:, None, :]).astype(jnp.int32), axis=-1))
    allowed = (segment[:, :, None] == segment[:, None, :]) & (position[None, None, :] <= position[None, :, None])
    allowed = allowed.reshape(DEVICES // group, group, TOK_DEV, TOK_DEV)
    expert_ids = hash_ids[:, 0].astype(jnp.int32)
    choose = (expert_ids[:, None] == jnp.arange(EXPERTS).astype(jnp.int32)[None, :]).astype(jnp.int32)
    prior = jnp.cumsum(choose, axis=0).astype(jnp.int32) - choose
    rank = lax.optimization_barrier(jnp.sum(prior * choose, axis=1)).astype(jnp.int32)
    counts = lax.optimization_barrier(jnp.sum(choose, axis=0)).astype(jnp.int32)
    block_count = ((counts + ROW_BLOCK - 1) // ROW_BLOCK).astype(jnp.int32)
    primals = tuple((item.astype(jnp.float32) for item in (tokens, w_query, w_key, w_value, w_output, norm1_gain, norm1_bias, norm2_gain, norm2_bias, expert_in, expert_out)))

    def whole(*params):
        return forward(*params, allowed, expert_ids, rank, block_count)
    result, pull = jax.vjp(whole, *primals)
    grads = pull(out_grad.astype(jnp.float32))
    new_average = 0.7 * load_average + 0.3 * counts.astype(jnp.float32)
    return (result.astype(jnp.bfloat16), grads[0], grads[1], grads[2], grads[3], grads[4], grads[5], grads[6], grads[7], grads[8], grads[9], grads[10], counts, new_average)
```

```python
import functools

import jax
import jax.numpy as jnp
from jax import lax
from jax.experimental import pallas as pl
from jax.experimental.pallas import tpu as pltpu
from jax.sharding import PartitionSpec as P

HEADS = 16
HEAD_DIM = 64
EPSILON = 1e-05
SWAP = [(0, 1), (1, 0)]
VMEM_LIMIT = 56 * 1024 * 1024


def layer_norm(values, gain, shift):
    center = values - jnp.mean(values, axis=-1, keepdims=True)
    spread = jnp.mean(center * center, axis=-1, keepdims=True)
    return center * lax.rsqrt(spread + EPSILON) * gain + shift


def norm_backward(values, gain, shift, upstream):
    _, norm_pull = jax.vjp(layer_norm, values, gain, shift)
    return norm_pull(upstream)


def swap(value):
    return lax.ppermute(value, "rep", SWAP)


def dot_nt(left, right):
    return lax.dot_general(
        left, right, (((1,), (1,)), ((), ())), preferred_element_type=jnp.float32
    )


def dot_tn(left, right):
    return lax.dot_general(
        left, right, (((0,), (0,)), ((), ())), preferred_element_type=jnp.float32
    )


def params():
    return pltpu.CompilerParams(
        dimension_semantics=("arbitrary",), vmem_limit_bytes=VMEM_LIMIT
    )


def act_grad_kernel(grad_ref, out_w_ref, made_ref):
    made_ref[...] = dot_nt(grad_ref[...], out_w_ref[...]).astype(jnp.bfloat16)


def act_grad_call(grads, weight_out, tile=512):
    rows, width = grads.shape
    hidden = weight_out.shape[0]
    return pl.pallas_call(
        act_grad_kernel,
        grid=(hidden // tile,),
        in_specs=[
            pl.BlockSpec((rows, width), lambda i: (0, 0)),
            pl.BlockSpec((tile, width), lambda i: (i, 0)),
        ],
        out_specs=pl.BlockSpec((rows, tile), lambda i: (0, i)),
        out_shape=jax.ShapeDtypeStruct((rows, hidden), jnp.bfloat16),
        compiler_params=params(),
        cost_estimate=pl.CostEstimate(
            flops=2 * rows * width * hidden, bytes_accessed=10 << 20, transcendentals=0
        ),
        name="act_grad",
    )(grads, weight_out)


def gelu_parts(pre):
    square = pre * pre
    turn = jnp.tanh(0.7978845608028654 * pre * (1.0 + 0.044715 * square))
    half = 0.5 * (1.0 + turn)
    slope = half + 0.5 * pre * (1.0 - turn * turn) * (
        0.7978845608028654 * (1.0 + 3.0 * 0.044715 * square)
    )
    return pre * half, slope


def expert_kernel(rows_ref, in_w_ref, up_ref, act_ref, pre_grad_ref, own_ref, other_ref, total):
    step = pl.program_id(0)
    pre = jnp.dot(rows_ref[...], in_w_ref[...], preferred_element_type=jnp.float32)
    act, slope = gelu_parts(pre)
    act_ref[...] = act.astype(jnp.bfloat16)
    pre_grad = (up_ref[...].astype(jnp.float32) * slope).astype(jnp.bfloat16)
    pre_grad_ref[...] = pre_grad
    made = dot_nt(pre_grad, in_w_ref[...])

    @pl.when(step == 0)
    def _():
        total[...] = made

    @pl.when(step > 0)
    def _():
        total[...] += made

    @pl.when(step == pl.num_programs(0) - 1)
    def _():
        half = own_ref.shape[0]
        own_ref[...] = total[:half, :]
        other_ref[...] = total[half:, :].astype(jnp.bfloat16)


def expert_call(rows_in, weight_in, act_up, tile=256):
    rows, width = rows_in.shape
    hidden = weight_in.shape[1]
    return pl.pallas_call(
        expert_kernel,
        grid=(hidden // tile,),
        in_specs=[
            pl.BlockSpec((rows, width), lambda i: (0, 0)),
            pl.BlockSpec((width, tile), lambda i: (0, i)),
            pl.BlockSpec((rows, tile), lambda i: (0, i)),
        ],
        out_specs=[
            pl.BlockSpec((rows, tile), lambda i: (0, i)),
            pl.BlockSpec((rows, tile), lambda i: (0, i)),
            pl.BlockSpec((rows // 2, width), lambda i: (0, 0)),
            pl.BlockSpec((rows // 2, width), lambda i: (0, 0)),
        ],
        out_shape=[
            jax.ShapeDtypeStruct((rows, hidden), jnp.bfloat16),
            jax.ShapeDtypeStruct((rows, hidden), jnp.bfloat16),
            jax.ShapeDtypeStruct((rows // 2, width), jnp.float32),
            jax.ShapeDtypeStruct((rows // 2, width), jnp.bfloat16),
        ],
        scratch_shapes=[pltpu.VMEM((rows, width), jnp.float32)],
        compiler_params=params(),
        cost_estimate=pl.CostEstimate(
            flops=4 * rows * width * hidden,
            bytes_accessed=24 << 20,
            transcendentals=rows * hidden,
        ),
        name="expert_pre",
    )(rows_in, weight_in, act_up)


def result_kernel(act_ref, out_w_ref, own_ref, other_ref, total):
    step = pl.program_id(0)
    made = jnp.dot(act_ref[...], out_w_ref[...], preferred_element_type=jnp.float32)

    @pl.when(step == 0)
    def _():
        total[...] = made

    @pl.when(step > 0)
    def _():
        total[...] += made

    @pl.when(step == pl.num_programs(0) - 1)
    def _():
        half = own_ref.shape[0]
        own_ref[...] = total[:half, :]
        other_ref[...] = total[half:, :].astype(jnp.bfloat16)


def result_call(act, weight_out, tile=512):
    rows, hidden = act.shape
    width = weight_out.shape[1]
    return pl.pallas_call(
        result_kernel,
        grid=(hidden // tile,),
        in_specs=[
            pl.BlockSpec((rows, tile), lambda i: (0, i)),
            pl.BlockSpec((tile, width), lambda i: (i, 0)),
        ],
        out_specs=[
            pl.BlockSpec((rows // 2, width), lambda i: (0, 0)),
            pl.BlockSpec((rows // 2, width), lambda i: (0, 0)),
        ],
        out_shape=[
            jax.ShapeDtypeStruct((rows // 2, width), jnp.float32),
            jax.ShapeDtypeStruct((rows // 2, width), jnp.bfloat16),
        ],
        scratch_shapes=[pltpu.VMEM((rows, width), jnp.float32)],
        compiler_params=params(),
        cost_estimate=pl.CostEstimate(
            flops=2 * rows * width * hidden, bytes_accessed=12 << 20, transcendentals=0
        ),
        name="expert_result",
    )(act, weight_out)


def weight_grad_kernel(left_ref, right_ref, made_ref):
    made_ref[...] = dot_tn(left_ref[...], right_ref[...])


def weight_grad_call(left, right, split_left, tile=512):
    rows = left.shape[0]
    high, wide = left.shape[1], right.shape[1]
    if split_left:
        grid = high // tile
        left_spec = pl.BlockSpec((rows, tile), lambda i: (0, i))
        right_spec = pl.BlockSpec((rows, wide), lambda i: (0, 0))
        made_spec = pl.BlockSpec((tile, wide), lambda i: (i, 0))
    else:
        grid = wide // tile
        left_spec = pl.BlockSpec((rows, high), lambda i: (0, 0))
        right_spec = pl.BlockSpec((rows, tile), lambda i: (0, i))
        made_spec = pl.BlockSpec((high, tile), lambda i: (0, i))
    return pl.pallas_call(
        weight_grad_kernel,
        grid=(grid,),
        in_specs=[left_spec, right_spec],
        out_specs=made_spec,
        out_shape=jax.ShapeDtypeStruct((high, wide), jnp.float32),
        compiler_params=params(),
        cost_estimate=pl.CostEstimate(
            flops=2 * rows * high * wide, bytes_accessed=14 << 20, transcendentals=0
        ),
        name="weight_grad",
    )(left, right)


def per_device(
    tokens,
    hash_ids,
    doc_lengths,
    w_query,
    w_key,
    w_value,
    w_output,
    norm1_gain,
    norm1_bias,
    norm2_gain,
    norm2_bias,
    expert_in,
    expert_out,
    load_average,
    out_grad,
):
    tok_count, width = tokens.shape
    experts_total = load_average.shape[0]
    groups = lax.axis_size("exp")
    devices = groups * lax.axis_size("rep")
    capacity = 8
    slots = experts_total * capacity
    scale = HEAD_DIM ** (-0.5)
    my_rep = lax.axis_index("rep")
    position = jnp.arange(tok_count, dtype=jnp.int32)

    expert_ids = hash_ids[:, 0]
    choose = (expert_ids[:, None] == jnp.arange(experts_total, dtype=jnp.int32)[None, :]).astype(
        jnp.float32
    )
    own_counts = jnp.sum(choose, axis=0)
    norms = jnp.stack([norm1_gain, norm1_bias, norm2_gain, norm2_bias], axis=1)
    extra = jnp.concatenate(
        [
            norms,
            own_counts.reshape(8, 8).astype(jnp.bfloat16),
            jnp.zeros((8, 116), jnp.bfloat16),
        ],
        axis=1,
    )
    packed = jnp.concatenate([w_query, w_key, w_value, w_output, extra], axis=1)
    gathered = lax.all_gather(packed, ("rep", "exp"), axis=0, tiled=True)

    earlier = (position[None, :] < position[:, None]).astype(jnp.float32)
    before = jnp.dot(earlier, choose, preferred_element_type=jnp.float32)
    rank = jnp.sum(before * choose, axis=1).astype(jnp.int32)
    slot = expert_ids * capacity + rank
    placing = (jnp.arange(slots, dtype=jnp.int32)[:, None] == slot[None, :]).astype(jnp.bfloat16)

    def send_rows(rows):
        outgoing = jnp.dot(placing, rows, preferred_element_type=jnp.float32).astype(jnp.bfloat16)
        outgoing = outgoing.reshape(groups, capacity, width)
        incoming = lax.all_to_all(outgoing, "exp", split_axis=0, concat_axis=0, tiled=True)
        incoming = incoming.reshape(slots, width)
        return jnp.concatenate([incoming, swap(incoming)], axis=0)

    def return_rows(own, other):
        rows = (own + swap(other).astype(jnp.float32)).astype(jnp.bfloat16)
        rows = rows.reshape(groups, capacity, width)
        back = lax.all_to_all(rows, "exp", split_axis=0, concat_axis=0, tiled=True)
        return jnp.einsum(
            "st,sd->td", placing, back.reshape(slots, width), preferred_element_type=jnp.float32
        )

    weight_in, weight_out = expert_in[0], expert_out[0]
    grad_rows = send_rows(out_grad)
    act_up = act_grad_call(grad_rows, weight_out)

    full_qkv = gathered[:, : 3 * width]
    full_output = gathered[:, 3 * width : 4 * width]
    tail = gathered[:, 4 * width :]
    gain_one, bias_one, gain_two, bias_two = (tail[:, i].astype(jnp.float32) for i in range(4))
    counts = (
        jnp.sum(tail[:, 4:12].reshape(devices, 8, 8).astype(jnp.float32), axis=0)
        .reshape(experts_total)
        .astype(jnp.int32)
    )
    new_average = 0.7 * load_average + 0.3 * counts.astype(jnp.float32)

    ends = jnp.cumsum(doc_lengths[0])
    segment = jnp.sum((position[:, None] >= ends[None, :]).astype(jnp.int32), axis=1)
    allowed = (segment[:, None] == segment[None, :]) & (position[None, :] <= position[:, None])
    inputs = tokens.astype(jnp.float32)
    normed_low = layer_norm(inputs, gain_one, bias_one).astype(jnp.bfloat16)
    qkv = jnp.dot(normed_low, full_qkv, preferred_element_type=jnp.float32).astype(jnp.bfloat16)
    queries, keys, values = (
        qkv[:, i * width : (i + 1) * width].reshape(tok_count, HEADS, HEAD_DIM) for i in range(3)
    )
    raw = jnp.einsum("qhd,khd->hqk", queries, keys, preferred_element_type=jnp.float32) * scale
    scores = jnp.where(allowed[None], raw, -1e30)
    top_score = jnp.max(scores, axis=-1, keepdims=True)
    raised = jnp.exp(scores - top_score)
    probs = raised / jnp.sum(raised, axis=-1, keepdims=True)
    probs_low = probs.astype(jnp.bfloat16)
    attended = jnp.einsum("hqk,khd->qhd", probs_low, values, preferred_element_type=jnp.float32)
    attended = attended.astype(jnp.bfloat16).reshape(tok_count, width)
    branch = jnp.dot(attended, full_output, preferred_element_type=jnp.float32)
    hidden_one = inputs + branch
    normed_two_low = layer_norm(hidden_one, gain_two, bias_two).astype(jnp.bfloat16)

    expert_rows = send_rows(normed_two_low)
    act, pre_grad, rows_grad, rows_grad_other = expert_call(expert_rows, weight_in, act_up)
    normed_two_grad = return_rows(rows_grad, rows_grad_other)
    expert_part = return_rows(*result_call(act, weight_out))
    output = (hidden_one + expert_part).astype(jnp.bfloat16)
    in_weight_grad = weight_grad_call(expert_rows, pre_grad, False)[None]
    out_weight_grad = weight_grad_call(act, grad_rows, True)[None]

    upstream = out_grad.astype(jnp.float32)
    hidden_part, gain_two_grad, bias_two_grad = norm_backward(
        hidden_one, gain_two, bias_two, normed_two_grad
    )
    hidden_grad = upstream + hidden_part
    branch_low = hidden_grad.astype(jnp.bfloat16)
    attended_grad = dot_nt(branch_low, full_output)
    attended_grad = attended_grad.astype(jnp.bfloat16).reshape(tok_count, HEADS, HEAD_DIM)
    probs_grad = jnp.einsum(
        "qhd,khd->hqk", attended_grad, values, preferred_element_type=jnp.float32
    )
    value_grad = jnp.einsum(
        "hqk,qhd->khd", probs_low, attended_grad, preferred_element_type=jnp.float32
    ).astype(jnp.bfloat16)
    score_grad = probs * (probs_grad - jnp.sum(probs * probs_grad, axis=-1, keepdims=True))
    score_grad = score_grad.astype(jnp.bfloat16)
    query_grad = (
        jnp.einsum("hqk,khd->qhd", score_grad, keys, preferred_element_type=jnp.float32) * scale
    ).astype(jnp.bfloat16)
    key_grad = (
        jnp.einsum("hqk,qhd->khd", score_grad, queries, preferred_element_type=jnp.float32) * scale
    ).astype(jnp.bfloat16)
    qkv_grad = jnp.concatenate(
        [piece.reshape(tok_count, width) for piece in (query_grad, key_grad, value_grad)], axis=1
    )
    normed_one_grad = dot_nt(qkv_grad, full_qkv)
    input_part, gain_one_grad, bias_one_grad = norm_backward(
        inputs, gain_one, bias_one, normed_one_grad
    )
    input_grad = hidden_grad + input_part

    half = width // 2

    def both(value):
        return jnp.concatenate([value, swap(value)], axis=0)

    def both_halves(value):
        halves = value.reshape(tok_count, 2, half)
        mine = lax.dynamic_index_in_dim(halves, my_rep, 1, keepdims=False)
        theirs = lax.dynamic_index_in_dim(halves, 1 - my_rep, 1, keepdims=False)
        return jnp.concatenate([mine, swap(theirs)], axis=0)

    qkv_weight_grad = dot_tn(both_halves(normed_low), both(qkv_grad))
    output_weight_grad = dot_tn(both_halves(attended), both(branch_low))
    norm_grads = jnp.stack([gain_one_grad, bias_one_grad, gain_two_grad, bias_two_grad], axis=1)
    norm_grads = norm_grads + swap(norm_grads)
    norm_grads = lax.dynamic_slice_in_dim(norm_grads, my_rep * half, half, axis=0)
    partial = jnp.concatenate(
        [
            qkv_weight_grad.astype(jnp.bfloat16),
            output_weight_grad.astype(jnp.bfloat16),
            norm_grads.astype(jnp.bfloat16),
            jnp.zeros((half, 124), jnp.bfloat16),
        ],
        axis=1,
    )
    partial = partial.reshape(groups, 8, 4 * width + 128)
    pieces = lax.all_to_all(partial, "exp", split_axis=0, concat_axis=0, tiled=True)
    summed = jnp.sum(pieces.astype(jnp.float32), axis=0)
    return (
        output,
        input_grad,
        summed[:, :width],
        summed[:, width : 2 * width],
        summed[:, 2 * width : 3 * width],
        summed[:, 3 * width : 4 * width],
        summed[:, 4 * width],
        summed[:, 4 * width + 1],
        summed[:, 4 * width + 2],
        summed[:, 4 * width + 3],
        in_weight_grad,
        out_weight_grad,
        counts,
        new_average,
    )


def solution(mesh):
    rows = P(("rep", "exp"), None)
    vector = P(("rep", "exp"))
    return jax.shard_map(
        per_device,
        mesh=mesh,
        in_specs=(rows,) * 7
        + (vector,) * 4
        + (P("exp", None, "rep"), P("exp", "rep", None), P(), rows),
        out_specs=(rows,) * 6
        + (vector,) * 4
        + (P("exp", None, "rep"), P("exp", "rep", None), P(), P()),
        check_vma=False,
    )
```

```python
import functools

import jax
import jax.numpy as jnp
from jax import lax
from jax.experimental import pallas as pl
from jax.experimental.pallas import tpu as pltpu
from jax.sharding import PartitionSpec as P

HEADS = 16
HEAD_DIM = 64
SCALE = HEAD_DIM ** (-0.5)
EPSILON = 1e-05
SWAP = [(0, 1), (1, 0)]
CAPACITY = 8
TOK = 128
WIDTH = 1024
HALF = WIDTH // 2
SLOTS = 512
FLOW = 3 * WIDTH
ALL = 4 * WIDTH
LENGTH = ALL + 128
PART = 2 * WIDTH + 128
BLOCKS = 4
SENT = PART + WIDTH
LINE = 4
LOW = jnp.bfloat16
FULL = jnp.float32
VMEM = pl.BlockSpec(memory_space=pltpu.VMEM)
SMEM = pl.BlockSpec(memory_space=pltpu.SMEM)
HBM = pl.BlockSpec(memory_space=pltpu.HBM)


def swap(value):
    return lax.ppermute(value, "rep", SWAP)


def along(value, stride):
    count = lax.axis_size("exp")
    return lax.ppermute(value, "exp", [(i, i ^ stride) for i in range(count)])


def exchange(value):
    return lax.all_to_all(value, "exp", split_axis=0, concat_axis=0, tiled=True)


def dot(left, right):
    return jnp.dot(left, right, preferred_element_type=FULL)


def dot_nt(left, right):
    return lax.dot_general(left, right, (((1,), (1,)), ((), ())), preferred_element_type=FULL)


def dot_tn(left, right):
    return lax.dot_general(left, right, (((0,), (0,)), ((), ())), preferred_element_type=FULL)


def kernel_call(
    body, specs, outs, scratch=(), copies=0, flops=0, moved=0, name=None, aliases=None
):
    shapes = [pltpu.VMEM(shape, dtype) for shape, dtype in scratch]
    if copies:
        shapes.append(pltpu.SemaphoreType.DMA((copies,)))
    return pl.pallas_call(
        body,
        in_specs=specs,
        out_specs=[spec for _, _, spec in outs],
        out_shape=[jax.ShapeDtypeStruct(shape, dtype) for shape, dtype, _ in outs],
        scratch_shapes=shapes,
        input_output_aliases=aliases or {},
        compiler_params=pltpu.CompilerParams(vmem_limit_bytes=62 << 20),
        cost_estimate=pl.CostEstimate(flops=flops, bytes_accessed=moved, transcendentals=0),
        name=name,
    )


def start(source, target, sem):
    copy = pltpu.make_async_copy(source, target, sem)
    copy.start()
    return copy


def lanes(first, size):
    return pl.ds(pl.multiple_of(first, size), size)


def centered(rows):
    center = rows - jnp.mean(rows, axis=-1, keepdims=True)
    spread = jnp.mean(center * center, axis=-1, keepdims=True)
    inverse = lax.rsqrt(spread + EPSILON)
    return center * inverse, inverse


def norm_pull(upstream, unit, inverse, gain):
    scaled = upstream * gain
    return inverse * (
        scaled
        - jnp.mean(scaled, axis=-1, keepdims=True)
        - unit * jnp.mean(scaled * unit, axis=-1, keepdims=True)
    )


def placed(slot, part):
    row_at = lax.broadcasted_iota(jnp.int32, (TOK, TOK), 0) + part * TOK
    return (row_at == slot).astype(LOW)


def pack_kernel(norms, ids, query, key, value, output, grad, packed, slot, *scratch):
    ids_in, rows, grad_in, lined, rows_made, sems = scratch
    loads = [start(ids, ids_in, sems.at[0])]
    for index, ref in enumerate((query, key, value, output)):
        loads.append(start(ref, rows.at[index], sems.at[1 + index]))
    grad_load = start(grad, grad_in, sems.at[5])
    tile = jnp.concatenate([norms[...].astype(FULL), jnp.zeros((TOK - 4, 8), FULL)], axis=0)
    tile = jnp.concatenate([tile, jnp.zeros((TOK, TOK - 8), FULL)], axis=1)
    loads[0].wait()
    row_at = lax.broadcasted_iota(jnp.int32, (TOK, TOK), 0)
    column_at = lax.broadcasted_iota(jnp.int32, (TOK, TOK), 1)
    by_column = jnp.broadcast_to(ids_in[...].astype(FULL), (TOK, TOK))
    before = (by_column.T == by_column) & (row_at < column_at)
    rank = jnp.sum(before.astype(FULL), axis=0, keepdims=True).astype(jnp.int32)
    target = ids_in[...] * CAPACITY + rank
    slot[...] = target
    chosen = (ids_in[...] == row_at - 64).astype(LOW)
    counts = dot_nt(jnp.ones((8, TOK), LOW), chosen)
    first = lax.broadcasted_iota(jnp.int32, (8, TOK), 0) == 0
    extra = tile.T[:8, :] + jnp.where(first, counts, 0.0)
    for load in loads[1:]:
        load.wait()
    low_half = [rows[index, :, :HALF].astype(FULL) for index in range(4)]
    high_half = [rows[index, :, HALF:].astype(FULL) for index in range(4)]
    copies = []
    for by_y in range(2):
        for by_x in range(2):
            made = []
            for z in range(LINE):
                pieces = [low_half[z % 2], high_half[by_y], low_half[2 + by_x]]
                pieces += [high_half[2 + z // 2], extra]
                made.append(jnp.concatenate(pieces, axis=1))
            variant = 2 * by_y + by_x
            lined[variant] = jnp.concatenate(made, axis=0).astype(LOW)
    for y in range(LINE):
        for x in range(LINE):
            index = y * LINE + x
            at = packed.at[pl.ds(index * 32, 32), pl.ds(0, PART)]
            copies.append(start(lined.at[y % 2 * 2 + x % 2], at, sems.at[6 + index]))
    grad_load.wait()
    for part in range(4):
        at = pl.ds(part * TOK, TOK)
        rows_made[at, :] = dot(placed(target, part), grad_in[...]).astype(LOW)
        goal = packed.at[at, pl.ds(PART, WIDTH)]
        copies.append(start(rows_made.at[at, :], goal, sems.at[22 + part]))
    for copy in copies:
        copy.wait()


def split_kernel(shares, *refs):
    targets, held, sems = refs[:BLOCKS], refs[BLOCKS], refs[BLOCKS + 1]
    loads, copies = [], []
    for index in range(BLOCKS):
        source = shares.at[:, pl.ds(index * HALF, HALF)]
        loads.append(start(source, held.at[index], sems.at[index]))
    for index, target in enumerate(targets):
        loads[index].wait()
        copies.append(start(held.at[index], target, sems.at[BLOCKS + index]))
    for copy in copies:
        copy.wait()


def attend_kernel(
    place, slot, lengths, shares, other_shares, *refs
):
    received, tokens = refs[: 2 * BLOCKS], refs[2 * BLOCKS]
    refs = refs[2 * BLOCKS + 1 :]
    outgoing_out, hidden_out, qkv_out, probs_out, normed_out, joined_out, norms_out = refs[:7]
    weights_out, extra_out, theirs_out, *scratch = refs[7:]
    tokens_in, extra, weights, norms, normed, qkv, raw, low, joined, hidden, outgoing, sems = scratch
    rep, bits = place[0, 0], [place[0, 1 + index] for index in range(BLOCKS)]
    halves = (lanes(rep * HALF, HALF), lanes((1 - rep) * HALF, HALF))
    tokens_load = start(tokens, tokens_in, sems.at[1])
    extra_loads, block_loads = [], []
    for side, ref in enumerate((shares, other_shares)):
        source = ref.at[:, pl.ds(2 * WIDTH, 128)]
        extra_loads.append(start(source, extra.at[halves[side], :], sems.at[18 + side]))
    for index in range(BLOCKS):
        matrix, cols = index // 2 * 2, pl.ds(index % 2 * HALF, HALF)
        block_loads.append([])
        for side, ref in enumerate((shares, other_shares)):
            source = ref.at[:, pl.ds(index * HALF, HALF)]
            target = weights.at[matrix + bits[index], halves[side], cols]
            sem = sems.at[20 + 4 * index + side]
            block_loads[index].append(start(source, target, sem))
            source = received[2 * index + side]
            target = weights.at[matrix + 1 - bits[index], halves[side], cols]
            sem = sems.at[22 + 4 * index + side]
            block_loads[index].append(start(source, target, sem))
    for load in extra_loads:
        load.wait()
    norms[...] = extra[...].astype(FULL).T[:8, :]
    copies = [start(norms, norms_out, sems.at[6]), start(extra, extra_out, sems.at[0])]
    tokens_load.wait()
    inputs = tokens_in[...].astype(FULL)
    unit, _ = centered(inputs)
    normed[...] = (unit * norms[0:1, :] + norms[1:2, :]).astype(LOW)
    copies.append(start(normed, normed_out, sems.at[7]))
    for index in range(3):
        if index % 2 == 0:
            for load in block_loads[index] + block_loads[index + 1]:
                load.wait()
            pair = pl.ds(index, 2)
            copies.append(start(weights.at[pair], weights_out.at[pair], sems.at[2 + index // 2]))
        qkv[index] = dot(normed[...], weights[index]).astype(LOW)
    copies.append(start(qkv, qkv_out, sems.at[8]))

    query_at = lax.broadcasted_iota(jnp.int32, (TOK, TOK), 0)
    key_at = lax.broadcasted_iota(jnp.int32, (TOK, TOK), 1)
    end = jnp.int32(0)
    query_doc = jnp.zeros((TOK, TOK), jnp.int32)
    key_doc = jnp.zeros((TOK, TOK), jnp.int32)
    for j in range(3):
        end = end + lengths[0, j]
        query_doc += (query_at >= end).astype(jnp.int32)
        key_doc += (key_at >= end).astype(jnp.int32)
    allowed = (query_doc == key_doc) & (key_at <= query_at)
    for first in range(0, HEADS, 8):
        heads = range(first, first + 8)
        for head in heads:
            at = slice(head * HEAD_DIM, (head + 1) * HEAD_DIM)
            raw[head] = dot_nt(qkv[0, :, at], qkv[1, :, at])
        for head in heads:
            scores = jnp.where(allowed, raw[head] * SCALE, -1e30)
            raised = jnp.exp(scores - jnp.max(scores, axis=-1, keepdims=True))
            chance = raised / jnp.sum(raised, axis=-1, keepdims=True)
            low[head] = chance.astype(LOW)
        block = pl.ds(first, 8)
        copies.append(start(low.at[block], probs_out.at[block], sems.at[9 + first // 8]))
        for head in range(first, first + 8, 2):
            made = []
            for one in (head, head + 1):
                made.append(dot(low[one], qkv[2, :, one * HEAD_DIM : (one + 1) * HEAD_DIM]))
            at = slice(head * HEAD_DIM, (head + 2) * HEAD_DIM)
            joined[:, at] = jnp.concatenate(made, axis=1).astype(LOW)
    for index, half in enumerate((rep, 1 - rep)):
        source = joined.at[:, lanes(half * HALF, HALF)]
        target = joined_out.at[:, pl.ds(index * HALF, HALF)]
        copies.append(start(source, target, sems.at[11 + index]))
    for index, ref in enumerate((normed, joined)):
        source = ref.at[:, lanes((1 - rep) * HALF, HALF)]
        target = theirs_out.at[:, pl.ds(index * HALF, HALF)]
        copies.append(start(source, target, sems.at[36 + index]))
    made = inputs + dot(joined[...], weights[3])
    hidden[...] = made
    copies.append(start(hidden, hidden_out, sems.at[13]))
    unit, _ = centered(made)
    second = (unit * norms[2:3, :] + norms[3:4, :]).astype(LOW)
    for part in range(4):
        rows = pl.ds(part * TOK, TOK)
        outgoing[rows, :] = dot(placed(slot[...], part), second).astype(LOW)
        copies.append(start(outgoing.at[rows, :], outgoing_out.at[rows, :], sems.at[14 + part]))
    for copy in copies:
        copy.wait()


def gelu_parts(pre):
    square = pre * pre
    turn = jnp.tanh(pre * (0.7978845608028654 + 0.035677408136300125 * square))
    half = 0.5 + 0.5 * turn
    slope = half + (0.5 - 0.5 * turn * turn) * (
        pre * (0.7978845608028654 + 0.10703222440890037 * square)
    )
    return pre * half, slope


def expert_kernel(rows_in, weight_own, weight_other, up_own, up_other, out, *refs):
    acts, flows, scratch = refs[:2], refs[2:4], refs[4:]
    rows, weight, up, act, flow, back, sems = scratch
    hidden = weight.shape[1]
    half = hidden // 2
    chunk = 512
    parts = hidden // chunk

    def load(j):
        cols = pl.ds(j * chunk, chunk)
        at = pl.ds(j * chunk % half, chunk)
        weight_in, up_in = (weight_own, up_own) if j * chunk < half else (weight_other, up_other)
        return (
            start(weight_in.at[:, at], weight.at[:, cols], sems.at[1 + j]),
            start(up_in.at[:, at], up.at[:, cols], sems.at[1 + parts + j]),
        )

    rows_load = start(rows_in, rows, sems.at[0])
    loads = [load(0), load(1)]
    rows_load.wait()
    copies = []
    for j in range(parts):
        cols = slice(j * chunk, (j + 1) * chunk)
        if j + 2 < parts:
            loads.append(load(j + 2))
        for copy in loads[j]:
            copy.wait()
        value, slope = gelu_parts(dot(rows[...], weight[:, cols]))
        act[:, cols] = value.astype(LOW)
        flow[:, cols] = (up[:, cols].astype(FULL) * slope).astype(LOW)
        at = pl.ds(j * chunk, chunk)
        side = j * chunk // half
        target_at = pl.ds(j * chunk % half, chunk)
        for index, (source, targets) in enumerate(((act, acts), (flow, flows))):
            sem = sems.at[1 + 2 * parts + 2 * j + index]
            copies.append(start(source.at[:, at], targets[side].at[:, target_at], sem))
    for index in range(2):
        block = slice(index * 256, (index + 1) * 256)
        back[block, :] = dot_nt(flow[block, :], weight[...]).astype(LOW)
        at = pl.ds(index * 256, 256)
        copies.append(start(back.at[at, :], out.at[at, :], sems.at[1 + 4 * parts + index]))
    for copy in copies:
        copy.wait()


def result_kernel(act_own, act_other, weight_own, weight_other, out, act, weight, made, sems):
    half = weight_own.shape[0]
    loads = [
        start(act_own, act.at[:, pl.ds(0, half)], sems.at[0]),
        start(act_other, act.at[:, pl.ds(half, half)], sems.at[5]),
        start(weight_own, weight.at[pl.ds(0, half), :], sems.at[1]),
        start(weight_other, weight.at[pl.ds(half, half), :], sems.at[2]),
    ]
    for load in loads:
        load.wait()
    copies = []
    for index in range(2):
        block = slice(index * 256, (index + 1) * 256)
        made[block, :] = dot(act[block, :], weight[...]).astype(LOW)
        at = pl.ds(index * 256, 256)
        target = out.at[at, pl.ds(PART, WIDTH)]
        copies.append(start(made.at[at, :], target, sems.at[3 + index]))
    for copy in copies:
        copy.wait()


def weight_grad_kernel(by_rows, at, first, second, streamed_first, streamed_second, made, held, sems):
    half = first.shape[0]
    cols = pl.ds(at, held.shape[1])

    @pl.when(pl.program_id(0) == 0)
    def _():
        loads = [
            start(first.at[:, cols], held.at[pl.ds(0, half), :], sems.at[0]),
            start(second.at[:, cols], held.at[pl.ds(half, half), :], sems.at[1]),
        ]
        for load in loads:
            load.wait()

    streamed = jnp.concatenate([streamed_first[...], streamed_second[...]], axis=0)
    made[...] = dot_tn(streamed, held[...]) if by_rows else dot_tn(held[...], streamed)


def weight_grad_call(held, at, streamed, by_rows, tile=256):
    rows, wide = streamed[0].shape
    width = WIDTH
    shape = (wide, width) if by_rows else (width, wide)
    block = (tile, width) if by_rows else (width, tile)
    return pl.pallas_call(
        functools.partial(weight_grad_kernel, by_rows, at),
        grid=(wide // tile,),
        in_specs=[HBM, HBM] + [pl.BlockSpec((rows, tile), lambda i: (0, i))] * 2,
        out_specs=pl.BlockSpec(block, (lambda i: (i, 0)) if by_rows else (lambda i: (0, i))),
        out_shape=jax.ShapeDtypeStruct(shape, FULL),
        scratch_shapes=[pltpu.VMEM((2 * rows, width), LOW), pltpu.SemaphoreType.DMA((2,))],
        compiler_params=pltpu.CompilerParams(
            dimension_semantics=("arbitrary",), vmem_limit_bytes=62 << 20
        ),
        cost_estimate=pl.CostEstimate(
            flops=4 * rows * wide * width, bytes_accessed=14 << 20, transcendentals=0
        ),
        name="weight_grad",
    )(*held, *streamed)


def attend_back_kernel(
    place, slot, norms, back, hidden, grad, full, qkv_in, probs_in, grad_out, flow_out,
    keep_out, near_out, side_out, gains, *scratch,
):
    hidden_in, grad_in, weight, qkv, probs, total, above, raw, low, flow, sems = scratch
    hidden_load = start(hidden, hidden_in, sems.at[4])
    grad_load = start(grad, grad_in, sems.at[5])
    weight_load = start(full.at[3], weight, sems.at[6])
    qkv_load = start(qkv_in, qkv, sems.at[7])
    probs_load = start(probs_in, probs, sems.at[8])
    upstream = jnp.zeros((TOK, WIDTH), FULL)
    for part in range(4):
        rows = back[part * TOK : (part + 1) * TOK, :]
        upstream = upstream + dot_tn(placed(slot[...], part), rows)
    hidden_load.wait()
    grad_load.wait()
    unit, inverse = centered(hidden_in[...])
    made = grad_in[...].astype(FULL) + norm_pull(upstream, unit, inverse, norms[2:3, :])
    total[...] = made
    copies = [start(total, grad_out, sems.at[9])]
    flow[:, FLOW:] = made.astype(LOW)
    gains[...] = jnp.zeros(gains.shape, FULL)
    gains[2:3, :] = jnp.sum(upstream * unit, axis=0, keepdims=True)
    gains[3:4, :] = jnp.sum(upstream, axis=0, keepdims=True)
    weight_load.wait()
    above[...] = dot_nt(flow[:, FLOW:], weight[...]).astype(LOW)
    qkv_load.wait()
    probs_load.wait()

    def head_of(part, head):
        return qkv[part, :, head * HEAD_DIM : (head + 1) * HEAD_DIM]

    def above_of(head):
        return above[:, head * HEAD_DIM : (head + 1) * HEAD_DIM]

    def store(part, first, pieces):
        at = part * WIDTH + first * HEAD_DIM
        flow[:, at : at + 2 * HEAD_DIM] = jnp.concatenate(pieces, axis=1).astype(LOW)

    for first in range(0, HEADS, 8):
        heads = range(first, first + 8)
        pairs = range(first, first + 8, 2)
        for head in heads:
            raw[head] = dot_nt(above_of(head), head_of(2, head))
        for head in pairs:
            store(2, head, [dot_tn(probs[h], above_of(h)) for h in (head, head + 1)])
        for head in heads:
            chance, pulled = probs[head].astype(FULL), raw[head]
            taken = jnp.sum(chance * pulled, axis=-1, keepdims=True)
            low[head] = (chance * (pulled - taken)).astype(LOW)
        for head in pairs:
            store(0, head, [dot(low[h], head_of(1, h)) * SCALE for h in (head, head + 1)])
            store(1, head, [dot_tn(low[h], head_of(0, h)) * SCALE for h in (head, head + 1)])
    by_z, by_x = place[0, 1], place[0, 3]
    for index, (target, first) in enumerate(
        (
            (keep_out.at[0], by_z),
            (keep_out.at[1], 2 + by_x),
            (near_out, 1 - by_z),
            (side_out, 3 - by_x),
        )
    ):
        source = flow.at[:, lanes(first * WIDTH, WIDTH)]
        copies.append(start(source, target, sems.at[10 + index]))
    copies.append(start(flow, flow_out, sems.at[14]))
    for copy in copies:
        copy.wait()


def left_kernel(place, normed, joined, other_halves, normed_out, joined_out, side_out, held, sems):
    mine = lanes(place[0, 0] * HALF, HALF)
    first, second = pl.ds(0, TOK), pl.ds(TOK, TOK)
    loads = [
        start(normed.at[:, mine], held.at[0, first, :], sems.at[0]),
        start(other_halves.at[:, pl.ds(0, HALF)], held.at[0, second, :], sems.at[1]),
        start(joined.at[:, pl.ds(0, HALF)], held.at[1, first, :], sems.at[2]),
        start(other_halves.at[:, pl.ds(HALF, HALF)], held.at[1, second, :], sems.at[3]),
    ]
    for load in loads:
        load.wait()
    copies = [
        start(held.at[0], normed_out, sems.at[4]),
        start(held.at[place[0, 3]], joined_out, sems.at[5]),
        start(held.at[1 - place[0, 3]], side_out, sems.at[6]),
    ]
    for copy in copies:
        copy.wait()


def weights_kernel(place, chip_near, chip_side, near_left, side_left, *refs):
    flows, full, extra, gains_in, other_gains_in, packed, out = refs[:6], *refs[6:12]
    left, right, weights, made, gains, sems = refs[12:]
    rep, by_z, by_x = place[0, 0], place[0, 1], place[0, 3]
    mine = lanes(rep * HALF, HALF)
    own, next_to = pl.ds(0, 2 * TOK), pl.ds(2 * TOK, 2 * TOK)
    keep, other_keep, near, other_near, side, other_side = flows
    loads = [[], []]
    for part, (kept, received) in enumerate(((0, (near, other_near)), (1, (side, other_side)))):
        sources = (
            (chip_near if part == 0 else chip_side, left.at[part, own, :]),
            (near_left if part == 0 else side_left, left.at[part, next_to, :]),
            (keep.at[kept], right.at[part, pl.ds(0, TOK), :]),
            (other_keep.at[kept], right.at[part, pl.ds(TOK, TOK), :]),
            (received[0], right.at[part, pl.ds(2 * TOK, TOK), :]),
            (received[1], right.at[part, pl.ds(3 * TOK, TOK), :]),
        )
        for index, (source, target) in enumerate(sources):
            loads[part].append(start(source, target, sems.at[6 * part + index]))
    chosen = (by_z, 2 + by_x)
    weight_loads = [
        start(full.at[chosen[part], mine, :], weights.at[part], sems.at[12 + part])
        for part in range(2)
    ]
    small = [
        start(extra.at[mine, :], made.at[:, pl.ds(2 * WIDTH, 128)], sems.at[14]),
        start(gains_in, gains.at[0], sems.at[15]),
        start(other_gains_in, gains.at[1], sems.at[16]),
    ]
    bias = jnp.zeros((HALF, 1), FULL)
    gain = jnp.zeros((HALF, 1), FULL)
    copies = []
    for part in range(2):
        for load in loads[part]:
            load.wait()
        value = dot_tn(left[part], right[part])
        cols = slice(part * WIDTH, (part + 1) * WIDTH)
        made[:, cols] = value.astype(LOW)
        at = pl.ds(part * WIDTH, WIDTH)
        copies.append(start(made.at[:, at], out.at[:, at], sems.at[17 + part]))
        weight_loads[part].wait()
        weight = weights[part].astype(FULL)
        total = jnp.sum(right[part].astype(FULL), axis=0, keepdims=True)
        bias_part = jnp.sum(weight * total, axis=1, keepdims=True)
        gain_part = jnp.sum(weight * value, axis=1, keepdims=True)
        if part == 1:
            bias_part = jnp.where(by_x == 0, bias_part, 0.0)
            gain_part = jnp.where(by_x == 0, gain_part, 0.0)
        bias = bias + bias_part
        gain = gain + gain_part
    for load in small:
        load.wait()
    params = made[:, 2 * WIDTH :].astype(FULL)
    gain = (gain - params[:, 1:2] * bias) / params[:, 0:1]
    columns = gains[0] + gains[1]
    columns = jnp.concatenate([columns, jnp.zeros((TOK - 8, WIDTH), FULL)], axis=0)
    turned = jnp.where(rep == 0, columns[:, :HALF], columns[:, HALF:]).T
    lane_at = lax.broadcasted_iota(jnp.int32, (HALF, 128), 1)
    tail = jnp.where(lane_at == 0, gain, jnp.where(lane_at == 1, bias, turned))
    made[:, 2 * WIDTH :] = tail.astype(LOW)
    at = pl.ds(2 * WIDTH, 128)
    copies.append(start(made.at[:, at], out.at[:, at], sems.at[19]))
    for copy in copies:
        copy.wait()


def input_kernel(norms, tokens, hidden_grad, flow, full, made_out, *scratch):
    tokens_in, grad_in, flow_in, weights, made, sems = scratch
    loads = [
        start(tokens, tokens_in, sems.at[0]),
        start(hidden_grad, grad_in, sems.at[1]),
        start(flow.at[:, pl.ds(0, FLOW)], flow_in, sems.at[2]),
    ]
    weight_loads = []
    for index in range(3):
        weight_loads.append(start(full.at[index], weights.at[index], sems.at[3 + index]))
    for load in loads:
        load.wait()
    upstream = jnp.zeros((TOK, WIDTH), FULL)
    for index in range(3):
        weight_loads[index].wait()
        cols = slice(index * WIDTH, (index + 1) * WIDTH)
        upstream = upstream + dot_nt(flow_in[:, cols], weights[index])
    unit, inverse = centered(tokens_in[...].astype(FULL))
    made[...] = grad_in[...] + norm_pull(upstream, unit, inverse, norms[0:1, :])
    start(made, made_out, sems.at[6]).wait()


def reduce_kernel(slot, pieces, hidden, query, key, value, output, result, *refs):
    norms, held, hidden_in, sems = refs[:4], *refs[4:]
    hidden_load = start(hidden, hidden_in, sems.at[4])
    loads = []
    for part in range(4):
        rows = pl.ds(part * TOK, TOK)
        loads.append(start(pieces.at[rows, :], held.at[rows, :], sems.at[part]))
    first = [jnp.zeros((8, WIDTH), FULL) for _ in range(2)]
    second = [jnp.zeros((8, WIDTH), FULL) for _ in range(2)]
    tail = jnp.zeros((8, 128), FULL)
    hidden_load.wait()
    made = hidden_in[...]
    for part in range(4):
        loads[part].wait()
        for pair in range(8):
            at = part * TOK + pair * 16
            rows = held[at : at + 16, :PART].astype(FULL)
            by_x = pair // 2 % 2
            for by_z in range(2):
                piece = rows[by_z * 8 : (by_z + 1) * 8, :]
                first[by_z] = first[by_z] + piece[:, :WIDTH]
                second[by_x] = second[by_x] + piece[:, WIDTH : 2 * WIDTH]
                tail = tail + piece[:, 2 * WIDTH :]
        at = slice(part * TOK, (part + 1) * TOK)
        made = made + dot_tn(placed(slot[...], part), held[at, PART:])
    result[...] = made.astype(LOW)
    for ref, total in zip((query, key, value, output), first + second):
        ref[...] = total
    tail = jnp.concatenate([tail, jnp.zeros((TOK - 8, 128), FULL)], axis=0).T
    for index, norm in enumerate(norms):
        norm[...] = tail[index : index + 1, :8]


def tied(*values):
    return lax.optimization_barrier(values)


def per_device(
    tokens,
    hash_ids,
    doc_lengths,
    w_query,
    w_key,
    w_value,
    w_output,
    norm1_gain,
    norm1_bias,
    norm2_gain,
    norm2_bias,
    expert_in,
    expert_out,
    load_average,
    out_grad,
):
    experts = load_average.shape[0]
    groups = lax.axis_size("exp")
    devices = 2 * groups
    rep = lax.axis_index("rep")
    at = lax.axis_index("exp")
    bits = [lax.rem(lax.div(at, step), 2) for step in (1, LINE * LINE, LINE, 2)]
    place = jnp.stack([rep, *bits]).astype(jnp.int32).reshape(1, 1 + BLOCKS)
    weight_in, weight_out = expert_in[0], expert_out[0]
    hidden = weight_in.shape[1]

    norm_params = jnp.concatenate([norm1_gain, norm1_bias, norm2_gain, norm2_bias]).reshape(4, 8)
    packed, slot = kernel_call(
        pack_kernel,
        [VMEM] + [HBM] * 6,
        [((SLOTS, SENT), LOW, HBM), ((1, TOK), jnp.int32, VMEM)],
        scratch=[
            ((1, TOK), jnp.int32),
            ((4, 8, WIDTH), LOW),
            ((TOK, WIDTH), LOW),
            ((4, 32, PART), LOW),
            ((SLOTS, WIDTH), LOW),
        ],
        copies=26,
        flops=2 * SLOTS * TOK * WIDTH,
        moved=6 << 20,
        name="pack",
    )(norm_params, hash_ids.reshape(1, TOK), w_query, w_key, w_value, w_output, out_grad)
    shares = exchange(packed.reshape(groups, 8, SENT)).reshape(SLOTS, SENT)
    weight_in_other, weight_out_other = swap(weight_in), swap(weight_out)
    shares, weight_in_other, weight_out_other = tied(shares, weight_in_other, weight_out_other)
    blocks = kernel_call(
        split_kernel,
        [HBM],
        [((SLOTS, HALF), LOW, HBM)] * BLOCKS,
        scratch=[((BLOCKS, SLOTS, HALF), LOW)],
        copies=2 * BLOCKS,
        moved=4 << 20,
        name="split",
    )(shares)
    blocks = [along(block, step) for block, step in zip(blocks, (1, LINE * LINE, LINE, 3))]
    other_shares = swap(shares)
    received = [one for block in blocks for one in (block, swap(block))]

    def send(rows):
        return exchange(rows.reshape(groups, CAPACITY, WIDTH)).reshape(SLOTS, WIDTH)

    outgoing, hidden_one, qkv, probs, normed, joined, norms, full, extra, theirs = kernel_call(
        attend_kernel,
        [SMEM, VMEM, SMEM] + [HBM] * (3 + 2 * BLOCKS),
        [
            ((SLOTS, WIDTH), LOW, HBM),
            ((TOK, WIDTH), FULL, HBM),
            ((3, TOK, WIDTH), LOW, HBM),
            ((HEADS, TOK, TOK), LOW, HBM),
            ((TOK, WIDTH), LOW, HBM),
            ((TOK, WIDTH), LOW, HBM),
            ((8, WIDTH), FULL, HBM),
            ((4, WIDTH, WIDTH), LOW, HBM),
            ((WIDTH, 128), LOW, HBM),
            ((TOK, WIDTH), LOW, HBM),
        ],
        scratch=[
            ((TOK, WIDTH), LOW),
            ((WIDTH, 128), LOW),
            ((4, WIDTH, WIDTH), LOW),
            ((8, WIDTH), FULL),
            ((TOK, WIDTH), LOW),
            ((3, TOK, WIDTH), LOW),
            ((HEADS, TOK, TOK), FULL),
            ((HEADS, TOK, TOK), LOW),
            ((TOK, WIDTH), LOW),
            ((TOK, WIDTH), FULL),
            ((SLOTS, WIDTH), LOW),
        ],
        copies=38,
        flops=2 * TOK * WIDTH * 5000,
        moved=12 << 20,
        name="attend",
    )(place, slot, doc_lengths, shares, other_shares, *received, tokens)

    grad_rows = shares[:, PART:]
    up_own = dot_nt(grad_rows, weight_out).astype(LOW)
    up_other = dot_nt(grad_rows, weight_out_other).astype(LOW)
    rows, up_own, up_other = tied(send(outgoing), up_own, up_other)
    other_halves = swap(theirs)
    chip_near, chip_side, side_sent = kernel_call(
        left_kernel,
        [SMEM] + [HBM] * 3,
        [((2 * TOK, HALF), LOW, HBM)] * 3,
        scratch=[((2, 2 * TOK, HALF), LOW)],
        copies=7,
        moved=1 << 20,
        name="left",
    )(place, normed, joined, other_halves)
    rows, chip_near, side_sent = tied(rows, chip_near, side_sent)
    back_rows, *acts_flows = kernel_call(
        expert_kernel,
        [HBM] * 5,
        [
            ((SLOTS, WIDTH), LOW, HBM),
        ]
        + [((SLOTS, hidden), LOW, HBM)] * 4,
        scratch=[
            ((SLOTS, WIDTH), LOW),
            ((WIDTH, 2 * hidden), LOW),
            ((SLOTS, 2 * hidden), LOW),
            ((SLOTS, 2 * hidden), LOW),
            ((SLOTS, 2 * hidden), LOW),
            ((SLOTS, WIDTH), LOW),
        ],
        copies=3 + 8 * (hidden // 512),
        flops=8 * SLOTS * WIDTH * hidden,
        moved=24 << 20,
        name="expert",
    )(rows, weight_in, weight_in_other, up_own, up_other)
    act, act_theirs, flow, flow_theirs = acts_flows
    back_rows, chip_near, side_sent = tied(back_rows, chip_near, side_sent)
    near_left = along(chip_near, 1)
    side_left = along(side_sent, LINE)
    back = send(back_rows)
    (result,) = kernel_call(
        result_kernel,
        [HBM] * 4,
        [((SLOTS, SENT), LOW, HBM)],
        scratch=[
            ((SLOTS, 2 * hidden), LOW),
            ((2 * hidden, WIDTH), LOW),
            ((SLOTS, WIDTH), LOW),
        ],
        copies=6,
        flops=4 * SLOTS * hidden * WIDTH,
        moved=14 << 20,
        name="result",
    )(act, act_theirs, weight_out, weight_out_other)
    act_other, flow_other, rows_other = swap(act_theirs), swap(flow_theirs), swap(rows)
    back, result, act_other, flow_other, rows_other, near_left, side_left = tied(
        back, result, act_other, flow_other, rows_other, near_left, side_left
    )

    hidden_grad, attend_flow, keep, near, side, gains = kernel_call(
        attend_back_kernel,
        [SMEM, VMEM, VMEM, VMEM] + [HBM] * 5,
        [
            ((TOK, WIDTH), FULL, HBM),
            ((TOK, ALL), LOW, HBM),
            ((2, TOK, WIDTH), LOW, HBM),
            ((TOK, WIDTH), LOW, HBM),
            ((TOK, WIDTH), LOW, HBM),
            ((8, WIDTH), FULL, VMEM),
        ],
        scratch=[
            ((TOK, WIDTH), FULL),
            ((TOK, WIDTH), LOW),
            ((WIDTH, WIDTH), LOW),
            ((3, TOK, WIDTH), LOW),
            ((HEADS, TOK, TOK), LOW),
            ((TOK, WIDTH), FULL),
            ((TOK, WIDTH), LOW),
            ((HEADS, TOK, TOK), FULL),
            ((HEADS, TOK, TOK), LOW),
            ((TOK, ALL), LOW),
        ],
        copies=15,
        flops=2 * TOK * WIDTH * 3000,
        moved=8 << 20,
        name="attend_back",
    )(place, slot, norms, back, hidden_one, out_grad, full, qkv, probs)
    near, side = along(near, 1), along(side, LINE)
    (weight_part,) = kernel_call(
        weights_kernel,
        [SMEM] + [HBM] * 15,
        [((SLOTS, SENT), LOW, HBM)],
        scratch=[
            ((2, 4 * TOK, HALF), LOW),
            ((2, 4 * TOK, WIDTH), LOW),
            ((2, HALF, WIDTH), LOW),
            ((HALF, PART), LOW),
            ((2, 8, WIDTH), FULL),
        ],
        copies=20,
        flops=8 * TOK * HALF * 2 * WIDTH,
        moved=10 << 20,
        name="weights",
        aliases={15: 0},
    )(
        place,
        chip_near,
        chip_side,
        near_left,
        side_left,
        keep,
        swap(keep),
        near,
        swap(near),
        side,
        swap(side),
        full,
        extra,
        gains,
        swap(gains),
        result,
    )
    pieces = exchange(weight_part.reshape(groups, 8, SENT)).reshape(SLOTS, SENT)

    act, flow, attend_flow, _ = tied(act, flow, attend_flow, weight_part)
    in_weight_grad = weight_grad_call((rows, rows_other), 0, (flow, flow_other), False)
    out_weight_grad = weight_grad_call((shares, other_shares), PART, (act, act_other), True)
    (input_grad,) = kernel_call(
        input_kernel,
        [VMEM] + [HBM] * 4,
        [((TOK, WIDTH), FULL, HBM)],
        scratch=[
            ((TOK, WIDTH), LOW),
            ((TOK, WIDTH), FULL),
            ((TOK, FLOW), LOW),
            ((3, WIDTH, WIDTH), LOW),
            ((TOK, WIDTH), FULL),
        ],
        copies=7,
        flops=2 * TOK * WIDTH * FLOW,
        moved=8 << 20,
        name="input_grad",
    )(norms, tokens, hidden_grad, attend_flow, full)
    tails = extra[:, 64:].reshape(devices, 8, experts)[:, 0]
    counts = jnp.sum(tails.astype(FULL), axis=0)
    new_average = 0.7 * load_average + 0.3 * counts
    pieces, out_weight_grad, in_weight_grad, input_grad, counts, new_average = tied(
        pieces, out_weight_grad, in_weight_grad, input_grad, counts, new_average
    )
    *grads, output, gain_one, bias_one, gain_two, bias_two = kernel_call(
        reduce_kernel,
        [VMEM, HBM, HBM],
        [((8, WIDTH), FULL, VMEM)] * 4
        + [((TOK, WIDTH), LOW, VMEM)]
        + [((1, 8), FULL, VMEM)] * 4,
        scratch=[((SLOTS, SENT), LOW), ((TOK, WIDTH), FULL)],
        copies=5,
        moved=5 << 20,
        name="reduce",
    )(slot, pieces, hidden_one)
    return (
        output,
        input_grad,
        *grads,
        gain_one.reshape(8),
        bias_one.reshape(8),
        gain_two.reshape(8),
        bias_two.reshape(8),
        in_weight_grad[None],
        out_weight_grad[None],
        counts.astype(jnp.int32),
        new_average,
    )


def solution(mesh):
    rows = P(("rep", "exp"), None)
    vector = P(("rep", "exp"))
    return jax.shard_map(
        per_device,
        mesh=mesh,
        in_specs=(rows,) * 7
        + (vector,) * 4
        + (P("exp", None, "rep"), P("exp", "rep", None), P(), rows),
        out_specs=(rows,) * 6
        + (vector,) * 4
        + (P("exp", None, "rep"), P("exp", "rep", None), P(), P()),
        check_vma=False,
    )
```

```python
import functools

import jax
import jax.numpy as jnp
from jax import lax
from jax.experimental import pallas as pl
from jax.experimental.pallas import tpu as pltpu
from jax.sharding import PartitionSpec as P

HEADS = 16
HEAD_DIM = 64
SCALE = HEAD_DIM ** (-0.5)
EPSILON = 1e-05
SWAP = [(0, 1), (1, 0)]
CAPACITY = 8
TOK = 128
WIDTH = 1024
HALF = WIDTH // 2
SLOTS = 512
FLOW = 3 * WIDTH
ALL = 4 * WIDTH
LENGTH = ALL + 128
STAR = WIDTH + 128
LAST = STAR + WIDTH
LINE = 4
VMEM_BYTES = 511 << 17
LOW = jnp.bfloat16
FULL = jnp.float32
VMEM = pl.BlockSpec(memory_space=pltpu.VMEM)
SMEM = pl.BlockSpec(memory_space=pltpu.SMEM)
HBM = pl.BlockSpec(memory_space=pltpu.HBM)


def swap(value):
    return lax.ppermute(value, "rep", SWAP)


def moved_on(index, stride, step):
    at = index // stride % LINE
    return index + ((at + step) % LINE - at) * stride


def shifted(value, stride, step):
    count = lax.axis_size("exp")
    pairs = [(index, moved_on(index, stride, step)) for index in range(count)]
    return lax.ppermute(value, "exp", pairs)


def from_two(value, first, second):
    count = lax.axis_size("exp")
    pairs = []
    for rep, way in enumerate((first, second)):
        pairs += [(rep * count + moved_on(i, *way), rep * count + i) for i in range(count)]
    return lax.ppermute(value, ("rep", "exp"), pairs)


def exchange(value):
    return lax.all_to_all(value, "exp", split_axis=0, concat_axis=0, tiled=True)


def dot(left, right):
    return jnp.dot(left, right, preferred_element_type=FULL)


def dot_nt(left, right):
    return lax.dot_general(left, right, (((1,), (1,)), ((), ())), preferred_element_type=FULL)


def dot_tn(left, right):
    return lax.dot_general(left, right, (((0,), (0,)), ((), ())), preferred_element_type=FULL)


def kernel_call(
    body, specs, outs, scratch=(), copies=0, flops=0, moved=0, name=None, aliases=None
):
    shapes = [pltpu.VMEM(shape, dtype) for shape, dtype in scratch]
    if copies:
        shapes.append(pltpu.SemaphoreType.DMA((copies,)))
    return pl.pallas_call(
        body,
        in_specs=specs,
        out_specs=[spec for _, _, spec in outs],
        out_shape=[jax.ShapeDtypeStruct(shape, dtype) for shape, dtype, _ in outs],
        scratch_shapes=shapes,
        input_output_aliases=aliases or {},
        compiler_params=pltpu.CompilerParams(vmem_limit_bytes=VMEM_BYTES),
        cost_estimate=pl.CostEstimate(flops=flops, bytes_accessed=moved, transcendentals=0),
        name=name,
    )


def start(source, target, sem):
    copy = pltpu.make_async_copy(source, target, sem)
    copy.start()
    return copy


def lanes(first, size):
    return pl.ds(pl.multiple_of(first, size), size)


def load_all(sources, place, weights, sems, first):
    loads = []
    for index, pair in enumerate(sources):
        matrix = lax.rem(place[0, 1] + index, 4)
        for side, half in enumerate((place[0, 0], 1 - place[0, 0])):
            target = weights.at[matrix, lanes(half * HALF, HALF), :]
            loads.append(start(pair[side], target, sems.at[first + 2 * index + side]))
    return loads


def load_one(sources, place, matrix, weight, sems, first):
    loads = []
    for side, half in enumerate((place[0, 0], 1 - place[0, 0])):
        target, sem = weight.at[lanes(half * HALF, HALF), :], sems.at[first + side]
        for index, pair in enumerate(sources):

            @pl.when(lax.rem(place[0, 1] + index, 4) == matrix)
            def _(source=pair[side], target=target, sem=sem):
                pltpu.make_async_copy(source, target, sem).start()

        loads.append(pltpu.make_async_copy(sources[1][side], target, sem))
    return loads


def as_sources(shares, other_shares, received):
    at = pl.ds(0, WIDTH)
    made = [(shares.at[:, at], other_shares.at[:, at])]
    return made + [(received[2 * index], received[2 * index + 1]) for index in range(3)]


def centered(rows):
    center = rows - jnp.mean(rows, axis=-1, keepdims=True)
    spread = jnp.mean(center * center, axis=-1, keepdims=True)
    inverse = lax.rsqrt(spread + EPSILON)
    return center * inverse, inverse


def norm_pull(upstream, unit, inverse, gain):
    scaled = upstream * gain
    return inverse * (
        scaled
        - jnp.mean(scaled, axis=-1, keepdims=True)
        - unit * jnp.mean(scaled * unit, axis=-1, keepdims=True)
    )


def placed(slot, part):
    row_at = lax.broadcasted_iota(jnp.int32, (TOK, TOK), 0) + part * TOK
    return (row_at == slot).astype(LOW)


def pack_kernel(norms, ids, query, key, value, output, grad, packed, slot, *scratch):
    ids_in, rows, grad_in, lined, rows_made, sems = scratch
    loads = [start(ids, ids_in, sems.at[0])]
    for index, ref in enumerate((query, key, value, output)):
        loads.append(start(ref, rows.at[index], sems.at[1 + index]))
    grad_load = start(grad, grad_in, sems.at[5])
    row = jnp.concatenate([norms[...].astype(FULL), jnp.zeros((1, TOK - 32), FULL)], axis=1)
    tile = jnp.broadcast_to(row, (TOK, TOK)).T
    lane_at = lax.broadcasted_iota(jnp.int32, (8, TOK), 1)
    params = jnp.zeros((8, TOK), FULL)
    for index in range(4):
        params = params + jnp.where(lane_at == index, tile[index * 8 : (index + 1) * 8, :], 0.0)
    loads[0].wait()
    row_at = lax.broadcasted_iota(jnp.int32, (TOK, TOK), 0)
    column_at = lax.broadcasted_iota(jnp.int32, (TOK, TOK), 1)
    by_column = jnp.broadcast_to(ids_in[...].astype(FULL), (TOK, TOK))
    before = (by_column.T == by_column) & (row_at < column_at)
    rank = jnp.sum(before.astype(FULL), axis=0, keepdims=True).astype(jnp.int32)
    target = ids_in[...] * CAPACITY + rank
    slot[...] = target
    chosen = (ids_in[...] == row_at - 64).astype(LOW)
    counts = dot_nt(jnp.ones((8, TOK), LOW), chosen)
    first = lax.broadcasted_iota(jnp.int32, (8, TOK), 0) == 0
    extra = params + jnp.where(first, counts, 0.0)
    for load in loads[1:]:
        load.wait()
    rows_full = [rows[index].astype(FULL) for index in range(4)]
    copies = []
    for base in range(4):
        made = [
            jnp.concatenate([rows_full[(base + 3 * z) % 4], extra], axis=1) for z in range(LINE)
        ]
        lined[base] = jnp.concatenate(made, axis=0).astype(LOW)
    for y in range(LINE):
        for x in range(LINE):
            index = y * LINE + x
            at = packed.at[pl.ds(index * 32, 32), pl.ds(0, STAR)]
            copies.append(start(lined.at[(x + 2 * y) % 4], at, sems.at[6 + index]))
    grad_load.wait()
    for part in range(4):
        at = pl.ds(part * TOK, TOK)
        rows_made[at, :] = dot(placed(target, part), grad_in[...]).astype(LOW)
        goal = packed.at[at, pl.ds(STAR, WIDTH)]
        copies.append(start(rows_made.at[at, :], goal, sems.at[22 + part]))
    for copy in copies:
        copy.wait()


def split_kernel(shares, target, held, sems):
    start(shares.at[:, pl.ds(0, WIDTH)], held, sems.at[0]).wait()
    start(held, target, sems.at[1]).wait()


def attend_kernel(
    place, slot, lengths, shares, other_shares, *refs
):
    received, tokens, refs = refs[:6], refs[6], refs[7:]
    outgoing_out, hidden_out, qkv_out, probs_out, normed_out, joined_out, norms_out = refs[:7]
    extra_out, theirs_out, *scratch = refs[7:]
    tokens_in, extra, weights, norms, normed, qkv, raw, low, joined, hidden, outgoing, sems = scratch
    rep = place[0, 0]
    halves = (lanes(rep * HALF, HALF), lanes((1 - rep) * HALF, HALF))
    tokens_load = start(tokens, tokens_in, sems.at[1])
    extra_loads = []
    for side, ref in enumerate((shares, other_shares)):
        source = ref.at[:, pl.ds(WIDTH, 128)]
        extra_loads.append(start(source, extra.at[halves[side], :], sems.at[18 + side]))
    sources = as_sources(shares, other_shares, received)
    weight_loads = load_all(sources, place, weights, sems, 20)
    for load in extra_loads:
        load.wait()
    norms[...] = extra[...].astype(FULL).T[:8, :]
    copies = [start(norms, norms_out, sems.at[6]), start(extra, extra_out, sems.at[0])]
    tokens_load.wait()
    inputs = tokens_in[...].astype(FULL)
    unit, _ = centered(inputs)
    normed[...] = (unit * norms[0:1, :] + norms[1:2, :]).astype(LOW)
    copies.append(start(normed, normed_out, sems.at[7]))
    for load in weight_loads:
        load.wait()
    for index in range(3):
        qkv[index] = dot(normed[...], weights[index]).astype(LOW)
    copies.append(start(qkv, qkv_out, sems.at[8]))

    query_at = lax.broadcasted_iota(jnp.int32, (TOK, TOK), 0)
    key_at = lax.broadcasted_iota(jnp.int32, (TOK, TOK), 1)
    end = jnp.int32(0)
    query_doc = jnp.zeros((TOK, TOK), jnp.int32)
    key_doc = jnp.zeros((TOK, TOK), jnp.int32)
    for j in range(3):
        end = end + lengths[0, j]
        query_doc += (query_at >= end).astype(jnp.int32)
        key_doc += (key_at >= end).astype(jnp.int32)
    allowed = (query_doc == key_doc) & (key_at <= query_at)
    for first in range(0, HEADS, 8):
        heads = range(first, first + 8)
        for head in heads:
            at = slice(head * HEAD_DIM, (head + 1) * HEAD_DIM)
            raw[head] = dot_nt(qkv[0, :, at], qkv[1, :, at])
        for head in heads:
            scores = jnp.where(allowed, raw[head] * SCALE, -1e30)
            raised = jnp.exp(scores - jnp.max(scores, axis=-1, keepdims=True))
            chance = raised / jnp.sum(raised, axis=-1, keepdims=True)
            low[head] = chance.astype(LOW)
        block = pl.ds(first, 8)
        copies.append(start(low.at[block], probs_out.at[block], sems.at[9 + first // 8]))
        for head in range(first, first + 8, 2):
            made = []
            for one in (head, head + 1):
                made.append(dot(low[one], qkv[2, :, one * HEAD_DIM : (one + 1) * HEAD_DIM]))
            at = slice(head * HEAD_DIM, (head + 2) * HEAD_DIM)
            joined[:, at] = jnp.concatenate(made, axis=1).astype(LOW)
    for index, half in enumerate((rep, 1 - rep)):
        source = joined.at[:, lanes(half * HALF, HALF)]
        target = joined_out.at[:, pl.ds(index * HALF, HALF)]
        copies.append(start(source, target, sems.at[11 + index]))
    for index, ref in enumerate((normed, joined)):
        source = ref.at[:, lanes((1 - rep) * HALF, HALF)]
        target = theirs_out.at[:, pl.ds(index * HALF, HALF)]
        copies.append(start(source, target, sems.at[36 + index]))
    made = inputs + dot(joined[...], weights[3])
    hidden[...] = made
    copies.append(start(hidden, hidden_out, sems.at[13]))
    unit, _ = centered(made)
    second = (unit * norms[2:3, :] + norms[3:4, :]).astype(LOW)
    for part in range(4):
        rows = pl.ds(part * TOK, TOK)
        outgoing[rows, :] = dot(placed(slot[...], part), second).astype(LOW)
        copies.append(start(outgoing.at[rows, :], outgoing_out.at[rows, :], sems.at[14 + part]))
    for copy in copies:
        copy.wait()


def gelu_parts(pre):
    square = pre * pre
    turn = jnp.tanh(pre * (0.7978845608028654 + 0.035677408136300125 * square))
    half = 0.5 + 0.5 * turn
    slope = half + (0.5 - 0.5 * turn * turn) * (
        pre * (0.7978845608028654 + 0.10703222440890037 * square)
    )
    return pre * half, slope


def expert_kernel(rows_in, weight_own, weight_other, up_own, up_other, out, *refs):
    acts, flows, scratch = refs[:2], refs[2:4], refs[4:]
    rows, weight, up, act, flow, back, sems = scratch
    hidden = weight.shape[1]
    half = hidden // 2
    chunk = 1024
    parts = hidden // chunk

    def load(j):
        cols = pl.ds(j * chunk, chunk)
        at = pl.ds(j * chunk % half, chunk)
        weight_in, up_in = (weight_own, up_own) if j * chunk < half else (weight_other, up_other)
        return (
            start(weight_in.at[:, at], weight.at[:, cols], sems.at[1 + j]),
            start(up_in.at[:, at], up.at[:, cols], sems.at[1 + parts + j]),
        )

    rows_load = start(rows_in, rows, sems.at[0])
    loads = [load(0), load(1)]
    rows_load.wait()
    copies = []
    for j in range(parts):
        cols = slice(j * chunk, (j + 1) * chunk)
        if j + 2 < parts:
            loads.append(load(j + 2))
        for copy in loads[j]:
            copy.wait()
        value, slope = gelu_parts(dot(rows[...], weight[:, cols]))
        act[:, cols] = value.astype(LOW)
        flow[:, cols] = (up[:, cols].astype(FULL) * slope).astype(LOW)
        at = pl.ds(j * chunk, chunk)
        side = j * chunk // half
        target_at = pl.ds(j * chunk % half, chunk)
        for index, (source, targets) in enumerate(((act, acts), (flow, flows))):
            sem = sems.at[1 + 2 * parts + 2 * j + index]
            copies.append(start(source.at[:, at], targets[side].at[:, target_at], sem))
    for index in range(2):
        block = slice(index * 256, (index + 1) * 256)
        back[block, :] = dot_nt(flow[block, :], weight[...]).astype(LOW)
        at = pl.ds(index * 256, 256)
        copies.append(start(back.at[at, :], out.at[at, :], sems.at[1 + 4 * parts + index]))
    for copy in copies:
        copy.wait()


def result_kernel(act_own, act_other, weight_own, weight_other, out, act, weight, made, sems):
    half = weight_own.shape[0]
    loads = [
        start(act_own, act.at[:, pl.ds(0, half)], sems.at[0]),
        start(act_other, act.at[:, pl.ds(half, half)], sems.at[5]),
        start(weight_own, weight.at[pl.ds(0, half), :], sems.at[1]),
        start(weight_other, weight.at[pl.ds(half, half), :], sems.at[2]),
    ]
    for load in loads:
        load.wait()
    copies = []
    for index in range(2):
        block = slice(index * 256, (index + 1) * 256)
        made[block, :] = dot(act[block, :], weight[...]).astype(LOW)
        at = pl.ds(index * 256, 256)
        target = out.at[at, pl.ds(STAR, WIDTH)]
        copies.append(start(made.at[at, :], target, sems.at[3 + index]))
    for copy in copies:
        copy.wait()


def weight_grad_kernel(by_rows, at, first, second, streamed_first, streamed_second, made, held, sems):
    half = first.shape[0]
    cols = pl.ds(at, held.shape[1])

    @pl.when(pl.program_id(0) == 0)
    def _():
        loads = [
            start(first.at[:, cols], held.at[pl.ds(0, half), :], sems.at[0]),
            start(second.at[:, cols], held.at[pl.ds(half, half), :], sems.at[1]),
        ]
        for load in loads:
            load.wait()

    streamed = jnp.concatenate([streamed_first[...], streamed_second[...]], axis=0)
    made[...] = dot_tn(streamed, held[...]) if by_rows else dot_tn(held[...], streamed)


def weight_grad_call(held, at, streamed, by_rows, tile=512):
    rows, wide = streamed[0].shape
    width = WIDTH
    shape = (wide, width) if by_rows else (width, wide)
    block = (tile, width) if by_rows else (width, tile)
    return pl.pallas_call(
        functools.partial(weight_grad_kernel, by_rows, at),
        grid=(wide // tile,),
        in_specs=[HBM, HBM] + [pl.BlockSpec((rows, tile), lambda i: (0, i))] * 2,
        out_specs=pl.BlockSpec(block, (lambda i: (i, 0)) if by_rows else (lambda i: (0, i))),
        out_shape=jax.ShapeDtypeStruct(shape, FULL),
        scratch_shapes=[pltpu.VMEM((2 * rows, width), LOW), pltpu.SemaphoreType.DMA((2,))],
        compiler_params=pltpu.CompilerParams(
            dimension_semantics=("arbitrary",), vmem_limit_bytes=VMEM_BYTES
        ),
        cost_estimate=pl.CostEstimate(
            flops=4 * rows * wide * width, bytes_accessed=14 << 20, transcendentals=0
        ),
        name="weight_grad",
    )(*held, *streamed)


def attend_back_kernel(
    place, slot, norms, back, hidden, grad, shares, other_shares, *refs
):
    received, (qkv_in, probs_in, grad_out, flow_out) = refs[:6], refs[6:10]
    parts_out, gains, scratch = refs[10:14], refs[14], refs[15:]
    back_in, hidden_in, grad_in, weight, qkv, probs, total, above, raw, low, flow, sems = scratch
    back_loads = []
    for part in range(2):
        at = pl.ds(part * 2 * TOK, 2 * TOK)
        back_loads.append(start(back.at[at, :], back_in.at[at, :], sems.at[part]))
    hidden_load = start(hidden, hidden_in, sems.at[4])
    grad_load = start(grad, grad_in, sems.at[5])
    sources = as_sources(shares, other_shares, received)
    weight_loads = load_one(sources, place, 3, weight, sems, 15)
    qkv_load = start(qkv_in, qkv, sems.at[7])
    probs_load = start(probs_in, probs, sems.at[8])
    upstream = jnp.zeros((TOK, WIDTH), FULL)
    for part in range(4):
        if part % 2 == 0:
            back_loads[part // 2].wait()
        rows = back_in[part * TOK : (part + 1) * TOK, :]
        upstream = upstream + dot_tn(placed(slot[...], part), rows)
    hidden_load.wait()
    grad_load.wait()
    unit, inverse = centered(hidden_in[...])
    made = grad_in[...].astype(FULL) + norm_pull(upstream, unit, inverse, norms[2:3, :])
    total[...] = made
    copies = [start(total, grad_out, sems.at[9])]
    flow[:, FLOW:] = made.astype(LOW)
    gains[...] = jnp.zeros(gains.shape, FULL)
    gains[2:3, :] = jnp.sum(upstream * unit, axis=0, keepdims=True)
    gains[3:4, :] = jnp.sum(upstream, axis=0, keepdims=True)
    for load in weight_loads:
        load.wait()
    above[...] = dot_nt(flow[:, FLOW:], weight[...]).astype(LOW)
    qkv_load.wait()
    probs_load.wait()

    def head_of(part, head):
        return qkv[part, :, head * HEAD_DIM : (head + 1) * HEAD_DIM]

    def above_of(head):
        return above[:, head * HEAD_DIM : (head + 1) * HEAD_DIM]

    def store(part, first, pieces):
        at = part * WIDTH + first * HEAD_DIM
        flow[:, at : at + 2 * HEAD_DIM] = jnp.concatenate(pieces, axis=1).astype(LOW)

    for first in range(0, HEADS, 8):
        heads = range(first, first + 8)
        pairs = range(first, first + 8, 2)
        for head in heads:
            raw[head] = dot_nt(above_of(head), head_of(2, head))
        for head in pairs:
            store(2, head, [dot_tn(probs[h], above_of(h)) for h in (head, head + 1)])
        for head in heads:
            chance, pulled = probs[head].astype(FULL), raw[head]
            taken = jnp.sum(chance * pulled, axis=-1, keepdims=True)
            low[head] = (chance * (pulled - taken)).astype(LOW)
        for head in pairs:
            store(0, head, [dot(low[h], head_of(1, h)) * SCALE for h in (head, head + 1)])
            store(1, head, [dot_tn(low[h], head_of(0, h)) * SCALE for h in (head, head + 1)])
    for index, target in enumerate(parts_out):
        source = flow.at[:, lanes(lax.rem(place[0, 1] + index, 4) * WIDTH, WIDTH)]
        copies.append(start(source, target, sems.at[10 + index]))
    copies.append(start(flow, flow_out, sems.at[14]))
    for copy in copies:
        copy.wait()


def left_kernel(place, normed, joined, other_halves, *refs):
    targets, held, sems = refs[:4], refs[4], refs[5]
    mine = lanes(place[0, 0] * HALF, HALF)
    first, second = pl.ds(0, TOK), pl.ds(TOK, TOK)
    loads = [
        start(normed.at[:, mine], held.at[0, first, :], sems.at[0]),
        start(other_halves.at[:, pl.ds(0, HALF)], held.at[0, second, :], sems.at[1]),
        start(joined.at[:, pl.ds(0, HALF)], held.at[1, first, :], sems.at[2]),
        start(other_halves.at[:, pl.ds(HALF, HALF)], held.at[1, second, :], sems.at[3]),
    ]
    for load in loads:
        load.wait()
    copies = []
    for index, target in enumerate(targets):
        kind = lax.div(lax.rem(place[0, 1] + index, 4), 3)
        copies.append(start(held.at[kind], target, sems.at[4 + index]))
    for copy in copies:
        copy.wait()


def weights_kernel(place, *refs):
    lefts, flows, refs = refs[:4], refs[4:12], refs[12:]
    shares, gains_in, other_gains_in, packed, out = refs[:5]
    left, right, weight, made, gains, sems = refs[5:]
    rep, colour = place[0, 0], place[0, 1]
    loads = []
    for index, source in enumerate(lefts):
        target = left.at[pl.ds(index * 2 * TOK, 2 * TOK), :]
        loads.append(start(source, target, sems.at[index]))
    for index, source in enumerate(flows):
        target = right.at[pl.ds(index * TOK, TOK), :]
        loads.append(start(source, target, sems.at[4 + index]))
    small = [
        start(shares.at[:, pl.ds(0, WIDTH)], weight, sems.at[12]),
        start(shares.at[:, pl.ds(WIDTH, 128)], made.at[:, pl.ds(WIDTH, 128)], sems.at[14]),
        start(gains_in, gains.at[0], sems.at[15]),
        start(other_gains_in, gains.at[1], sems.at[16]),
    ]
    for load in loads:
        load.wait()
    value = dot_tn(left[...], right[...])
    made[:, :WIDTH] = value.astype(LOW)
    at = pl.ds(0, WIDTH)
    copies = [start(made.at[:, at], out.at[:, at], sems.at[17])]
    for load in small:
        load.wait()
    weight_full = weight[...].astype(FULL)
    total = jnp.sum(right[...].astype(FULL), axis=0, keepdims=True)
    params = made[:, WIDTH:].astype(FULL)
    bias = jnp.sum(weight_full * total, axis=1, keepdims=True)
    gain = jnp.sum(weight_full * value, axis=1, keepdims=True)
    gain = (gain - params[:, 1:2] * bias) / params[:, 0:1]
    projects = colour < 3
    columns = gains[0] + gains[1]
    columns = jnp.concatenate([columns, jnp.zeros((TOK - 8, WIDTH), FULL)], axis=0)
    turned = jnp.where(rep == 0, columns[:, :HALF], columns[:, HALF:]).T
    lane_at = lax.broadcasted_iota(jnp.int32, (HALF, 128), 1)
    first = jnp.where(projects, gain, 0.0)
    second = jnp.where(projects, bias, 0.0)
    tail = jnp.where(lane_at == 0, first, jnp.where(lane_at == 1, second, turned))
    made[:, WIDTH:] = tail.astype(LOW)
    at = pl.ds(WIDTH, 128)
    copies.append(start(made.at[:, at], out.at[:, at], sems.at[18]))
    for copy in copies:
        copy.wait()


def input_kernel(place, norms, tokens, hidden_grad, flow, shares, other_shares, *refs):
    received, made_out, scratch = refs[:6], refs[6], refs[7:]
    tokens_in, grad_in, flow_in, weights, made, sems = scratch
    loads = [
        start(tokens, tokens_in, sems.at[0]),
        start(hidden_grad, grad_in, sems.at[1]),
        start(flow.at[:, pl.ds(0, FLOW)], flow_in, sems.at[2]),
    ]
    sources = as_sources(shares, other_shares, received)
    weight_loads = load_all(sources, place, weights, sems, 4)
    for load in loads:
        load.wait()
    for load in weight_loads:
        load.wait()
    upstream = jnp.zeros((TOK, WIDTH), FULL)
    for index in range(3):
        cols = slice(index * WIDTH, (index + 1) * WIDTH)
        upstream = upstream + dot_nt(flow_in[:, cols], weights[index])
    unit, inverse = centered(tokens_in[...].astype(FULL))
    made[...] = grad_in[...] + norm_pull(upstream, unit, inverse, norms[0:1, :])
    start(made, made_out, sems.at[3]).wait()


def reduce_kernel(slot, pieces, hidden, query, key, value, output, result, *refs):
    norms, held, hidden_in, sems = refs[:4], *refs[4:]
    hidden_load = start(hidden, hidden_in, sems.at[4])
    loads = []
    for part in range(4):
        rows = pl.ds(part * TOK, TOK)
        loads.append(start(pieces.at[rows, :], held.at[rows, :], sems.at[part]))
    sums = [jnp.zeros((8, WIDTH), FULL) for _ in range(4)]
    tail = jnp.zeros((8, 128), FULL)
    hidden_load.wait()
    made = hidden_in[...]
    for part in range(4):
        loads[part].wait()
        for pair in range(8):
            at = part * TOK + pair * 16
            rows = held[at : at + 16, :STAR].astype(FULL)
            for side in range(2):
                index = part * 16 + pair * 2 + side
                y, x, z = index // 16, index // 4 % 4, index % 4
                colour = (x + 2 * y - z) % 4
                piece = rows[side * 8 : (side + 1) * 8, :]
                sums[colour] = sums[colour] + piece[:, :WIDTH]
                tail = tail + piece[:, WIDTH:]
        at = slice(part * TOK, (part + 1) * TOK)
        made = made + dot_tn(placed(slot[...], part), held[at, STAR:])
    result[...] = made.astype(LOW)
    for ref, total in zip((query, key, value, output), sums):
        ref[...] = total
    tail = jnp.concatenate([tail, jnp.zeros((TOK - 8, 128), FULL)], axis=0).T
    for index, norm in enumerate(norms):
        norm[...] = tail[index : index + 1, :8]


def tied(*values):
    return lax.optimization_barrier(values)


def per_device(
    tokens,
    hash_ids,
    doc_lengths,
    w_query,
    w_key,
    w_value,
    w_output,
    norm1_gain,
    norm1_bias,
    norm2_gain,
    norm2_bias,
    expert_in,
    expert_out,
    load_average,
    out_grad,
):
    experts = load_average.shape[0]
    groups = lax.axis_size("exp")
    devices = 2 * groups
    rep = lax.axis_index("rep")
    at = lax.axis_index("exp")
    y, x, z = lax.div(at, LINE * LINE), lax.rem(lax.div(at, LINE), LINE), lax.rem(at, LINE)
    colour = lax.rem(x + 2 * y + 3 * z, 4)
    place = jnp.stack([rep, colour]).astype(jnp.int32).reshape(1, 2)
    weight_in, weight_out = expert_in[0], expert_out[0]
    hidden = weight_in.shape[1]

    norm_params = jnp.concatenate([norm1_gain, norm1_bias, norm2_gain, norm2_bias]).reshape(1, 32)
    packed, slot = kernel_call(
        pack_kernel,
        [VMEM] + [HBM] * 6,
        [((SLOTS, LAST), LOW, HBM), ((1, TOK), jnp.int32, VMEM)],
        scratch=[
            ((1, TOK), jnp.int32),
            ((4, 8, WIDTH), LOW),
            ((TOK, WIDTH), LOW),
            ((4, 32, STAR), LOW),
            ((SLOTS, WIDTH), LOW),
        ],
        copies=26,
        flops=2 * SLOTS * TOK * WIDTH,
        moved=6 << 20,
        name="pack",
    )(norm_params, hash_ids.reshape(1, TOK), w_query, w_key, w_value, w_output, out_grad)
    shares = exchange(packed.reshape(groups, 8, LAST)).reshape(SLOTS, LAST)
    weight_in_other, weight_out_other = swap(weight_in), swap(weight_out)
    shares, weight_in_other, weight_out_other = tied(shares, weight_in_other, weight_out_other)
    (own,) = kernel_call(
        split_kernel,
        [HBM],
        [((SLOTS, WIDTH), LOW, HBM)],
        scratch=[((SLOTS, WIDTH), LOW)],
        copies=2,
        moved=2 << 20,
        name="split",
    )(shares)
    received = [
        from_two(own, (LINE, 1), (1, -1)),
        from_two(own, (LINE * LINE, 1), (LINE * LINE, -1)),
        from_two(own, (LINE, -1), (1, 1)),
    ]
    other_shares = swap(shares)
    received = [one for part in received for one in (part, swap(part))]

    def send(rows):
        return exchange(rows.reshape(groups, CAPACITY, WIDTH)).reshape(SLOTS, WIDTH)

    outgoing, hidden_one, qkv, probs, normed, joined, norms, extra, theirs = kernel_call(
        attend_kernel,
        [SMEM, VMEM, SMEM] + [HBM] * 9,
        [
            ((SLOTS, WIDTH), LOW, HBM),
            ((TOK, WIDTH), FULL, HBM),
            ((3, TOK, WIDTH), LOW, HBM),
            ((HEADS, TOK, TOK), LOW, HBM),
            ((TOK, WIDTH), LOW, HBM),
            ((TOK, WIDTH), LOW, HBM),
            ((8, WIDTH), FULL, HBM),
            ((WIDTH, 128), LOW, HBM),
            ((TOK, WIDTH), LOW, HBM),
        ],
        scratch=[
            ((TOK, WIDTH), LOW),
            ((WIDTH, 128), LOW),
            ((4, WIDTH, WIDTH), LOW),
            ((8, WIDTH), FULL),
            ((TOK, WIDTH), LOW),
            ((3, TOK, WIDTH), LOW),
            ((HEADS, TOK, TOK), FULL),
            ((HEADS, TOK, TOK), LOW),
            ((TOK, WIDTH), LOW),
            ((TOK, WIDTH), FULL),
            ((SLOTS, WIDTH), LOW),
        ],
        copies=38,
        flops=2 * TOK * WIDTH * 5000,
        moved=12 << 20,
        name="attend",
    )(place, slot, doc_lengths, shares, other_shares, *received, tokens)

    grad_rows = shares[:, STAR:]
    up_own = dot_nt(grad_rows, weight_out).astype(LOW)
    up_other = dot_nt(grad_rows, weight_out_other).astype(LOW)
    rows, up_own, up_other = tied(send(outgoing), up_own, up_other)
    other_halves = swap(theirs)
    lefts = kernel_call(
        left_kernel,
        [SMEM] + [HBM] * 3,
        [((2 * TOK, HALF), LOW, HBM)] * 4,
        scratch=[((2, 2 * TOK, HALF), LOW)],
        copies=8,
        moved=1 << 20,
        name="left",
    )(place, normed, joined, other_halves)
    rows, *lefts = tied(rows, *lefts)

    def to_neighbours(values):
        ways = ((LINE, 1), (LINE * LINE, 1), (LINE, -1))
        return [shifted(value, *way) for value, way in zip(values, ways)]

    back_rows, *acts_flows = kernel_call(
        expert_kernel,
        [HBM] * 5,
        [
            ((SLOTS, WIDTH), LOW, HBM),
        ]
        + [((SLOTS, hidden), LOW, HBM)] * 4,
        scratch=[
            ((SLOTS, WIDTH), LOW),
            ((WIDTH, 2 * hidden), LOW),
            ((SLOTS, 2 * hidden), LOW),
            ((SLOTS, 2 * hidden), LOW),
            ((SLOTS, 2 * hidden), LOW),
            ((SLOTS, WIDTH), LOW),
        ],
        copies=3 + 8 * (hidden // 512),
        flops=8 * SLOTS * WIDTH * hidden,
        moved=24 << 20,
        name="expert",
    )(rows, weight_in, weight_in_other, up_own, up_other)
    act, act_theirs, flow, flow_theirs = acts_flows
    back_rows, *lefts = tied(back_rows, *lefts)
    lefts = [lefts[0]] + to_neighbours(lefts[1:])
    back = send(back_rows)
    (result,) = kernel_call(
        result_kernel,
        [HBM] * 4,
        [((SLOTS, LAST), LOW, HBM)],
        scratch=[
            ((SLOTS, 2 * hidden), LOW),
            ((2 * hidden, WIDTH), LOW),
            ((SLOTS, WIDTH), LOW),
        ],
        copies=6,
        flops=4 * SLOTS * hidden * WIDTH,
        moved=14 << 20,
        name="result",
    )(act, act_theirs, weight_out, weight_out_other)
    act_other, flow_other = swap(act_theirs), swap(flow_theirs)
    back, result, act_other, flow_other, *lefts = tied(
        back, result, act_other, flow_other, *lefts
    )

    hidden_grad, attend_flow, *parts, gains = kernel_call(
        attend_back_kernel,
        [SMEM, VMEM, VMEM] + [HBM] * 13,
        [
            ((TOK, WIDTH), FULL, HBM),
            ((TOK, ALL), LOW, HBM),
        ]
        + [((TOK, WIDTH), LOW, HBM)] * 4
        + [
            ((8, WIDTH), FULL, VMEM),
        ],
        scratch=[
            ((SLOTS, WIDTH), LOW),
            ((TOK, WIDTH), FULL),
            ((TOK, WIDTH), LOW),
            ((WIDTH, WIDTH), LOW),
            ((3, TOK, WIDTH), LOW),
            ((HEADS, TOK, TOK), LOW),
            ((TOK, WIDTH), FULL),
            ((TOK, WIDTH), LOW),
            ((HEADS, TOK, TOK), FULL),
            ((HEADS, TOK, TOK), LOW),
            ((TOK, ALL), LOW),
        ],
        copies=19,
        flops=2 * TOK * WIDTH * 3000,
        moved=8 << 20,
        name="attend_back",
    )(
        place,
        slot,
        norms,
        back,
        hidden_one,
        out_grad,
        shares,
        other_shares,
        *received,
        qkv,
        probs,
    )
    parts = [parts[0]] + to_neighbours(parts[1:])
    parts = [one for part in parts for one in (part, swap(part))]
    (weight_part,) = kernel_call(
        weights_kernel,
        [SMEM] + [HBM] * 16,
        [((SLOTS, LAST), LOW, HBM)],
        scratch=[
            ((8 * TOK, HALF), LOW),
            ((8 * TOK, WIDTH), LOW),
            ((HALF, WIDTH), LOW),
            ((HALF, STAR), LOW),
            ((2, 8, WIDTH), FULL),
        ],
        copies=19,
        flops=16 * TOK * HALF * WIDTH,
        moved=10 << 20,
        name="weights",
        aliases={16: 0},
    )(place, *lefts, *parts, shares, gains, swap(gains), result)
    pieces = exchange(weight_part.reshape(groups, 8, LAST)).reshape(SLOTS, LAST)

    act, flow, rows, attend_flow, _ = tied(act, flow, rows, attend_flow, weight_part)
    rows_other = swap(rows)
    out_weight_grad = weight_grad_call((shares, other_shares), STAR, (act, act_other), True)
    in_weight_grad = weight_grad_call((rows, rows_other), 0, (flow, flow_other), False)
    (input_grad,) = kernel_call(
        input_kernel,
        [SMEM, VMEM] + [HBM] * 11,
        [((TOK, WIDTH), FULL, HBM)],
        scratch=[
            ((TOK, WIDTH), LOW),
            ((TOK, WIDTH), FULL),
            ((TOK, FLOW), LOW),
            ((4, WIDTH, WIDTH), LOW),
            ((TOK, WIDTH), FULL),
        ],
        copies=20,
        flops=2 * TOK * WIDTH * FLOW,
        moved=8 << 20,
        name="input_grad",
    )(place, norms, tokens, hidden_grad, attend_flow, shares, other_shares, *received)
    tails = extra[:, 64:].reshape(devices, 8, experts)[:, 0]
    counts = jnp.sum(tails.astype(FULL), axis=0)
    new_average = 0.7 * load_average + 0.3 * counts
    counts = counts.astype(jnp.int32)
    pieces, out_weight_grad, in_weight_grad, input_grad, counts, new_average = tied(
        pieces, out_weight_grad, in_weight_grad, input_grad, counts, new_average
    )
    *grads, output, gain_one, bias_one, gain_two, bias_two = kernel_call(
        reduce_kernel,
        [VMEM, HBM, HBM],
        [((8, WIDTH), FULL, VMEM)] * 4
        + [((TOK, WIDTH), LOW, VMEM)]
        + [((1, 8), FULL, VMEM)] * 4,
        scratch=[((SLOTS, LAST), LOW), ((TOK, WIDTH), FULL)],
        copies=5,
        moved=5 << 20,
        name="reduce",
    )(slot, pieces, hidden_one)
    return (
        output,
        input_grad,
        *grads,
        gain_one.reshape(8),
        bias_one.reshape(8),
        gain_two.reshape(8),
        bias_two.reshape(8),
        in_weight_grad[None],
        out_weight_grad[None],
        counts,
        new_average,
    )


def solution(mesh):
    rows = P(("rep", "exp"), None)
    vector = P(("rep", "exp"))
    return jax.shard_map(
        per_device,
        mesh=mesh,
        in_specs=(rows,) * 7
        + (vector,) * 4
        + (P("exp", None, "rep"), P("exp", "rep", None), P(), rows),
        out_specs=(rows,) * 6
        + (vector,) * 4
        + (P("exp", None, "rep"), P("exp", "rep", None), P(), P()),
        check_vma=False,
    )
```

```python
import functools

import jax
import jax.numpy as jnp
from jax import lax
from jax.experimental import pallas as pl
from jax.experimental.pallas import tpu as pltpu
from jax.sharding import PartitionSpec as P

HEADS = 16
HEAD_DIM = 64
SCALE = HEAD_DIM ** (-0.5)
EPSILON = 1e-05
SWAP = [(0, 1), (1, 0)]
CAPACITY = 8
TOK = 128
WIDTH = 1024
HALF = WIDTH // 2
SLOTS = 512
FLOW = 3 * WIDTH
ALL = 4 * WIDTH
LENGTH = ALL + 128
STAR = WIDTH + 128
LAST = STAR + WIDTH
LINE = 4
VMEM_BYTES = 511 << 17
LOW = jnp.bfloat16
FULL = jnp.float32
VMEM = pl.BlockSpec(memory_space=pltpu.VMEM)
SMEM = pl.BlockSpec(memory_space=pltpu.SMEM)
HBM = pl.BlockSpec(memory_space=pltpu.HBM)


def swap(value):
    return lax.ppermute(value, "rep", SWAP)


def moved_on(index, stride, step):
    at = index // stride % LINE
    return index + ((at + step) % LINE - at) * stride


WAYS = (((LINE, 1), (1, -1)), ((LINE * LINE, 1), (LINE * LINE, -1)), ((LINE, -1), (1, 1)))


def between(value, ways, back):
    count = lax.axis_size("exp")
    pairs = []
    for rep, way in enumerate(ways):
        for index in range(count):
            near, far = rep * count + index, rep * count + moved_on(index, *way)
            pairs.append((far, near) if back else (near, far))
    return lax.ppermute(value, ("rep", "exp"), pairs)


def exchange(value):
    return lax.all_to_all(value, "exp", split_axis=0, concat_axis=0, tiled=True)


def dot(left, right):
    return jnp.dot(left, right, preferred_element_type=FULL)


def dot_nt(left, right):
    return lax.dot_general(left, right, (((1,), (1,)), ((), ())), preferred_element_type=FULL)


def dot_tn(left, right):
    return lax.dot_general(left, right, (((0,), (0,)), ((), ())), preferred_element_type=FULL)


def kernel_call(
    body, specs, outs, scratch=(), copies=0, flops=0, moved=0, name=None, aliases=None
):
    shapes = [pltpu.VMEM(shape, dtype) for shape, dtype in scratch]
    if copies:
        shapes.append(pltpu.SemaphoreType.DMA((copies,)))
    return pl.pallas_call(
        body,
        in_specs=specs,
        out_specs=[spec for _, _, spec in outs],
        out_shape=[jax.ShapeDtypeStruct(shape, dtype) for shape, dtype, _ in outs],
        scratch_shapes=shapes,
        input_output_aliases=aliases or {},
        compiler_params=pltpu.CompilerParams(vmem_limit_bytes=VMEM_BYTES),
        cost_estimate=pl.CostEstimate(flops=flops, bytes_accessed=moved, transcendentals=0),
        name=name,
    )


def start(source, target, sem):
    copy = pltpu.make_async_copy(source, target, sem)
    copy.start()
    return copy


def lanes(first, size):
    return pl.ds(pl.multiple_of(first, size), size)


def load_all(sources, place, weights, sems, first):
    loads = []
    for index, pair in enumerate(sources):
        matrix = lax.rem(place[0, 1] + index, 4)
        for side, half in enumerate((place[0, 0], 1 - place[0, 0])):
            target = weights.at[matrix, lanes(half * HALF, HALF), :]
            loads.append(start(pair[side], target, sems.at[first + 2 * index + side]))
    return loads


def load_one(sources, place, matrix, weight, sems, first):
    loads = []
    for side, half in enumerate((place[0, 0], 1 - place[0, 0])):
        target, sem = weight.at[lanes(half * HALF, HALF), :], sems.at[first + side]
        for index, pair in enumerate(sources):

            @pl.when(lax.rem(place[0, 1] + index, 4) == matrix)
            def _(source=pair[side], target=target, sem=sem):
                pltpu.make_async_copy(source, target, sem).start()

        loads.append(pltpu.make_async_copy(sources[1][side], target, sem))
    return loads


def as_sources(shares, other_shares, received):
    at = pl.ds(0, WIDTH)
    made = [(shares.at[:, at], other_shares.at[:, at])]
    return made + [(received[2 * index], received[2 * index + 1]) for index in range(3)]


def centered(rows):
    center = rows - jnp.mean(rows, axis=-1, keepdims=True)
    spread = jnp.mean(center * center, axis=-1, keepdims=True)
    inverse = lax.rsqrt(spread + EPSILON)
    return center * inverse, inverse


def norm_pull(upstream, unit, inverse, gain):
    scaled = upstream * gain
    return inverse * (
        scaled
        - jnp.mean(scaled, axis=-1, keepdims=True)
        - unit * jnp.mean(scaled * unit, axis=-1, keepdims=True)
    )


def same_document(lengths, query_at, key_at):
    end = jnp.int32(0)
    query_doc = jnp.zeros((TOK, TOK), jnp.int32)
    key_doc = jnp.zeros((TOK, TOK), jnp.int32)
    for j in range(3):
        end = end + lengths[0, j]
        query_doc += (query_at >= end).astype(jnp.int32)
        key_doc += (key_at >= end).astype(jnp.int32)
    return query_doc == key_doc


def placed(slot, part):
    row_at = lax.broadcasted_iota(jnp.int32, (TOK, TOK), 0) + part * TOK
    return (row_at == slot).astype(LOW)


def pack_kernel(norms, ids, query, key, value, output, grad, packed, slot, by_row, *scratch):
    ids_in, rows, grad_in, lined, rows_made, sems = scratch
    loads = [start(ids, ids_in, sems.at[0])]
    for index, ref in enumerate((query, key, value, output)):
        loads.append(start(ref, rows.at[index], sems.at[1 + index]))
    grad_load = start(grad, grad_in, sems.at[5])
    row = jnp.concatenate([norms[...].astype(FULL), jnp.zeros((1, TOK - 32), FULL)], axis=1)
    tile = jnp.broadcast_to(row, (TOK, TOK)).T
    lane_at = lax.broadcasted_iota(jnp.int32, (8, TOK), 1)
    params = jnp.zeros((8, TOK), FULL)
    for index in range(4):
        params = params + jnp.where(lane_at == index, tile[index * 8 : (index + 1) * 8, :], 0.0)
    loads[0].wait()
    row_at = lax.broadcasted_iota(jnp.int32, (TOK, TOK), 0)
    column_at = lax.broadcasted_iota(jnp.int32, (TOK, TOK), 1)
    by_column = jnp.broadcast_to(ids_in[...].astype(FULL), (TOK, TOK))
    before = (by_column.T == by_column) & (row_at < column_at)
    rank = jnp.sum(before.astype(FULL), axis=0, keepdims=True).astype(jnp.int32)
    target = ids_in[...] * CAPACITY + rank
    slot[...] = target
    by_row[...] = jnp.broadcast_to(target.astype(FULL), (TOK, TOK)).T.astype(jnp.int32)
    chosen = (ids_in[...] == row_at - 64).astype(LOW)
    counts = dot_nt(jnp.ones((8, TOK), LOW), chosen)
    first = lax.broadcasted_iota(jnp.int32, (8, TOK), 0) == 0
    extra = params + jnp.where(first, counts, 0.0)
    for load in loads[1:]:
        load.wait()
    rows_full = [rows[index].astype(FULL) for index in range(4)]
    copies = []
    for base in range(4):
        made = [
            jnp.concatenate([rows_full[(base + 3 * z) % 4], extra], axis=1) for z in range(LINE)
        ]
        lined[base] = jnp.concatenate(made, axis=0).astype(LOW)
    for y in range(LINE):
        for x in range(LINE):
            index = y * LINE + x
            at = packed.at[pl.ds(index * 32, 32), pl.ds(0, STAR)]
            copies.append(start(lined.at[(x + 2 * y) % 4], at, sems.at[6 + index]))
    grad_load.wait()
    for part in range(4):
        at = pl.ds(part * TOK, TOK)
        rows_made[at, :] = dot(placed(target, part), grad_in[...]).astype(LOW)
        goal = packed.at[at, pl.ds(STAR, WIDTH)]
        copies.append(start(rows_made.at[at, :], goal, sems.at[22 + part]))
    for copy in copies:
        copy.wait()


def placed_rows(by_row, part):
    lane_at = lax.broadcasted_iota(jnp.int32, (TOK, TOK), 1) + part * TOK
    return (lane_at == by_row).astype(LOW)


def split_kernel(shares, target, held, sems):
    start(shares.at[:, pl.ds(0, WIDTH)], held, sems.at[0]).wait()
    start(held, target, sems.at[1]).wait()


def attend_kernel(
    place, slot, lengths, shares, other_shares, *refs
):
    received, tokens, refs = refs[:6], refs[6], refs[7:]
    outgoing_out, hidden_out, qkv_out, probs_out, joined_out, normed_out = refs[:6]
    norms_out, extra_out, *scratch = refs[6:]
    tokens_in, extra, weights, norms, normed, qkv, raw, low, joined, hidden, outgoing, sems = scratch
    rep = place[0, 0]
    extra_loads = []
    for side, ref in enumerate((shares, other_shares)):
        rows = lanes((rep if side == 0 else 1 - rep) * HALF, HALF)
        source = ref.at[:, pl.ds(WIDTH, 128)]
        extra_loads.append(start(source, extra.at[rows, :], sems.at[18 + side]))
    tokens_load = start(tokens, tokens_in, sems.at[1])
    sources = as_sources(shares, other_shares, received)
    weight_loads = load_all(sources, place, weights, sems, 20)
    for load in extra_loads:
        load.wait()
    norms[...] = extra[...].astype(FULL).T[:8, :]
    copies = [start(norms, norms_out, sems.at[6]), start(extra, extra_out, sems.at[0])]
    tokens_load.wait()
    inputs = tokens_in[...].astype(FULL)
    unit, _ = centered(inputs)
    normed[...] = (unit * norms[0:1, :] + norms[1:2, :]).astype(LOW)
    copies.append(start(normed, normed_out, sems.at[7]))
    for load in weight_loads:
        load.wait()
    for index in range(3):
        qkv[index] = dot(normed[...], weights[index]).astype(LOW)
    copies.append(start(qkv, qkv_out, sems.at[8]))

    query_at = lax.broadcasted_iota(jnp.int32, (TOK, TOK), 0)
    key_at = lax.broadcasted_iota(jnp.int32, (TOK, TOK), 1)
    allowed = same_document(lengths, query_at, key_at) & (key_at <= query_at)
    for first in range(0, HEADS, 8):
        heads = range(first, first + 8)
        for head in heads:
            at = slice(head * HEAD_DIM, (head + 1) * HEAD_DIM)
            raw[head] = dot_nt(qkv[0, :, at], qkv[1, :, at])
        for head in heads:
            scores = jnp.where(allowed, raw[head] * SCALE, -1e30)
            raised = jnp.exp(scores - jnp.max(scores, axis=-1, keepdims=True))
            chance = raised / jnp.sum(raised, axis=-1, keepdims=True)
            low[head] = chance.astype(LOW)
        block = pl.ds(first, 8)
        copies.append(start(low.at[block], probs_out.at[block], sems.at[9 + first // 8]))
        for head in range(first, first + 8, 2):
            made = []
            for one in (head, head + 1):
                made.append(dot(low[one], qkv[2, :, one * HEAD_DIM : (one + 1) * HEAD_DIM]))
            at = slice(head * HEAD_DIM, (head + 2) * HEAD_DIM)
            joined[:, at] = jnp.concatenate(made, axis=1).astype(LOW)
    copies.append(start(joined, joined_out, sems.at[28]))
    made = inputs + dot(joined[...], weights[3])
    hidden[...] = made
    copies.append(start(hidden, hidden_out, sems.at[13]))
    unit, _ = centered(made)
    second = (unit * norms[2:3, :] + norms[3:4, :]).astype(LOW)
    for part in range(4):
        rows = pl.ds(part * TOK, TOK)
        outgoing[rows, :] = dot(placed(slot[...], part), second).astype(LOW)
        copies.append(start(outgoing.at[rows, :], outgoing_out.at[rows, :], sems.at[14 + part]))
    for copy in copies:
        copy.wait()


def left_kernel(place, normed, joined, *refs):
    targets, held, turned, sems = refs[:4], refs[4], refs[5], refs[6]
    loads = [start(ref, held.at[i], sems.at[i]) for i, ref in enumerate((normed, joined))]
    for index, load in enumerate(loads):
        load.wait()
        turned[index] = held[index].T
    copies = []
    for index, target in enumerate(targets):
        kind = lax.div(lax.rem(place[0, 1] + index, 4), 3)
        copies.append(start(turned.at[kind], target, sems.at[2 + index]))
    for copy in copies:
        copy.wait()


def gelu_parts(pre):
    square = pre * pre
    turn = jnp.tanh(pre * (0.7978845608028654 + 0.035677408136300125 * square))
    half = 0.5 + 0.5 * turn
    slope = half + (0.5 - 0.5 * turn * turn) * (
        pre * (0.7978845608028654 + 0.10703222440890037 * square)
    )
    return pre * half, slope


def expert_kernel(rows_in, weight_own, weight_other, up_own, up_other, out, *refs):
    acts, flows, scratch = refs[:2], refs[2:4], refs[4:]
    rows, weight, up, act, flow, back, sems = scratch
    hidden = weight.shape[1]
    half = hidden // 2
    chunk = 1024
    parts = hidden // chunk

    def load(j):
        cols = pl.ds(j * chunk, chunk)
        at = pl.ds(j * chunk % half, chunk)
        weight_in, up_in = (weight_own, up_own) if j * chunk < half else (weight_other, up_other)
        return (
            start(weight_in.at[:, at], weight.at[:, cols], sems.at[1 + j]),
            start(up_in.at[:, at], up.at[:, cols], sems.at[1 + parts + j]),
        )

    rows_load = start(rows_in, rows, sems.at[0])
    loads = [load(0), load(1)]
    rows_load.wait()
    copies = []
    for j in range(parts):
        cols = slice(j * chunk, (j + 1) * chunk)
        if j + 2 < parts:
            loads.append(load(j + 2))
        for copy in loads[j]:
            copy.wait()
        value, slope = gelu_parts(dot(rows[...], weight[:, cols]))
        act[:, cols] = value.astype(LOW)
        flow[:, cols] = (up[:, cols].astype(FULL) * slope).astype(LOW)
        at = pl.ds(j * chunk, chunk)
        side = j * chunk // half
        target_at = pl.ds(j * chunk % half, chunk)
        for index, (source, targets) in enumerate(((act, acts), (flow, flows))):
            sem = sems.at[1 + 2 * parts + 2 * j + index]
            copies.append(start(source.at[:, at], targets[side].at[:, target_at], sem))
    for index in range(2):
        block = slice(index * 256, (index + 1) * 256)
        back[block, :] = dot_nt(flow[block, :], weight[...]).astype(LOW)
        at = pl.ds(index * 256, 256)
        copies.append(start(back.at[at, :], out.at[at, :], sems.at[1 + 4 * parts + index]))
    for copy in copies:
        copy.wait()


def result_kernel(act_own, act_other, weight_own, weight_other, out, act, weight, made, sems):
    sides = []
    for side, (act_in, weight_in) in enumerate(((act_own, weight_own), (act_other, weight_other))):
        sides.append(
            [
                start(act_in, act.at[side], sems.at[2 * side]),
                start(weight_in, weight.at[side], sems.at[2 * side + 1]),
            ]
        )
        if side == 0:
            for load in sides[0]:
                load.wait()
    made[...] = dot(act[0], weight[0])
    for load in sides[1]:
        load.wait()
    act[0, :, :WIDTH] = (made[...] + dot(act[1], weight[1])).astype(LOW)
    source = act.at[0, :, pl.ds(0, WIDTH)]
    start(source, out.at[:, pl.ds(STAR, WIDTH)], sems.at[4]).wait()


def weight_grad_kernel(by_rows, at, first, second, streamed_first, streamed_second, made, held, sems):
    half = first.shape[0]
    cols = pl.ds(at, held.shape[1])

    @pl.when(pl.program_id(0) == 0)
    def _():
        loads = [
            start(first.at[:, cols], held.at[pl.ds(0, half), :], sems.at[0]),
            start(second.at[:, cols], held.at[pl.ds(half, half), :], sems.at[1]),
        ]
        for load in loads:
            load.wait()

    streamed = jnp.concatenate([streamed_first[...], streamed_second[...]], axis=0)
    made[...] = dot_tn(streamed, held[...]) if by_rows else dot_tn(held[...], streamed)


def weight_grad_call(held, at, streamed, by_rows, tile=1024):
    rows, wide = streamed[0].shape
    width = WIDTH
    shape = (wide, width) if by_rows else (width, wide)
    block = (tile, width) if by_rows else (width, tile)
    return pl.pallas_call(
        functools.partial(weight_grad_kernel, by_rows, at),
        grid=(wide // tile,),
        in_specs=[HBM, HBM] + [pl.BlockSpec((rows, tile), lambda i: (0, i))] * 2,
        out_specs=pl.BlockSpec(block, (lambda i: (i, 0)) if by_rows else (lambda i: (0, i))),
        out_shape=jax.ShapeDtypeStruct(shape, FULL),
        scratch_shapes=[pltpu.VMEM((2 * rows, width), LOW), pltpu.SemaphoreType.DMA((2,))],
        compiler_params=pltpu.CompilerParams(
            dimension_semantics=("arbitrary",), vmem_limit_bytes=VMEM_BYTES
        ),
        cost_estimate=pl.CostEstimate(
            flops=4 * rows * wide * width, bytes_accessed=14 << 20, transcendentals=0
        ),
        name="weight_grad",
    )(*held, *streamed)


def attend_back_kernel(
    place, by_row, lengths, norms, back, hidden, grad, shares, other_shares, *refs
):
    received, (qkv_in, probs_in, grad_out) = refs[:6], refs[6:9]
    parts_out, gains, scratch = refs[9:13], refs[13], refs[14:]
    back_in, hidden_in, grad_in, weight, qkv, probs, total, above, flow, *scratch = scratch
    raw, turned, pulled, low, low_turned, chance_turned, sems = scratch
    back_loads = []
    for part in range(2):
        at = pl.ds(part * 2 * TOK, 2 * TOK)
        back_loads.append(start(back.at[at, :], back_in.at[at, :], sems.at[part]))
    hidden_load = start(hidden, hidden_in, sems.at[4])
    grad_load = start(grad, grad_in, sems.at[5])
    sources = as_sources(shares, other_shares, received)
    weight_loads = load_one(sources, place, 3, weight, sems, 15)
    qkv_load = start(qkv_in, qkv, sems.at[7])
    probs_load = start(probs_in, probs, sems.at[8])
    upstream = jnp.zeros((TOK, WIDTH), FULL)
    for part in range(4):
        if part % 2 == 0:
            back_loads[part // 2].wait()
        rows = back_in[part * TOK : (part + 1) * TOK, :]
        upstream = upstream + dot(placed_rows(by_row[...], part), rows)
    hidden_load.wait()
    grad_load.wait()
    unit, inverse = centered(hidden_in[...])
    made = grad_in[...].astype(FULL) + norm_pull(upstream, unit, inverse, norms[2:3, :])
    total[...] = made
    copies = [start(total, grad_out, sems.at[9])]
    flow[:, FLOW:] = made.astype(LOW)
    gains[...] = jnp.zeros(gains.shape, FULL)
    gains[2:3, :] = jnp.sum(upstream * unit, axis=0, keepdims=True)
    gains[3:4, :] = jnp.sum(upstream, axis=0, keepdims=True)
    for load in weight_loads:
        load.wait()
    above[...] = dot_nt(flow[:, FLOW:], weight[...]).astype(LOW)
    qkv_load.wait()
    probs_load.wait()

    def head_of(part, head):
        return qkv[part, :, head * HEAD_DIM : (head + 1) * HEAD_DIM]

    def above_of(head):
        return above[:, head * HEAD_DIM : (head + 1) * HEAD_DIM]

    def store(part, first, pieces):
        at = part * WIDTH + first * HEAD_DIM
        flow[:, at : at + 2 * HEAD_DIM] = jnp.concatenate(pieces, axis=1).astype(LOW)

    key_at = lax.broadcasted_iota(jnp.int32, (TOK, TOK), 0)
    query_at = lax.broadcasted_iota(jnp.int32, (TOK, TOK), 1)
    allowed = same_document(lengths, query_at, key_at) & (key_at <= query_at)
    for first in range(0, HEADS, 8):
        heads = range(first, first + 8)
        pairs = range(first, first + 8, 2)
        for head in heads:
            raw[head] = dot_nt(above_of(head), head_of(2, head))
            turned[head] = dot_nt(head_of(1, head), head_of(0, head))
            pulled[head] = dot_nt(head_of(2, head), above_of(head))
        for head in heads:
            chance = probs[head].astype(FULL)
            taken = jnp.sum(chance * raw[head], axis=-1, keepdims=True)
            low[head] = (chance * (raw[head] - taken)).astype(LOW)
        for head in heads:
            scores = jnp.where(allowed, turned[head] * SCALE, -1e30)
            raised = jnp.exp(scores - jnp.max(scores, axis=0, keepdims=True))
            chance = raised / jnp.sum(raised, axis=0, keepdims=True)
            chance_turned[head] = chance.astype(LOW)
            taken = jnp.sum(chance * pulled[head], axis=0, keepdims=True)
            low_turned[head] = (chance * (pulled[head] - taken)).astype(LOW)
        for head in pairs:
            both = (head, head + 1)
            store(2, head, [dot(chance_turned[h], above_of(h)) for h in both])
            store(0, head, [dot(low[h], head_of(1, h)) * SCALE for h in both])
            store(1, head, [dot(low_turned[h], head_of(0, h)) * SCALE for h in both])
    for index, target in enumerate(parts_out):
        source = flow.at[:, lanes(lax.rem(place[0, 1] + index, 4) * WIDTH, WIDTH)]
        copies.append(start(source, target, sems.at[10 + index]))
    for copy in copies:
        copy.wait()


def weights_kernel(place, *refs):
    lefts, flows, shares, other_shares, gains_in = refs[:4], refs[4:8], *refs[8:11]
    mine, theirs, left, right, weight, made, gains, sems = refs[11:]
    rep, colour = place[0, 0], place[0, 1]
    loads = []
    for index in range(4):
        rows = pl.ds(index * TOK, TOK)
        loads.append(start(lefts[index], left.at[:, rows], sems.at[index]))
        loads.append(start(flows[index], right.at[rows, :], sems.at[4 + index]))
    small = [start(gains_in, gains, sems.at[8])]
    for side, ref in enumerate((shares, other_shares)):
        rows = lanes((rep if side == 0 else 1 - rep) * HALF, HALF)
        source = ref.at[:, pl.ds(0, WIDTH)]
        small.append(start(source, weight.at[rows, :], sems.at[9 + side]))
        source, target = ref.at[:, pl.ds(WIDTH, 128)], made.at[rows, pl.ds(WIDTH, 128)]
        small.append(start(source, target, sems.at[11 + side]))
    for load in loads:
        load.wait()
    total = jnp.sum(right[...].astype(FULL), axis=0, keepdims=True)
    projects = colour < 3
    copies = []
    for side, (half, target) in enumerate(((1 - rep, theirs), (rep, mine))):
        rows = lanes(half * HALF, HALF)
        value = dot(left[rows, :], right[...])
        made[rows, :WIDTH] = value.astype(LOW)
        if side == 0:
            for load in small:
                load.wait()
            columns = jnp.concatenate([gains[...], jnp.zeros((TOK - 8, WIDTH), FULL)], axis=0)
        weight_half = weight[rows, :].astype(FULL)
        params = made[rows, WIDTH:].astype(FULL)
        bias = jnp.sum(weight_half * total, axis=1, keepdims=True)
        gain = jnp.sum(weight_half * value, axis=1, keepdims=True)
        gain = (gain - params[:, 1:2] * bias) / params[:, 0:1]
        turned = jnp.where(half == 0, columns[:, :HALF], columns[:, HALF:]).T
        lane_at = lax.broadcasted_iota(jnp.int32, (HALF, 128), 1)
        first = jnp.where(projects, gain, 0.0)
        second = jnp.where(projects, bias, 0.0)
        tail = jnp.where(lane_at == 0, first, jnp.where(lane_at == 1, second, turned))
        made[rows, WIDTH:] = tail.astype(LOW)
        copies.append(start(made.at[rows, :], target, sems.at[13 + side]))
    for copy in copies:
        copy.wait()


def add_kernel(mine, theirs, packed, out, held, made, sems):
    loads, copies = [], []
    parts = 2
    size = HALF // parts
    for part in range(parts):
        rows = pl.ds(part * size, size)
        loads.append(
            [
                start(ref.at[rows, :], held.at[side, rows, :], sems.at[2 * part + side])
                for side, ref in enumerate((mine, theirs))
            ]
        )
    for part in range(parts):
        for load in loads[part]:
            load.wait()
        at = slice(part * size, (part + 1) * size)
        made[at, :] = (held[0, at, :].astype(FULL) + held[1, at, :].astype(FULL)).astype(LOW)
        rows = pl.ds(part * size, size)
        target = out.at[rows, pl.ds(0, STAR)]
        copies.append(start(made.at[rows, :], target, sems.at[2 * parts + part]))
    for copy in copies:
        copy.wait()


def input_kernel(place, norms, tokens, hidden_grad, shares, other_shares, *refs):
    received, flows, made_out, scratch = refs[:6], refs[6:10], refs[10], refs[11:]
    tokens_in, grad_in, flow, weights, made, sems = scratch
    loads = []
    for index, pair in enumerate(as_sources(shares, other_shares, received)):
        loads.append([start(flows[index], flow.at[index], sems.at[4 + index])])
        for side, half in enumerate((place[0, 0], 1 - place[0, 0])):
            target = weights.at[index, lanes(half * HALF, HALF), :]
            loads[index].append(start(pair[side], target, sems.at[8 + 2 * index + side]))
    small = [start(tokens, tokens_in, sems.at[0]), start(hidden_grad, grad_in, sems.at[1])]
    upstream = jnp.zeros((TOK, WIDTH), FULL)
    for index in range(4):
        for load in loads[index]:
            load.wait()
        projects = lax.rem(place[0, 1] + index, 4) < 3
        pulled = dot_nt(flow[index], weights[index])
        upstream = upstream + jnp.where(projects, pulled, 0.0)
    for load in small:
        load.wait()
    unit, inverse = centered(tokens_in[...].astype(FULL))
    made[...] = grad_in[...] + norm_pull(upstream, unit, inverse, norms[0:1, :])
    start(made, made_out, sems.at[3]).wait()


def reduce_kernel(by_row, pieces, hidden, query, key, value, output, result, *refs):
    norms, held, hidden_in, sems = refs[:4], *refs[4:]
    hidden_load = start(hidden, hidden_in, sems.at[4])
    loads = []
    for part in range(4):
        rows = pl.ds(part * TOK, TOK)
        loads.append(start(pieces.at[rows, :], held.at[rows, :], sems.at[part]))
    sums = [jnp.zeros((8, WIDTH), FULL) for _ in range(4)]
    tail = jnp.zeros((8, 128), FULL)
    hidden_load.wait()
    made = hidden_in[...]
    for part in range(4):
        loads[part].wait()
        for pair in range(8):
            at = part * TOK + pair * 16
            rows = held[at : at + 16, :STAR].astype(FULL)
            for side in range(2):
                index = part * 16 + pair * 2 + side
                y, x, z = index // 16, index // 4 % 4, index % 4
                colour = (x + 2 * y - z) % 4
                piece = rows[side * 8 : (side + 1) * 8, :]
                sums[colour] = sums[colour] + piece[:, :WIDTH]
                tail = tail + piece[:, WIDTH:]
        at = slice(part * TOK, (part + 1) * TOK)
        made = made + dot(placed_rows(by_row[...], part), held[at, STAR:])
    result[...] = made.astype(LOW)
    for ref, total in zip((query, key, value, output), sums):
        ref[...] = total
    tail = jnp.concatenate([tail, jnp.zeros((TOK - 8, 128), FULL)], axis=0).T
    for index, norm in enumerate(norms):
        norm[...] = tail[index : index + 1, :8]


def tied(*values):
    return lax.optimization_barrier(values)


def per_device(
    tokens,
    hash_ids,
    doc_lengths,
    w_query,
    w_key,
    w_value,
    w_output,
    norm1_gain,
    norm1_bias,
    norm2_gain,
    norm2_bias,
    expert_in,
    expert_out,
    load_average,
    out_grad,
):
    experts = load_average.shape[0]
    groups = lax.axis_size("exp")
    devices = 2 * groups
    rep = lax.axis_index("rep")
    at = lax.axis_index("exp")
    y, x, z = lax.div(at, LINE * LINE), lax.rem(lax.div(at, LINE), LINE), lax.rem(at, LINE)
    colour = lax.rem(x + 2 * y + 3 * z, 4)
    place = jnp.stack([rep, colour]).astype(jnp.int32).reshape(1, 2)
    weight_in, weight_out = expert_in[0], expert_out[0]
    hidden = weight_in.shape[1]

    norm_params = jnp.concatenate([norm1_gain, norm1_bias, norm2_gain, norm2_bias]).reshape(1, 32)
    packed, slot, by_row = kernel_call(
        pack_kernel,
        [VMEM] + [HBM] * 6,
        [
            ((SLOTS, LAST), LOW, HBM),
            ((1, TOK), jnp.int32, VMEM),
            ((TOK, TOK), jnp.int32, VMEM),
        ],
        scratch=[
            ((1, TOK), jnp.int32),
            ((4, 8, WIDTH), LOW),
            ((TOK, WIDTH), LOW),
            ((4, 32, STAR), LOW),
            ((SLOTS, WIDTH), LOW),
        ],
        copies=26,
        flops=2 * SLOTS * TOK * WIDTH,
        moved=6 << 20,
        name="pack",
    )(norm_params, hash_ids.reshape(1, TOK), w_query, w_key, w_value, w_output, out_grad)
    shares = exchange(packed.reshape(groups, 8, LAST)).reshape(SLOTS, LAST)
    weight_in_other, weight_out_other = swap(weight_in), swap(weight_out)
    shares, place, weight_in_other, weight_out_other = tied(
        shares, place, weight_in_other, weight_out_other
    )
    (own,) = kernel_call(
        split_kernel,
        [HBM],
        [((SLOTS, WIDTH), LOW, HBM)],
        scratch=[((SLOTS, WIDTH), LOW)],
        copies=2,
        moved=2 << 20,
        name="split",
    )(shares)
    received = [between(own, ways, True) for ways in WAYS]
    other_shares = swap(shares)
    grad_rows = shares[:, STAR:]
    up_own = dot_nt(grad_rows, weight_out).astype(LOW)
    received[0], up_own = tied(received[0], up_own)
    received = [one for part in received for one in (part, swap(part))]

    def send(rows):
        return exchange(rows.reshape(groups, CAPACITY, WIDTH)).reshape(SLOTS, WIDTH)

    outgoing, hidden_one, qkv, probs, joined, normed, norms, extra = kernel_call(
        attend_kernel,
        [SMEM, VMEM, SMEM] + [HBM] * 9,
        [
            ((SLOTS, WIDTH), LOW, HBM),
            ((TOK, WIDTH), FULL, HBM),
            ((3, TOK, WIDTH), LOW, HBM),
            ((HEADS, TOK, TOK), LOW, HBM),
            ((TOK, WIDTH), LOW, HBM),
            ((TOK, WIDTH), LOW, HBM),
            ((8, WIDTH), FULL, HBM),
            ((WIDTH, 128), LOW, HBM),
        ],
        scratch=[
            ((TOK, WIDTH), LOW),
            ((WIDTH, 128), LOW),
            ((4, WIDTH, WIDTH), LOW),
            ((8, WIDTH), FULL),
            ((TOK, WIDTH), LOW),
            ((3, TOK, WIDTH), LOW),
            ((HEADS, TOK, TOK), FULL),
            ((HEADS, TOK, TOK), LOW),
            ((TOK, WIDTH), LOW),
            ((TOK, WIDTH), FULL),
            ((SLOTS, WIDTH), LOW),
        ],
        copies=32,
        flops=2 * TOK * WIDTH * 5000,
        moved=12 << 20,
        name="attend",
    )(place, slot, doc_lengths, shares, other_shares, *received, tokens)

    up_other = dot_nt(grad_rows, weight_out_other).astype(LOW)
    rows, up_own, up_other = tied(send(outgoing), up_own, up_other)
    lefts = kernel_call(
        left_kernel,
        [SMEM] + [HBM] * 2,
        [((WIDTH, TOK), LOW, HBM)] * 4,
        scratch=[((2, TOK, WIDTH), LOW), ((2, WIDTH, TOK), LOW)],
        copies=6,
        moved=2 << 20,
        name="left",
    )(place, normed, joined)
    rows, *lefts = tied(rows, *lefts)

    back_rows, *acts_flows = kernel_call(
        expert_kernel,
        [HBM] * 5,
        [
            ((SLOTS, WIDTH), LOW, HBM),
        ]
        + [((SLOTS, hidden), LOW, HBM)] * 4,
        scratch=[
            ((SLOTS, WIDTH), LOW),
            ((WIDTH, 2 * hidden), LOW),
            ((SLOTS, 2 * hidden), LOW),
            ((SLOTS, 2 * hidden), LOW),
            ((SLOTS, 2 * hidden), LOW),
            ((SLOTS, WIDTH), LOW),
        ],
        copies=3 + 8 * (hidden // 512),
        flops=8 * SLOTS * WIDTH * hidden,
        moved=24 << 20,
        name="expert",
    )(rows, weight_in, weight_in_other, up_own, up_other)
    act, act_theirs, flow, flow_theirs = acts_flows
    back_rows, *lefts = tied(back_rows, *lefts)
    far_lefts = [between(left, ways, False) for left, ways in zip(lefts[1:], WAYS)]
    lefts = [lefts[0]] + far_lefts
    back = send(back_rows)
    (result,) = kernel_call(
        result_kernel,
        [HBM] * 4,
        [((SLOTS, LAST), LOW, HBM)],
        scratch=[
            ((2, SLOTS, hidden), LOW),
            ((2, hidden, WIDTH), LOW),
            ((SLOTS, WIDTH), FULL),
        ],
        copies=5,
        flops=4 * SLOTS * hidden * WIDTH,
        moved=14 << 20,
        name="result",
    )(act, act_theirs, weight_out, weight_out_other)
    act_other, flow_other = swap(act_theirs), swap(flow_theirs)
    back, result, act_other, flow_other, *lefts = tied(
        back, result, act_other, flow_other, *lefts
    )

    hidden_grad, *parts, gains = kernel_call(
        attend_back_kernel,
        [SMEM, VMEM, SMEM, VMEM] + [HBM] * 13,
        [
            ((TOK, WIDTH), FULL, HBM),
        ]
        + [((TOK, WIDTH), LOW, HBM)] * 4
        + [
            ((8, WIDTH), FULL, VMEM),
        ],
        scratch=[
            ((SLOTS, WIDTH), LOW),
            ((TOK, WIDTH), FULL),
            ((TOK, WIDTH), LOW),
            ((WIDTH, WIDTH), LOW),
            ((3, TOK, WIDTH), LOW),
            ((HEADS, TOK, TOK), LOW),
            ((TOK, WIDTH), FULL),
            ((TOK, WIDTH), LOW),
            ((TOK, ALL), LOW),
            ((HEADS, TOK, TOK), FULL),
            ((HEADS, TOK, TOK), FULL),
            ((HEADS, TOK, TOK), FULL),
            ((HEADS, TOK, TOK), LOW),
            ((HEADS, TOK, TOK), LOW),
            ((HEADS, TOK, TOK), LOW),
        ],
        copies=19,
        flops=2 * TOK * WIDTH * 3000,
        moved=8 << 20,
        name="attend_back",
    )(
        place,
        by_row,
        doc_lengths,
        norms,
        back,
        hidden_one,
        out_grad,
        shares,
        other_shares,
        *received,
        qkv,
        probs,
    )
    own_parts = parts
    parts = [parts[0]] + [between(part, ways, False) for part, ways in zip(parts[1:], WAYS)]
    mine, theirs = kernel_call(
        weights_kernel,
        [SMEM] + [HBM] * 11,
        [((HALF, STAR), LOW, HBM)] * 2,
        scratch=[
            ((WIDTH, 4 * TOK), LOW),
            ((4 * TOK, WIDTH), LOW),
            ((WIDTH, WIDTH), LOW),
            ((WIDTH, STAR), LOW),
            ((8, WIDTH), FULL),
        ],
        copies=15,
        flops=8 * TOK * WIDTH * WIDTH,
        moved=8 << 20,
        name="weights",
    )(place, *lefts, *parts, shares, other_shares, gains)
    (weight_part,) = kernel_call(
        add_kernel,
        [HBM] * 3,
        [((SLOTS, LAST), LOW, HBM)],
        scratch=[((2, HALF, STAR), LOW), ((HALF, STAR), LOW)],
        copies=6,
        moved=4 << 20,
        name="add",
        aliases={2: 0},
    )(mine, swap(theirs), result)
    pieces = exchange(weight_part.reshape(groups, 8, LAST)).reshape(SLOTS, LAST)

    act, flow, rows, *own_parts, _ = tied(act, flow, rows, *own_parts, weight_part)
    rows_other = swap(rows)
    out_weight_grad = weight_grad_call((shares, other_shares), STAR, (act, act_other), True)
    in_weight_grad = weight_grad_call((rows, rows_other), 0, (flow, flow_other), False)
    (input_grad,) = kernel_call(
        input_kernel,
        [SMEM, VMEM] + [HBM] * 14,
        [((TOK, WIDTH), FULL, HBM)],
        scratch=[
            ((TOK, WIDTH), LOW),
            ((TOK, WIDTH), FULL),
            ((4, TOK, WIDTH), LOW),
            ((4, WIDTH, WIDTH), LOW),
            ((TOK, WIDTH), FULL),
        ],
        copies=20,
        flops=2 * TOK * WIDTH * FLOW,
        moved=8 << 20,
        name="input_grad",
    )(place, norms, tokens, hidden_grad, shares, other_shares, *received, *own_parts)
    tails = extra[:, 64:].reshape(devices, 8, experts)[:, 0]
    counts = jnp.sum(tails.astype(FULL), axis=0)
    new_average = 0.7 * load_average + 0.3 * counts
    counts = counts.astype(jnp.int32)
    pieces, out_weight_grad, in_weight_grad, input_grad, counts, new_average = tied(
        pieces, out_weight_grad, in_weight_grad, input_grad, counts, new_average
    )
    *grads, output, gain_one, bias_one, gain_two, bias_two = kernel_call(
        reduce_kernel,
        [VMEM, HBM, HBM],
        [((8, WIDTH), FULL, VMEM)] * 4
        + [((TOK, WIDTH), LOW, VMEM)]
        + [((1, 8), FULL, VMEM)] * 4,
        scratch=[((SLOTS, LAST), LOW), ((TOK, WIDTH), FULL)],
        copies=5,
        moved=5 << 20,
        name="reduce",
    )(by_row, pieces, hidden_one)
    return (
        output,
        input_grad,
        *grads,
        gain_one.reshape(8),
        bias_one.reshape(8),
        gain_two.reshape(8),
        bias_two.reshape(8),
        in_weight_grad[None],
        out_weight_grad[None],
        counts,
        new_average,
    )


def solution(mesh):
    rows = P(("rep", "exp"), None)
    vector = P(("rep", "exp"))
    return jax.shard_map(
        per_device,
        mesh=mesh,
        in_specs=(rows,) * 7
        + (vector,) * 4
        + (P("exp", None, "rep"), P("exp", "rep", None), P(), rows),
        out_specs=(rows,) * 6
        + (vector,) * 4
        + (P("exp", None, "rep"), P("exp", "rep", None), P(), P()),
        check_vma=False,
    )
```

```python
import functools

import jax
import jax.numpy as jnp
from jax import lax
from jax.experimental import pallas as pl
from jax.experimental.pallas import tpu as pltpu
from jax.sharding import PartitionSpec as P

HEADS = 16
HEAD_DIM = 64
SCALE = HEAD_DIM ** (-0.5)
EPSILON = 1e-05
SWAP = [(0, 1), (1, 0)]
CAPACITY = 8
TOK = 128
WIDTH = 1024
HALF = WIDTH // 2
SLOTS = 512
FLOW = 3 * WIDTH
ALL = 4 * WIDTH
LENGTH = ALL + 128
STAR = WIDTH + 128
LAST = STAR + WIDTH
LINE = 4
VMEM_BYTES = 511 << 17
LOW = jnp.bfloat16
FULL = jnp.float32
VMEM = pl.BlockSpec(memory_space=pltpu.VMEM)
SMEM = pl.BlockSpec(memory_space=pltpu.SMEM)
HBM = pl.BlockSpec(memory_space=pltpu.HBM)


def swap(value):
    return lax.ppermute(value, "rep", SWAP)


def moved_on(index, stride, step):
    at = index // stride % LINE
    return index + ((at + step) % LINE - at) * stride


WAYS = (((LINE, 1), (1, -1)), ((LINE * LINE, 1), (LINE * LINE, -1)), ((LINE, -1), (1, 1)))


def between(value, ways, back):
    count = lax.axis_size("exp")
    pairs = []
    for rep, way in enumerate(ways):
        for index in range(count):
            near, far = rep * count + index, rep * count + moved_on(index, *way)
            pairs.append((far, near) if back else (near, far))
    return lax.ppermute(value, ("rep", "exp"), pairs)


def exchange(value):
    return lax.all_to_all(value, "exp", split_axis=0, concat_axis=0, tiled=True)


def dot(left, right):
    return jnp.dot(left, right, preferred_element_type=FULL)


def dot_nt(left, right):
    return lax.dot_general(left, right, (((1,), (1,)), ((), ())), preferred_element_type=FULL)


def dot_tn(left, right):
    return lax.dot_general(left, right, (((0,), (0,)), ((), ())), preferred_element_type=FULL)


def kernel_call(
    body, specs, outs, scratch=(), copies=0, flops=0, moved=0, name=None, aliases=None
):
    shapes = [pltpu.VMEM(shape, dtype) for shape, dtype in scratch]
    if copies:
        shapes.append(pltpu.SemaphoreType.DMA((copies,)))
    return pl.pallas_call(
        body,
        in_specs=specs,
        out_specs=[spec for _, _, spec in outs],
        out_shape=[jax.ShapeDtypeStruct(shape, dtype) for shape, dtype, _ in outs],
        scratch_shapes=shapes,
        input_output_aliases=aliases or {},
        compiler_params=pltpu.CompilerParams(vmem_limit_bytes=VMEM_BYTES),
        cost_estimate=pl.CostEstimate(flops=flops, bytes_accessed=moved, transcendentals=0),
        name=name,
    )


def start(source, target, sem):
    copy = pltpu.make_async_copy(source, target, sem)
    copy.start()
    return copy


def lanes(first, size):
    return pl.ds(pl.multiple_of(first, size), size)


def load_all(sources, place, weights, sems, first):
    loads = []
    for index, pair in enumerate(sources):
        matrix = lax.rem(place[0, 1] + index, 4)
        for side, half in enumerate((place[0, 0], 1 - place[0, 0])):
            target = weights.at[matrix, lanes(half * HALF, HALF), :]
            loads.append(start(pair[side], target, sems.at[first + 2 * index + side]))
    return loads


def load_one(sources, place, matrix, weight, sems, first):
    loads = []
    for side, half in enumerate((place[0, 0], 1 - place[0, 0])):
        target, sem = weight.at[lanes(half * HALF, HALF), :], sems.at[first + side]
        for index, pair in enumerate(sources):

            @pl.when(lax.rem(place[0, 1] + index, 4) == matrix)
            def _(source=pair[side], target=target, sem=sem):
                pltpu.make_async_copy(source, target, sem).start()

        loads.append(pltpu.make_async_copy(sources[1][side], target, sem))
    return loads


def as_sources(shares, other_shares, received):
    at = pl.ds(0, WIDTH)
    pairs = [(shares, other_shares)]
    pairs += [(received[2 * index], received[2 * index + 1]) for index in range(3)]
    return [(own.at[:, at], other.at[:, at]) for own, other in pairs]


def centered(rows):
    center = rows - jnp.mean(rows, axis=-1, keepdims=True)
    spread = jnp.mean(center * center, axis=-1, keepdims=True)
    inverse = lax.rsqrt(spread + EPSILON)
    return center * inverse, inverse


def norm_pull(upstream, unit, inverse, gain):
    scaled = upstream * gain
    return inverse * (
        scaled
        - jnp.mean(scaled, axis=-1, keepdims=True)
        - unit * jnp.mean(scaled * unit, axis=-1, keepdims=True)
    )


def same_document(lengths, query_at, key_at):
    end = jnp.int32(0)
    query_doc = jnp.zeros((TOK, TOK), jnp.int32)
    key_doc = jnp.zeros((TOK, TOK), jnp.int32)
    for j in range(3):
        end = end + lengths[0, j]
        query_doc += (query_at >= end).astype(jnp.int32)
        key_doc += (key_at >= end).astype(jnp.int32)
    return query_doc == key_doc


def placed(slot, part):
    row_at = lax.broadcasted_iota(jnp.int32, (TOK, TOK), 0) + part * TOK
    return (row_at == slot).astype(LOW)


def pack_kernel(norms, ids, query, key, value, output, grad, packed, laid, slot, by_row, *scratch):
    ids_in, rows, grad_in, lined, rows_made, sems = scratch
    loads = [start(ids, ids_in, sems.at[0])]
    for index, ref in enumerate((query, key, value, output)):
        loads.append(start(ref, rows.at[index], sems.at[1 + index]))
    grad_load = start(grad, grad_in, sems.at[5])
    row = jnp.concatenate([norms[...].astype(FULL), jnp.zeros((1, TOK - 32), FULL)], axis=1)
    tile = jnp.broadcast_to(row, (TOK, TOK)).T
    lane_at = lax.broadcasted_iota(jnp.int32, (8, TOK), 1)
    params = jnp.zeros((8, TOK), FULL)
    for index in range(4):
        params = params + jnp.where(lane_at == index, tile[index * 8 : (index + 1) * 8, :], 0.0)
    loads[0].wait()
    row_at = lax.broadcasted_iota(jnp.int32, (TOK, TOK), 0)
    column_at = lax.broadcasted_iota(jnp.int32, (TOK, TOK), 1)
    by_column = jnp.broadcast_to(ids_in[...].astype(FULL), (TOK, TOK))
    before = (by_column.T == by_column) & (row_at < column_at)
    rank = jnp.sum(before.astype(FULL), axis=0, keepdims=True).astype(jnp.int32)
    target = ids_in[...] * CAPACITY + rank
    slot[...] = target
    by_row[...] = jnp.broadcast_to(target.astype(FULL), (TOK, TOK)).T.astype(jnp.int32)
    chosen = (ids_in[...] == row_at - 64).astype(LOW)
    counts = dot_nt(jnp.ones((8, TOK), LOW), chosen)
    first = lax.broadcasted_iota(jnp.int32, (8, TOK), 0) == 0
    extra = params + jnp.where(first, counts, 0.0)
    for load in loads[1:]:
        load.wait()
    rows_full = [rows[index].astype(FULL) for index in range(4)]
    copies = []
    for base in range(4):
        made = [
            jnp.concatenate([rows_full[(base + 3 * z) % 4], extra], axis=1) for z in range(LINE)
        ]
        lined[base] = jnp.concatenate(made, axis=0).astype(LOW)
    for y in range(LINE):
        for x in range(LINE):
            index = y * LINE + x
            at = packed.at[pl.ds(index * 32, 32), :]
            copies.append(start(lined.at[(x + 2 * y) % 4], at, sems.at[6 + index]))
    grad_load.wait()
    for part in range(4):
        at = pl.ds(part * TOK, TOK)
        rows_made[at, :] = dot(placed(target, part), grad_in[...]).astype(LOW)
        copies.append(start(rows_made.at[at, :], laid.at[at, :], sems.at[22 + part]))
    for copy in copies:
        copy.wait()


def placed_rows(by_row, part):
    lane_at = lax.broadcasted_iota(jnp.int32, (TOK, TOK), 1) + part * TOK
    return (lane_at == by_row).astype(LOW)


def attend_kernel(
    place, slot, lengths, shares, other_shares, *refs
):
    received, tokens, refs = refs[:6], refs[6], refs[7:]
    outgoing_out, hidden_out, qkv_out, probs_out, joined_out, normed_out = refs[:6]
    norms_out, extra_out, *scratch = refs[6:]
    tokens_in, extra, weights, norms, normed, qkv, raw, low, joined, hidden, outgoing, sems = scratch
    rep = place[0, 0]
    extra_loads = []
    for side, ref in enumerate((shares, other_shares)):
        rows = lanes((rep if side == 0 else 1 - rep) * HALF, HALF)
        source = ref.at[:, pl.ds(WIDTH, 128)]
        extra_loads.append(start(source, extra.at[rows, :], sems.at[18 + side]))
    tokens_load = start(tokens, tokens_in, sems.at[1])
    sources = as_sources(shares, other_shares, received)
    weight_loads = load_all(sources, place, weights, sems, 20)
    for load in extra_loads:
        load.wait()
    norms[...] = extra[...].astype(FULL).T[:8, :]
    copies = [start(norms, norms_out, sems.at[6]), start(extra, extra_out, sems.at[0])]
    tokens_load.wait()
    inputs = tokens_in[...].astype(FULL)
    unit, _ = centered(inputs)
    normed[...] = (unit * norms[0:1, :] + norms[1:2, :]).astype(LOW)
    copies.append(start(normed, normed_out, sems.at[7]))
    for load in weight_loads:
        load.wait()
    for index in range(3):
        qkv[index] = dot(normed[...], weights[index]).astype(LOW)
    copies.append(start(qkv, qkv_out, sems.at[8]))

    query_at = lax.broadcasted_iota(jnp.int32, (TOK, TOK), 0)
    key_at = lax.broadcasted_iota(jnp.int32, (TOK, TOK), 1)
    allowed = same_document(lengths, query_at, key_at) & (key_at <= query_at)
    for first in range(0, HEADS, 8):
        heads = range(first, first + 8)
        for head in heads:
            at = slice(head * HEAD_DIM, (head + 1) * HEAD_DIM)
            raw[head] = dot_nt(qkv[0, :, at], qkv[1, :, at])
        for head in heads:
            scores = jnp.where(allowed, raw[head] * SCALE, -1e30)
            raised = jnp.exp(scores - jnp.max(scores, axis=-1, keepdims=True))
            chance = raised / jnp.sum(raised, axis=-1, keepdims=True)
            low[head] = chance.astype(LOW)
        block = pl.ds(first, 8)
        copies.append(start(low.at[block], probs_out.at[block], sems.at[9 + first // 8]))
        for head in range(first, first + 8, 2):
            made = []
            for one in (head, head + 1):
                made.append(dot(low[one], qkv[2, :, one * HEAD_DIM : (one + 1) * HEAD_DIM]))
            at = slice(head * HEAD_DIM, (head + 2) * HEAD_DIM)
            joined[:, at] = jnp.concatenate(made, axis=1).astype(LOW)
    copies.append(start(joined, joined_out, sems.at[28]))
    made = inputs + dot(joined[...], weights[3])
    hidden[...] = made
    copies.append(start(hidden, hidden_out, sems.at[13]))
    unit, _ = centered(made)
    second = (unit * norms[2:3, :] + norms[3:4, :]).astype(LOW)
    for part in range(4):
        rows = pl.ds(part * TOK, TOK)
        outgoing[rows, :] = dot(placed(slot[...], part), second).astype(LOW)
        copies.append(start(outgoing.at[rows, :], outgoing_out.at[rows, :], sems.at[14 + part]))
    for copy in copies:
        copy.wait()


def left_kernel(place, normed, joined, *refs):
    targets, held, turned, sems = refs[:4], refs[4], refs[5], refs[6]
    loads = [start(ref, held.at[i], sems.at[i]) for i, ref in enumerate((normed, joined))]
    for index, load in enumerate(loads):
        load.wait()
        turned[index] = held[index].T
    copies = []
    for index, target in enumerate(targets):
        kind = lax.div(lax.rem(place[0, 1] + index, 4), 3)
        copies.append(start(turned.at[kind], target, sems.at[2 + index]))
    for copy in copies:
        copy.wait()


def gelu_parts(pre):
    square = pre * pre
    turn = jnp.tanh(pre * (0.7978845608028654 + 0.035677408136300125 * square))
    half = 0.5 + 0.5 * turn
    slope = half + (0.5 - 0.5 * turn * turn) * (
        pre * (0.7978845608028654 + 0.10703222440890037 * square)
    )
    return pre * half, slope


def expert_kernel(rows_in, weight_own, weight_other, up_own, up_other, out, *refs):
    acts, flows, scratch = refs[:2], refs[2:4], refs[4:]
    rows, weight, up, act, flow, back, sems = scratch
    hidden = weight.shape[1]
    half = hidden // 2
    chunk = 1024
    parts = hidden // chunk

    def load(j):
        cols = pl.ds(j * chunk, chunk)
        at = pl.ds(j * chunk % half, chunk)
        weight_in, up_in = (weight_own, up_own) if j * chunk < half else (weight_other, up_other)
        return (
            start(weight_in.at[:, at], weight.at[:, cols], sems.at[1 + j]),
            start(up_in.at[:, at], up.at[:, cols], sems.at[1 + parts + j]),
        )

    rows_load = start(rows_in, rows, sems.at[0])
    loads = [load(0), load(1)]
    rows_load.wait()
    copies = []
    for j in range(parts):
        cols = slice(j * chunk, (j + 1) * chunk)
        if j + 2 < parts:
            loads.append(load(j + 2))
        for copy in loads[j]:
            copy.wait()
        value, slope = gelu_parts(dot(rows[...], weight[:, cols]))
        act[:, cols] = value.astype(LOW)
        flow[:, cols] = (up[:, cols].astype(FULL) * slope).astype(LOW)
        at = pl.ds(j * chunk, chunk)
        side = j * chunk // half
        target_at = pl.ds(j * chunk % half, chunk)
        for index, (source, targets) in enumerate(((act, acts), (flow, flows))):
            sem = sems.at[1 + 2 * parts + 2 * j + index]
            copies.append(start(source.at[:, at], targets[side].at[:, target_at], sem))
    for index in range(2):
        block = slice(index * 256, (index + 1) * 256)
        back[block, :] = dot_nt(flow[block, :], weight[...]).astype(LOW)
        at = pl.ds(index * 256, 256)
        copies.append(start(back.at[at, :], out.at[at, :], sems.at[1 + 4 * parts + index]))
    for copy in copies:
        copy.wait()


def result_kernel(act_own, act_other, weight_own, weight_other, out, act, weight, made, sems):
    sides = []
    for side, (act_in, weight_in) in enumerate(((act_own, weight_own), (act_other, weight_other))):
        sides.append(
            [
                start(act_in, act.at[side], sems.at[2 * side]),
                start(weight_in, weight.at[side], sems.at[2 * side + 1]),
            ]
        )
        if side == 0:
            for load in sides[0]:
                load.wait()
    made[...] = dot(act[0], weight[0])
    for load in sides[1]:
        load.wait()
    act[0, :, :WIDTH] = (made[...] + dot(act[1], weight[1])).astype(LOW)
    source = act.at[0, :, pl.ds(0, WIDTH)]
    start(source, out.at[:, pl.ds(STAR, WIDTH)], sems.at[4]).wait()


def weight_grad_kernel(by_rows, at, first, second, streamed_first, streamed_second, made, held, sems):
    half = first.shape[0]
    cols = pl.ds(at, held.shape[1])

    @pl.when(pl.program_id(0) == 0)
    def _():
        loads = [
            start(first.at[:, cols], held.at[pl.ds(0, half), :], sems.at[0]),
            start(second.at[:, cols], held.at[pl.ds(half, half), :], sems.at[1]),
        ]
        for load in loads:
            load.wait()

    streamed = jnp.concatenate([streamed_first[...], streamed_second[...]], axis=0)
    made[...] = dot_tn(streamed, held[...]) if by_rows else dot_tn(held[...], streamed)


def weight_grad_call(held, at, streamed, by_rows, tile=1024):
    rows, wide = streamed[0].shape
    width = WIDTH
    shape = (wide, width) if by_rows else (width, wide)
    block = (tile, width) if by_rows else (width, tile)
    return pl.pallas_call(
        functools.partial(weight_grad_kernel, by_rows, at),
        grid=(wide // tile,),
        in_specs=[HBM, HBM] + [pl.BlockSpec((rows, tile), lambda i: (0, i))] * 2,
        out_specs=pl.BlockSpec(block, (lambda i: (i, 0)) if by_rows else (lambda i: (0, i))),
        out_shape=jax.ShapeDtypeStruct(shape, FULL),
        scratch_shapes=[pltpu.VMEM((2 * rows, width), LOW), pltpu.SemaphoreType.DMA((2,))],
        compiler_params=pltpu.CompilerParams(
            dimension_semantics=("arbitrary",), vmem_limit_bytes=VMEM_BYTES
        ),
        cost_estimate=pl.CostEstimate(
            flops=4 * rows * wide * width, bytes_accessed=14 << 20, transcendentals=0
        ),
        name="weight_grad",
    )(*held, *streamed)


def attend_back_kernel(
    place, by_row, lengths, norms, back, hidden, grad, shares, other_shares, *refs
):
    received, (qkv_in, probs_in, grad_out) = refs[:6], refs[6:9]
    parts_out, gains, scratch = refs[9:13], refs[13], refs[14:]
    back_in, hidden_in, grad_in, weight, qkv, probs, total, above, flow, *scratch = scratch
    raw, turned, pulled, low, low_turned, chance_turned, sems = scratch
    back_loads = []
    for part in range(2):
        at = pl.ds(part * 2 * TOK, 2 * TOK)
        back_loads.append(start(back.at[at, :], back_in.at[at, :], sems.at[part]))
    hidden_load = start(hidden, hidden_in, sems.at[4])
    grad_load = start(grad, grad_in, sems.at[5])
    sources = as_sources(shares, other_shares, received)
    weight_loads = load_one(sources, place, 3, weight, sems, 15)
    qkv_load = start(qkv_in, qkv, sems.at[7])
    probs_load = start(probs_in, probs, sems.at[8])
    upstream = jnp.zeros((TOK, WIDTH), FULL)
    for part in range(4):
        if part % 2 == 0:
            back_loads[part // 2].wait()
        rows = back_in[part * TOK : (part + 1) * TOK, :]
        upstream = upstream + dot(placed_rows(by_row[...], part), rows)
    hidden_load.wait()
    grad_load.wait()
    unit, inverse = centered(hidden_in[...])
    made = grad_in[...].astype(FULL) + norm_pull(upstream, unit, inverse, norms[2:3, :])
    total[...] = made
    copies = [start(total, grad_out, sems.at[9])]
    flow[:, FLOW:] = made.astype(LOW)
    gains[...] = jnp.zeros(gains.shape, FULL)
    gains[2:3, :] = jnp.sum(upstream * unit, axis=0, keepdims=True)
    gains[3:4, :] = jnp.sum(upstream, axis=0, keepdims=True)
    for load in weight_loads:
        load.wait()
    above[...] = dot_nt(flow[:, FLOW:], weight[...]).astype(LOW)
    qkv_load.wait()
    probs_load.wait()

    def head_of(part, head):
        return qkv[part, :, head * HEAD_DIM : (head + 1) * HEAD_DIM]

    def above_of(head):
        return above[:, head * HEAD_DIM : (head + 1) * HEAD_DIM]

    def store(part, first, pieces):
        at = part * WIDTH + first * HEAD_DIM
        flow[:, at : at + 2 * HEAD_DIM] = jnp.concatenate(pieces, axis=1).astype(LOW)

    key_at = lax.broadcasted_iota(jnp.int32, (TOK, TOK), 0)
    query_at = lax.broadcasted_iota(jnp.int32, (TOK, TOK), 1)
    allowed = same_document(lengths, query_at, key_at) & (key_at <= query_at)
    for first in range(0, HEADS, 8):
        heads = range(first, first + 8)
        pairs = range(first, first + 8, 2)
        for head in heads:
            raw[head] = dot_nt(above_of(head), head_of(2, head))
            turned[head] = dot_nt(head_of(1, head), head_of(0, head))
            pulled[head] = dot_nt(head_of(2, head), above_of(head))
        for head in heads:
            chance = probs[head].astype(FULL)
            taken = jnp.sum(chance * raw[head], axis=-1, keepdims=True)
            low[head] = (chance * (raw[head] - taken)).astype(LOW)
        for head in heads:
            scores = jnp.where(allowed, turned[head] * SCALE, -1e30)
            raised = jnp.exp(scores - jnp.max(scores, axis=0, keepdims=True))
            chance = raised / jnp.sum(raised, axis=0, keepdims=True)
            chance_turned[head] = chance.astype(LOW)
            taken = jnp.sum(chance * pulled[head], axis=0, keepdims=True)
            low_turned[head] = (chance * (pulled[head] - taken)).astype(LOW)
        for head in pairs:
            both = (head, head + 1)
            store(2, head, [dot(chance_turned[h], above_of(h)) for h in both])
            store(0, head, [dot(low[h], head_of(1, h)) * SCALE for h in both])
            store(1, head, [dot(low_turned[h], head_of(0, h)) * SCALE for h in both])
    for index, target in enumerate(parts_out):
        source = flow.at[:, lanes(lax.rem(place[0, 1] + index, 4) * WIDTH, WIDTH)]
        copies.append(start(source, target, sems.at[10 + index]))
    for copy in copies:
        copy.wait()


def weights_kernel(place, *refs):
    lefts, flows, shares, other_shares, gains_in = refs[:4], refs[4:8], *refs[8:11]
    mine, theirs, left, right, weight, made, gains, sems = refs[11:]
    rep, colour = place[0, 0], place[0, 1]
    loads = []
    for index in range(4):
        rows = pl.ds(index * TOK, TOK)
        loads.append(start(lefts[index], left.at[:, rows], sems.at[index]))
        loads.append(start(flows[index], right.at[rows, :], sems.at[4 + index]))
    small = [start(gains_in, gains, sems.at[8])]
    for side, ref in enumerate((shares, other_shares)):
        rows = lanes((rep if side == 0 else 1 - rep) * HALF, HALF)
        source = ref.at[:, pl.ds(0, WIDTH)]
        small.append(start(source, weight.at[rows, :], sems.at[9 + side]))
        source, target = ref.at[:, pl.ds(WIDTH, 128)], made.at[rows, pl.ds(WIDTH, 128)]
        small.append(start(source, target, sems.at[11 + side]))
    for load in loads:
        load.wait()
    total = jnp.sum(right[...].astype(FULL), axis=0, keepdims=True)
    projects = colour < 3
    copies = []
    for side, (half, target) in enumerate(((1 - rep, theirs), (rep, mine))):
        rows = lanes(half * HALF, HALF)
        value = dot(left[rows, :], right[...])
        made[rows, :WIDTH] = value.astype(LOW)
        if side == 0:
            for load in small:
                load.wait()
            columns = jnp.concatenate([gains[...], jnp.zeros((TOK - 8, WIDTH), FULL)], axis=0)
        weight_half = weight[rows, :].astype(FULL)
        params = made[rows, WIDTH:].astype(FULL)
        bias = jnp.sum(weight_half * total, axis=1, keepdims=True)
        gain = jnp.sum(weight_half * value, axis=1, keepdims=True)
        gain = (gain - params[:, 1:2] * bias) / params[:, 0:1]
        turned = jnp.where(half == 0, columns[:, :HALF], columns[:, HALF:]).T
        lane_at = lax.broadcasted_iota(jnp.int32, (HALF, 128), 1)
        first = jnp.where(projects, gain, 0.0)
        second = jnp.where(projects, bias, 0.0)
        tail = jnp.where(lane_at == 0, first, jnp.where(lane_at == 1, second, turned))
        made[rows, WIDTH:] = tail.astype(LOW)
        copies.append(start(made.at[rows, :], target, sems.at[13 + side]))
    for copy in copies:
        copy.wait()


def input_kernel(place, norms, tokens, hidden_grad, shares, other_shares, *refs):
    received, flows, made_out, scratch = refs[:6], refs[6:10], refs[10], refs[11:]
    tokens_in, grad_in, flow, weights, made, sems = scratch
    loads = []
    for index, pair in enumerate(as_sources(shares, other_shares, received)):
        loads.append([start(flows[index], flow.at[index], sems.at[4 + index])])
        for side, half in enumerate((place[0, 0], 1 - place[0, 0])):
            target = weights.at[index, lanes(half * HALF, HALF), :]
            loads[index].append(start(pair[side], target, sems.at[8 + 2 * index + side]))
    small = [start(tokens, tokens_in, sems.at[0]), start(hidden_grad, grad_in, sems.at[1])]
    upstream = jnp.zeros((TOK, WIDTH), FULL)
    for index in range(4):
        for load in loads[index]:
            load.wait()
        projects = lax.rem(place[0, 1] + index, 4) < 3
        pulled = dot_nt(flow[index], weights[index])
        upstream = upstream + jnp.where(projects, pulled, 0.0)
    for load in small:
        load.wait()
    unit, inverse = centered(tokens_in[...].astype(FULL))
    made[...] = grad_in[...] + norm_pull(upstream, unit, inverse, norms[0:1, :])
    start(made, made_out, sems.at[3]).wait()


def reduce_kernel(by_row, pieces, hidden, query, key, value, output, result, *refs):
    norms, held, hidden_in, sems = refs[:4], *refs[4:]
    hidden_load = start(hidden, hidden_in, sems.at[4])
    loads = []
    for part in range(4):
        rows = pl.ds(part * TOK, TOK)
        loads.append(start(pieces.at[rows, :], held.at[rows, :], sems.at[part]))
    sums = [jnp.zeros((8, WIDTH), FULL) for _ in range(4)]
    tail = jnp.zeros((8, 128), FULL)
    hidden_load.wait()
    made = hidden_in[...]
    for part in range(4):
        loads[part].wait()
        for pair in range(8):
            at = part * TOK + pair * 16
            rows = held[at : at + 16, :STAR].astype(FULL)
            for side in range(2):
                index = part * 16 + pair * 2 + side
                y, x, z = index // 16, index // 4 % 4, index % 4
                colour = (x + 2 * y - z) % 4
                piece = rows[side * 8 : (side + 1) * 8, :]
                sums[colour] = sums[colour] + piece[:, :WIDTH]
                tail = tail + piece[:, WIDTH:]
        at = slice(part * TOK, (part + 1) * TOK)
        made = made + dot(placed_rows(by_row[...], part), held[at, STAR:])
    result[...] = made.astype(LOW)
    for ref, total in zip((query, key, value, output), sums):
        ref[...] = total
    tail = jnp.concatenate([tail, jnp.zeros((TOK - 8, 128), FULL)], axis=0).T
    for index, norm in enumerate(norms):
        norm[...] = tail[index : index + 1, :8]


def tied(*values):
    return lax.optimization_barrier(values)


def per_device(
    tokens,
    hash_ids,
    doc_lengths,
    w_query,
    w_key,
    w_value,
    w_output,
    norm1_gain,
    norm1_bias,
    norm2_gain,
    norm2_bias,
    expert_in,
    expert_out,
    load_average,
    out_grad,
):
    experts = load_average.shape[0]
    groups = lax.axis_size("exp")
    devices = 2 * groups
    rep = lax.axis_index("rep")
    at = lax.axis_index("exp")
    y, x, z = lax.div(at, LINE * LINE), lax.rem(lax.div(at, LINE), LINE), lax.rem(at, LINE)
    colour = lax.rem(x + 2 * y + 3 * z, 4)
    place = jnp.stack([rep, colour]).astype(jnp.int32).reshape(1, 2)
    weight_in, weight_out = expert_in[0], expert_out[0]
    hidden = weight_in.shape[1]

    norm_params = jnp.concatenate([norm1_gain, norm1_bias, norm2_gain, norm2_bias]).reshape(1, 32)
    packed, laid, slot, by_row = kernel_call(
        pack_kernel,
        [VMEM] + [HBM] * 6,
        [
            ((SLOTS, STAR), LOW, HBM),
            ((SLOTS, WIDTH), LOW, HBM),
            ((1, TOK), jnp.int32, VMEM),
            ((TOK, TOK), jnp.int32, VMEM),
        ],
        scratch=[
            ((1, TOK), jnp.int32),
            ((4, 8, WIDTH), LOW),
            ((TOK, WIDTH), LOW),
            ((4, 32, STAR), LOW),
            ((SLOTS, WIDTH), LOW),
        ],
        copies=26,
        flops=2 * SLOTS * TOK * WIDTH,
        moved=6 << 20,
        name="pack",
    )(norm_params, hash_ids.reshape(1, TOK), w_query, w_key, w_value, w_output, out_grad)
    packed, first, second = tied(packed, weight_in, weight_out)
    shares = exchange(packed.reshape(groups, 8, STAR)).reshape(SLOTS, STAR)
    weight_in_other, weight_out_other = swap(first), swap(second)
    shares, place, weight_in_other, weight_out_other = tied(
        shares, place, weight_in_other, weight_out_other
    )
    received = [between(shares, ways, True) for ways in WAYS]
    other_shares = swap(shares)
    laid, *received = tied(laid, *received)
    grad_rows = exchange(laid.reshape(groups, CAPACITY, WIDTH)).reshape(SLOTS, WIDTH)
    received = [one for part in received for one in (part, swap(part))]

    def send(rows):
        return exchange(rows.reshape(groups, CAPACITY, WIDTH)).reshape(SLOTS, WIDTH)

    outgoing, hidden_one, qkv, probs, joined, normed, norms, extra = kernel_call(
        attend_kernel,
        [SMEM, VMEM, SMEM] + [HBM] * 9,
        [
            ((SLOTS, WIDTH), LOW, HBM),
            ((TOK, WIDTH), FULL, HBM),
            ((3, TOK, WIDTH), LOW, HBM),
            ((HEADS, TOK, TOK), LOW, HBM),
            ((TOK, WIDTH), LOW, HBM),
            ((TOK, WIDTH), LOW, HBM),
            ((8, WIDTH), FULL, HBM),
            ((WIDTH, 128), LOW, HBM),
        ],
        scratch=[
            ((TOK, WIDTH), LOW),
            ((WIDTH, 128), LOW),
            ((4, WIDTH, WIDTH), LOW),
            ((8, WIDTH), FULL),
            ((TOK, WIDTH), LOW),
            ((3, TOK, WIDTH), LOW),
            ((HEADS, TOK, TOK), FULL),
            ((HEADS, TOK, TOK), LOW),
            ((TOK, WIDTH), LOW),
            ((TOK, WIDTH), FULL),
            ((SLOTS, WIDTH), LOW),
        ],
        copies=32,
        flops=2 * TOK * WIDTH * 5000,
        moved=12 << 20,
        name="attend",
    )(place, slot, doc_lengths, shares, other_shares, *received, tokens)

    up_own = dot_nt(grad_rows, weight_out).astype(LOW)
    up_other = dot_nt(grad_rows, weight_out_other).astype(LOW)
    rows, up_own, up_other = tied(send(outgoing), up_own, up_other)
    lefts = kernel_call(
        left_kernel,
        [SMEM] + [HBM] * 2,
        [((WIDTH, TOK), LOW, HBM)] * 4,
        scratch=[((2, TOK, WIDTH), LOW), ((2, WIDTH, TOK), LOW)],
        copies=6,
        moved=2 << 20,
        name="left",
    )(place, normed, joined)

    back_rows, *acts_flows = kernel_call(
        expert_kernel,
        [HBM] * 5,
        [
            ((SLOTS, WIDTH), LOW, HBM),
        ]
        + [((SLOTS, hidden), LOW, HBM)] * 4,
        scratch=[
            ((SLOTS, WIDTH), LOW),
            ((WIDTH, 2 * hidden), LOW),
            ((SLOTS, 2 * hidden), LOW),
            ((SLOTS, 2 * hidden), LOW),
            ((SLOTS, 2 * hidden), LOW),
            ((SLOTS, WIDTH), LOW),
        ],
        copies=3 + 8 * (hidden // 512),
        flops=8 * SLOTS * WIDTH * hidden,
        moved=24 << 20,
        name="expert",
    )(rows, weight_in, weight_in_other, up_own, up_other)
    act, act_theirs, flow, flow_theirs = acts_flows
    far_lefts = [between(left, ways, False) for left, ways in zip(lefts[1:], WAYS)]
    lefts = [lefts[0]] + far_lefts
    back = send(back_rows)
    (result,) = kernel_call(
        result_kernel,
        [HBM] * 4,
        [((SLOTS, LAST), LOW, HBM)],
        scratch=[
            ((2, SLOTS, hidden), LOW),
            ((2, hidden, WIDTH), LOW),
            ((SLOTS, WIDTH), FULL),
        ],
        copies=5,
        flops=4 * SLOTS * hidden * WIDTH,
        moved=14 << 20,
        name="result",
    )(act, act_theirs, weight_out, weight_out_other)
    act_other, flow_other = swap(act_theirs), swap(flow_theirs)
    back, result, act_other, flow_other, *lefts = tied(
        back, result, act_other, flow_other, *lefts
    )

    hidden_grad, *parts, gains = kernel_call(
        attend_back_kernel,
        [SMEM, VMEM, SMEM, VMEM] + [HBM] * 13,
        [
            ((TOK, WIDTH), FULL, HBM),
        ]
        + [((TOK, WIDTH), LOW, HBM)] * 4
        + [
            ((8, WIDTH), FULL, VMEM),
        ],
        scratch=[
            ((SLOTS, WIDTH), LOW),
            ((TOK, WIDTH), FULL),
            ((TOK, WIDTH), LOW),
            ((WIDTH, WIDTH), LOW),
            ((3, TOK, WIDTH), LOW),
            ((HEADS, TOK, TOK), LOW),
            ((TOK, WIDTH), FULL),
            ((TOK, WIDTH), LOW),
            ((TOK, ALL), LOW),
            ((HEADS, TOK, TOK), FULL),
            ((HEADS, TOK, TOK), FULL),
            ((HEADS, TOK, TOK), FULL),
            ((HEADS, TOK, TOK), LOW),
            ((HEADS, TOK, TOK), LOW),
            ((HEADS, TOK, TOK), LOW),
        ],
        copies=19,
        flops=2 * TOK * WIDTH * 3000,
        moved=8 << 20,
        name="attend_back",
    )(
        place,
        by_row,
        doc_lengths,
        norms,
        back,
        hidden_one,
        out_grad,
        shares,
        other_shares,
        *received,
        qkv,
        probs,
    )
    own_parts = parts
    parts = [parts[0]] + [between(part, ways, False) for part, ways in zip(parts[1:], WAYS)]
    mine, theirs = kernel_call(
        weights_kernel,
        [SMEM] + [HBM] * 11,
        [((HALF, STAR), LOW, HBM)] * 2,
        scratch=[
            ((WIDTH, 4 * TOK), LOW),
            ((4 * TOK, WIDTH), LOW),
            ((WIDTH, WIDTH), LOW),
            ((WIDTH, STAR), LOW),
            ((8, WIDTH), FULL),
        ],
        copies=15,
        flops=8 * TOK * WIDTH * WIDTH,
        moved=8 << 20,
        name="weights",
    )(place, *lefts, *parts, shares, other_shares, gains)
    summed = (mine.astype(FULL) + swap(theirs).astype(FULL)).astype(LOW)
    weight_part = lax.dynamic_update_slice(result, summed, (0, 0))
    pieces = exchange(weight_part.reshape(groups, 8, LAST)).reshape(SLOTS, LAST)

    act, flow, rows, grad_rows, *own_parts, _ = tied(
        act, flow, rows, grad_rows, *own_parts, weight_part
    )
    rows_other, grad_other = swap(rows), swap(grad_rows)
    out_weight_grad = weight_grad_call((grad_rows, grad_other), 0, (act, act_other), True)
    in_weight_grad = weight_grad_call((rows, rows_other), 0, (flow, flow_other), False)
    (input_grad,) = kernel_call(
        input_kernel,
        [SMEM, VMEM] + [HBM] * 14,
        [((TOK, WIDTH), FULL, HBM)],
        scratch=[
            ((TOK, WIDTH), LOW),
            ((TOK, WIDTH), FULL),
            ((4, TOK, WIDTH), LOW),
            ((4, WIDTH, WIDTH), LOW),
            ((TOK, WIDTH), FULL),
        ],
        copies=20,
        flops=2 * TOK * WIDTH * FLOW,
        moved=8 << 20,
        name="input_grad",
    )(place, norms, tokens, hidden_grad, shares, other_shares, *received, *own_parts)
    tails = extra[:, 64:].reshape(devices, 8, experts)[:, 0]
    counts = jnp.sum(tails.astype(FULL), axis=0)
    new_average = 0.7 * load_average + 0.3 * counts
    counts = counts.astype(jnp.int32)
    pieces, out_weight_grad, in_weight_grad, input_grad, counts, new_average = tied(
        pieces, out_weight_grad, in_weight_grad, input_grad, counts, new_average
    )
    *grads, output, gain_one, bias_one, gain_two, bias_two = kernel_call(
        reduce_kernel,
        [VMEM, HBM, HBM],
        [((8, WIDTH), FULL, VMEM)] * 4
        + [((TOK, WIDTH), LOW, VMEM)]
        + [((1, 8), FULL, VMEM)] * 4,
        scratch=[((SLOTS, LAST), LOW), ((TOK, WIDTH), FULL)],
        copies=5,
        moved=5 << 20,
        name="reduce",
    )(by_row, pieces, hidden_one)
    return (
        output,
        input_grad,
        *grads,
        gain_one.reshape(8),
        bias_one.reshape(8),
        gain_two.reshape(8),
        bias_two.reshape(8),
        in_weight_grad[None],
        out_weight_grad[None],
        counts,
        new_average,
    )


def solution(mesh):
    rows = P(("rep", "exp"), None)
    vector = P(("rep", "exp"))
    return jax.shard_map(
        per_device,
        mesh=mesh,
        in_specs=(rows,) * 7
        + (vector,) * 4
        + (P("exp", None, "rep"), P("exp", "rep", None), P(), rows),
        out_specs=(rows,) * 6
        + (vector,) * 4
        + (P("exp", None, "rep"), P("exp", "rep", None), P(), P()),
        check_vma=False,
    )
```

```python
import functools

import jax
import jax.numpy as jnp
from jax import lax
from jax.experimental import pallas as pl
from jax.experimental.pallas import tpu as pltpu
from jax.sharding import PartitionSpec as P

HEADS = 16
HEAD_DIM = 64
SCALE = HEAD_DIM ** (-0.5)
EPSILON = 1e-05
SWAP = [(0, 1), (1, 0)]
CAPACITY = 8
TOK = 128
WIDTH = 1024
HALF = WIDTH // 2
SLOTS = 512
FLOW = 3 * WIDTH
ALL = 4 * WIDTH
LENGTH = ALL + 128
STAR = WIDTH + 128
LAST = STAR + WIDTH
LINE = 4
VMEM_BYTES = 511 << 17
LOW = jnp.bfloat16
FULL = jnp.float32
VMEM = pl.BlockSpec(memory_space=pltpu.VMEM)
SMEM = pl.BlockSpec(memory_space=pltpu.SMEM)
HBM = pl.BlockSpec(memory_space=pltpu.HBM)


def swap(value):
    return lax.ppermute(value, "rep", SWAP)


def moved_on(index, stride, step):
    at = index // stride % LINE
    return index + ((at + step) % LINE - at) * stride


WAYS = (((LINE, 1), (1, -1)), ((LINE * LINE, 1), (LINE * LINE, -1)), ((LINE, -1), (1, 1)))


def between(value, ways, back):
    count = lax.axis_size("exp")
    pairs = []
    for rep, way in enumerate(ways):
        for index in range(count):
            near, far = rep * count + index, rep * count + moved_on(index, *way)
            pairs.append((far, near) if back else (near, far))
    return lax.ppermute(value, ("rep", "exp"), pairs)


def exchange(value):
    return lax.all_to_all(value, "exp", split_axis=0, concat_axis=0, tiled=True)


def dot(left, right):
    return jnp.dot(left, right, preferred_element_type=FULL)


def dot_nt(left, right):
    return lax.dot_general(left, right, (((1,), (1,)), ((), ())), preferred_element_type=FULL)


def dot_tn(left, right):
    return lax.dot_general(left, right, (((0,), (0,)), ((), ())), preferred_element_type=FULL)


def kernel_call(
    body, specs, outs, scratch=(), copies=0, flops=0, moved=0, name=None, aliases=None
):
    shapes = [pltpu.VMEM(shape, dtype) for shape, dtype in scratch]
    if copies:
        shapes.append(pltpu.SemaphoreType.DMA((copies,)))
    return pl.pallas_call(
        body,
        in_specs=specs,
        out_specs=[spec for _, _, spec in outs],
        out_shape=[jax.ShapeDtypeStruct(shape, dtype) for shape, dtype, _ in outs],
        scratch_shapes=shapes,
        input_output_aliases=aliases or {},
        compiler_params=pltpu.CompilerParams(vmem_limit_bytes=VMEM_BYTES),
        cost_estimate=pl.CostEstimate(flops=flops, bytes_accessed=moved, transcendentals=0),
        name=name,
    )


def start(source, target, sem):
    copy = pltpu.make_async_copy(source, target, sem)
    copy.start()
    return copy


def lanes(first, size):
    return pl.ds(pl.multiple_of(first, size), size)


def load_all(sources, place, weights, sems, first):
    loads = []
    for index, pair in enumerate(sources):
        matrix = lax.rem(place[0, 1] + index, 4)
        for side, half in enumerate((place[0, 0], 1 - place[0, 0])):
            target = weights.at[matrix, lanes(half * HALF, HALF), :]
            loads.append(start(pair[side], target, sems.at[first + 2 * index + side]))
    return loads


def load_one(sources, place, matrix, weight, sems, first):
    loads = []
    for side, half in enumerate((place[0, 0], 1 - place[0, 0])):
        target, sem = weight.at[lanes(half * HALF, HALF), :], sems.at[first + side]
        for index, pair in enumerate(sources):

            @pl.when(lax.rem(place[0, 1] + index, 4) == matrix)
            def _(source=pair[side], target=target, sem=sem):
                pltpu.make_async_copy(source, target, sem).start()

        loads.append(pltpu.make_async_copy(sources[1][side], target, sem))
    return loads


def as_sources(shares, other_shares, received):
    at = pl.ds(0, WIDTH)
    pairs = [(shares, other_shares)]
    pairs += [(received[2 * index], received[2 * index + 1]) for index in range(3)]
    return [(own.at[:, at], other.at[:, at]) for own, other in pairs]


def centered(rows):
    center = rows - jnp.mean(rows, axis=-1, keepdims=True)
    spread = jnp.mean(center * center, axis=-1, keepdims=True)
    inverse = lax.rsqrt(spread + EPSILON)
    return center * inverse, inverse


def norm_pull(upstream, unit, inverse, gain):
    scaled = upstream * gain
    return inverse * (
        scaled
        - jnp.mean(scaled, axis=-1, keepdims=True)
        - unit * jnp.mean(scaled * unit, axis=-1, keepdims=True)
    )


def same_document(lengths, query_at, key_at):
    end = jnp.int32(0)
    query_doc = jnp.zeros((TOK, TOK), jnp.int32)
    key_doc = jnp.zeros((TOK, TOK), jnp.int32)
    for j in range(3):
        end = end + lengths[0, j]
        query_doc += (query_at >= end).astype(jnp.int32)
        key_doc += (key_at >= end).astype(jnp.int32)
    return query_doc == key_doc


def placed(slot, part):
    row_at = lax.broadcasted_iota(jnp.int32, (TOK, TOK), 0) + part * TOK
    return (row_at == slot).astype(LOW)


def pack_kernel(norms, ids, query, key, value, output, packed, *scratch):
    ids_in, rows, lined, sems = scratch
    loads = [start(ids, ids_in, sems.at[0])]
    for index, ref in enumerate((query, key, value, output)):
        loads.append(start(ref, rows.at[index], sems.at[1 + index]))
    row = jnp.concatenate([norms[...].astype(FULL), jnp.zeros((1, TOK - 32), FULL)], axis=1)
    tile = jnp.broadcast_to(row, (TOK, TOK)).T
    lane_at = lax.broadcasted_iota(jnp.int32, (8, TOK), 1)
    params = jnp.zeros((8, TOK), FULL)
    for index in range(4):
        params = params + jnp.where(lane_at == index, tile[index * 8 : (index + 1) * 8, :], 0.0)
    loads[0].wait()
    row_at = lax.broadcasted_iota(jnp.int32, (TOK, TOK), 0)
    chosen = (ids_in[...] == row_at - 64).astype(LOW)
    counts = dot_nt(jnp.ones((8, TOK), LOW), chosen)
    first = lax.broadcasted_iota(jnp.int32, (8, TOK), 0) == 0
    extra = params + jnp.where(first, counts, 0.0)
    for load in loads[1:]:
        load.wait()
    rows_full = [rows[index].astype(FULL) for index in range(4)]
    copies = []
    for base in range(4):
        made = [
            jnp.concatenate([rows_full[(base + 3 * z) % 4], extra], axis=1) for z in range(LINE)
        ]
        lined[base] = jnp.concatenate(made, axis=0).astype(LOW)
    for y in range(LINE):
        for x in range(LINE):
            index = y * LINE + x
            at = packed.at[pl.ds(index * 32, 32), :]
            copies.append(start(lined.at[(x + 2 * y) % 4], at, sems.at[6 + index]))
    for copy in copies:
        copy.wait()


def grad_kernel(ids, grad, laid, slot, by_row, ids_in, grad_in, rows_made, sems):
    loads = [start(ids, ids_in, sems.at[0]), start(grad, grad_in, sems.at[1])]
    row_at = lax.broadcasted_iota(jnp.int32, (TOK, TOK), 0)
    column_at = lax.broadcasted_iota(jnp.int32, (TOK, TOK), 1)
    loads[0].wait()
    by_column = jnp.broadcast_to(ids_in[...].astype(FULL), (TOK, TOK))
    before = (by_column.T == by_column) & (row_at < column_at)
    rank = jnp.sum(before.astype(FULL), axis=0, keepdims=True).astype(jnp.int32)
    target = ids_in[...] * CAPACITY + rank
    slot[...] = target
    by_row[...] = jnp.broadcast_to(target.astype(FULL), (TOK, TOK)).T.astype(jnp.int32)
    loads[1].wait()
    copies = []
    for part in range(4):
        at = pl.ds(part * TOK, TOK)
        rows_made[at, :] = dot(placed(target, part), grad_in[...]).astype(LOW)
        copies.append(start(rows_made.at[at, :], laid.at[at, :], sems.at[2 + part]))
    for copy in copies:
        copy.wait()


def placed_rows(by_row, part):
    lane_at = lax.broadcasted_iota(jnp.int32, (TOK, TOK), 1) + part * TOK
    return (lane_at == by_row).astype(LOW)


def attend_kernel(
    place, slot, lengths, shares, other_shares, *refs
):
    received, tokens, refs = refs[:6], refs[6], refs[7:]
    outgoing_out, hidden_out, qkv_out, probs_out, joined_out, normed_out = refs[:6]
    norms_out, extra_out, *scratch = refs[6:]
    tokens_in, extra, weights, norms, normed, qkv, raw, low, joined, hidden, outgoing, sems = scratch
    rep = place[0, 0]
    extra_loads = []
    for side, ref in enumerate((shares, other_shares)):
        rows = lanes((rep if side == 0 else 1 - rep) * HALF, HALF)
        source = ref.at[:, pl.ds(WIDTH, 128)]
        extra_loads.append(start(source, extra.at[rows, :], sems.at[18 + side]))
    tokens_load = start(tokens, tokens_in, sems.at[1])
    sources = as_sources(shares, other_shares, received)
    weight_loads = load_all(sources, place, weights, sems, 20)
    for load in extra_loads:
        load.wait()
    norms[...] = extra[...].astype(FULL).T[:8, :]
    copies = [start(norms, norms_out, sems.at[6]), start(extra, extra_out, sems.at[0])]
    tokens_load.wait()
    inputs = tokens_in[...].astype(FULL)
    unit, _ = centered(inputs)
    normed[...] = (unit * norms[0:1, :] + norms[1:2, :]).astype(LOW)
    copies.append(start(normed, normed_out, sems.at[7]))
    for load in weight_loads:
        load.wait()
    for index in range(3):
        qkv[index] = dot(normed[...], weights[index]).astype(LOW)
    copies.append(start(qkv, qkv_out, sems.at[8]))

    query_at = lax.broadcasted_iota(jnp.int32, (TOK, TOK), 0)
    key_at = lax.broadcasted_iota(jnp.int32, (TOK, TOK), 1)
    allowed = same_document(lengths, query_at, key_at) & (key_at <= query_at)
    for first in range(0, HEADS, 8):
        heads = range(first, first + 8)
        for head in heads:
            at = slice(head * HEAD_DIM, (head + 1) * HEAD_DIM)
            raw[head] = dot_nt(qkv[0, :, at], qkv[1, :, at])
        for head in heads:
            scores = jnp.where(allowed, raw[head] * SCALE, -1e30)
            raised = jnp.exp(scores - jnp.max(scores, axis=-1, keepdims=True))
            chance = raised / jnp.sum(raised, axis=-1, keepdims=True)
            low[head] = chance.astype(LOW)
        block = pl.ds(first, 8)
        copies.append(start(low.at[block], probs_out.at[block], sems.at[9 + first // 8]))
        for head in range(first, first + 8, 2):
            made = []
            for one in (head, head + 1):
                made.append(dot(low[one], qkv[2, :, one * HEAD_DIM : (one + 1) * HEAD_DIM]))
            at = slice(head * HEAD_DIM, (head + 2) * HEAD_DIM)
            joined[:, at] = jnp.concatenate(made, axis=1).astype(LOW)
    copies.append(start(joined, joined_out, sems.at[28]))
    made = inputs + dot(joined[...], weights[3])
    hidden[...] = made
    copies.append(start(hidden, hidden_out, sems.at[13]))
    unit, _ = centered(made)
    second = (unit * norms[2:3, :] + norms[3:4, :]).astype(LOW)
    for part in range(4):
        rows = pl.ds(part * TOK, TOK)
        outgoing[rows, :] = dot(placed(slot[...], part), second).astype(LOW)
        copies.append(start(outgoing.at[rows, :], outgoing_out.at[rows, :], sems.at[14 + part]))
    for copy in copies:
        copy.wait()


def left_kernel(place, normed, joined, *refs):
    targets, held, turned, sems = refs[:4], refs[4], refs[5], refs[6]
    loads = [start(ref, held.at[i], sems.at[i]) for i, ref in enumerate((normed, joined))]
    for index, load in enumerate(loads):
        load.wait()
        turned[index] = held[index].T
    copies = []
    for index, target in enumerate(targets):
        kind = lax.div(lax.rem(place[0, 1] + index, 4), 3)
        copies.append(start(turned.at[kind], target, sems.at[2 + index]))
    for copy in copies:
        copy.wait()


def gelu_parts(pre):
    square = pre * pre
    turn = jnp.tanh(pre * (0.7978845608028654 + 0.035677408136300125 * square))
    half = 0.5 + 0.5 * turn
    slope = half + (0.5 - 0.5 * turn * turn) * (
        pre * (0.7978845608028654 + 0.10703222440890037 * square)
    )
    return pre * half, slope


def expert_kernel(rows_in, weight_own, weight_other, up_own, up_other, out, *refs):
    acts, flows, scratch = refs[:2], refs[2:4], refs[4:]
    rows, weight, up, act, flow, back, sems = scratch
    hidden = weight.shape[1]
    half = hidden // 2
    chunk = 1024
    parts = hidden // chunk

    def load(j):
        cols = pl.ds(j * chunk, chunk)
        at = pl.ds(j * chunk % half, chunk)
        weight_in, up_in = (weight_own, up_own) if j * chunk < half else (weight_other, up_other)
        return (
            start(weight_in.at[:, at], weight.at[:, cols], sems.at[1 + j]),
            start(up_in.at[:, at], up.at[:, cols], sems.at[1 + parts + j]),
        )

    rows_load = start(rows_in, rows, sems.at[0])
    loads = [load(0), load(1)]
    rows_load.wait()
    copies = []
    for j in range(parts):
        cols = slice(j * chunk, (j + 1) * chunk)
        if j + 2 < parts:
            loads.append(load(j + 2))
        for copy in loads[j]:
            copy.wait()
        value, slope = gelu_parts(dot(rows[...], weight[:, cols]))
        act[:, cols] = value.astype(LOW)
        flow[:, cols] = (up[:, cols].astype(FULL) * slope).astype(LOW)
        at = pl.ds(j * chunk, chunk)
        side = j * chunk // half
        target_at = pl.ds(j * chunk % half, chunk)
        for index, (source, targets) in enumerate(((act, acts), (flow, flows))):
            sem = sems.at[1 + 2 * parts + 2 * j + index]
            copies.append(start(source.at[:, at], targets[side].at[:, target_at], sem))
    for index in range(2):
        block = slice(index * 256, (index + 1) * 256)
        back[block, :] = dot_nt(flow[block, :], weight[...]).astype(LOW)
        at = pl.ds(index * 256, 256)
        copies.append(start(back.at[at, :], out.at[at, :], sems.at[1 + 4 * parts + index]))
    for copy in copies:
        copy.wait()


def result_kernel(act_own, act_other, weight_own, weight_other, out, act, weight, made, sems):
    sides = []
    for side, (act_in, weight_in) in enumerate(((act_own, weight_own), (act_other, weight_other))):
        sides.append(
            [
                start(act_in, act.at[side], sems.at[2 * side]),
                start(weight_in, weight.at[side], sems.at[2 * side + 1]),
            ]
        )
        if side == 0:
            for load in sides[0]:
                load.wait()
    made[...] = dot(act[0], weight[0])
    for load in sides[1]:
        load.wait()
    act[0, :, :WIDTH] = (made[...] + dot(act[1], weight[1])).astype(LOW)
    source = act.at[0, :, pl.ds(0, WIDTH)]
    start(source, out.at[:, pl.ds(STAR, WIDTH)], sems.at[4]).wait()


def weight_grad_kernel(by_rows, at, first, second, streamed_first, streamed_second, made, held, sems):
    half = first.shape[0]
    cols = pl.ds(at, held.shape[1])

    @pl.when(pl.program_id(0) == 0)
    def _():
        loads = [
            start(first.at[:, cols], held.at[pl.ds(0, half), :], sems.at[0]),
            start(second.at[:, cols], held.at[pl.ds(half, half), :], sems.at[1]),
        ]
        for load in loads:
            load.wait()

    streamed = jnp.concatenate([streamed_first[...], streamed_second[...]], axis=0)
    made[...] = dot_tn(streamed, held[...]) if by_rows else dot_tn(held[...], streamed)


def weight_grad_call(held, at, streamed, by_rows, tile=1024):
    rows, wide = streamed[0].shape
    width = WIDTH
    shape = (wide, width) if by_rows else (width, wide)
    block = (tile, width) if by_rows else (width, tile)
    return pl.pallas_call(
        functools.partial(weight_grad_kernel, by_rows, at),
        grid=(wide // tile,),
        in_specs=[HBM, HBM] + [pl.BlockSpec((rows, tile), lambda i: (0, i))] * 2,
        out_specs=pl.BlockSpec(block, (lambda i: (i, 0)) if by_rows else (lambda i: (0, i))),
        out_shape=jax.ShapeDtypeStruct(shape, FULL),
        scratch_shapes=[pltpu.VMEM((2 * rows, width), LOW), pltpu.SemaphoreType.DMA((2,))],
        compiler_params=pltpu.CompilerParams(
            dimension_semantics=("arbitrary",), vmem_limit_bytes=VMEM_BYTES
        ),
        cost_estimate=pl.CostEstimate(
            flops=4 * rows * wide * width, bytes_accessed=14 << 20, transcendentals=0
        ),
        name="weight_grad",
    )(*held, *streamed)


def attend_back_kernel(
    place, by_row, lengths, norms, back, hidden, grad, shares, other_shares, *refs
):
    received, (qkv_in, probs_in, grad_out) = refs[:6], refs[6:9]
    parts_out, gains, scratch = refs[9:13], refs[13], refs[14:]
    back_in, hidden_in, grad_in, weight, qkv, probs, total, above, flow, *scratch = scratch
    raw, turned, pulled, low, low_turned, chance_turned, sems = scratch
    back_loads = []
    for part in range(2):
        at = pl.ds(part * 2 * TOK, 2 * TOK)
        back_loads.append(start(back.at[at, :], back_in.at[at, :], sems.at[part]))
    hidden_load = start(hidden, hidden_in, sems.at[4])
    grad_load = start(grad, grad_in, sems.at[5])
    sources = as_sources(shares, other_shares, received)
    weight_loads = load_one(sources, place, 3, weight, sems, 15)
    qkv_load = start(qkv_in, qkv, sems.at[7])
    probs_load = start(probs_in, probs, sems.at[8])
    upstream = jnp.zeros((TOK, WIDTH), FULL)
    for part in range(4):
        if part % 2 == 0:
            back_loads[part // 2].wait()
        rows = back_in[part * TOK : (part + 1) * TOK, :]
        upstream = upstream + dot(placed_rows(by_row[...], part), rows)
    hidden_load.wait()
    grad_load.wait()
    unit, inverse = centered(hidden_in[...])
    made = grad_in[...].astype(FULL) + norm_pull(upstream, unit, inverse, norms[2:3, :])
    total[...] = made
    copies = [start(total, grad_out, sems.at[9])]
    flow[:, FLOW:] = made.astype(LOW)
    gains[...] = jnp.zeros(gains.shape, FULL)
    gains[2:3, :] = jnp.sum(upstream * unit, axis=0, keepdims=True)
    gains[3:4, :] = jnp.sum(upstream, axis=0, keepdims=True)
    for load in weight_loads:
        load.wait()
    above[...] = dot_nt(flow[:, FLOW:], weight[...]).astype(LOW)
    qkv_load.wait()
    probs_load.wait()

    def head_of(part, head):
        return qkv[part, :, head * HEAD_DIM : (head + 1) * HEAD_DIM]

    def above_of(head):
        return above[:, head * HEAD_DIM : (head + 1) * HEAD_DIM]

    def store(part, first, pieces):
        at = part * WIDTH + first * HEAD_DIM
        flow[:, at : at + 2 * HEAD_DIM] = jnp.concatenate(pieces, axis=1).astype(LOW)

    key_at = lax.broadcasted_iota(jnp.int32, (TOK, TOK), 0)
    query_at = lax.broadcasted_iota(jnp.int32, (TOK, TOK), 1)
    allowed = same_document(lengths, query_at, key_at) & (key_at <= query_at)
    for first in range(0, HEADS, 8):
        heads = range(first, first + 8)
        pairs = range(first, first + 8, 2)
        for head in heads:
            raw[head] = dot_nt(above_of(head), head_of(2, head))
            turned[head] = dot_nt(head_of(1, head), head_of(0, head))
            pulled[head] = dot_nt(head_of(2, head), above_of(head))
        for head in heads:
            chance = probs[head].astype(FULL)
            taken = jnp.sum(chance * raw[head], axis=-1, keepdims=True)
            low[head] = (chance * (raw[head] - taken)).astype(LOW)
        for head in heads:
            scores = jnp.where(allowed, turned[head] * SCALE, -1e30)
            raised = jnp.exp(scores - jnp.max(scores, axis=0, keepdims=True))
            chance = raised / jnp.sum(raised, axis=0, keepdims=True)
            chance_turned[head] = chance.astype(LOW)
            taken = jnp.sum(chance * pulled[head], axis=0, keepdims=True)
            low_turned[head] = (chance * (pulled[head] - taken)).astype(LOW)
        for head in pairs:
            both = (head, head + 1)
            store(2, head, [dot(chance_turned[h], above_of(h)) for h in both])
            store(0, head, [dot(low[h], head_of(1, h)) * SCALE for h in both])
            store(1, head, [dot(low_turned[h], head_of(0, h)) * SCALE for h in both])
    for index, target in enumerate(parts_out):
        source = flow.at[:, lanes(lax.rem(place[0, 1] + index, 4) * WIDTH, WIDTH)]
        copies.append(start(source, target, sems.at[10 + index]))
    for copy in copies:
        copy.wait()


def weights_kernel(place, *refs):
    lefts, flows, shares, other_shares, gains_in = refs[:4], refs[4:8], *refs[8:11]
    mine, theirs, left, right, weight, made, gains, sems = refs[11:]
    rep, colour = place[0, 0], place[0, 1]
    loads = []
    for index in range(4):
        rows = pl.ds(index * TOK, TOK)
        loads.append(start(lefts[index], left.at[:, rows], sems.at[index]))
        loads.append(start(flows[index], right.at[rows, :], sems.at[4 + index]))
    small = [start(gains_in, gains, sems.at[8])]
    for side, ref in enumerate((shares, other_shares)):
        rows = lanes((rep if side == 0 else 1 - rep) * HALF, HALF)
        source = ref.at[:, pl.ds(0, WIDTH)]
        small.append(start(source, weight.at[rows, :], sems.at[9 + side]))
        source, target = ref.at[:, pl.ds(WIDTH, 128)], made.at[rows, pl.ds(WIDTH, 128)]
        small.append(start(source, target, sems.at[11 + side]))
    for load in loads:
        load.wait()
    total = jnp.sum(right[...].astype(FULL), axis=0, keepdims=True)
    projects = colour < 3
    copies = []
    for side, (half, target) in enumerate(((1 - rep, theirs), (rep, mine))):
        rows = lanes(half * HALF, HALF)
        value = dot(left[rows, :], right[...])
        made[rows, :WIDTH] = value.astype(LOW)
        if side == 0:
            for load in small:
                load.wait()
            columns = jnp.concatenate([gains[...], jnp.zeros((TOK - 8, WIDTH), FULL)], axis=0)
        weight_half = weight[rows, :].astype(FULL)
        params = made[rows, WIDTH:].astype(FULL)
        bias = jnp.sum(weight_half * total, axis=1, keepdims=True)
        gain = jnp.sum(weight_half * value, axis=1, keepdims=True)
        gain = (gain - params[:, 1:2] * bias) / params[:, 0:1]
        turned = jnp.where(half == 0, columns[:, :HALF], columns[:, HALF:]).T
        lane_at = lax.broadcasted_iota(jnp.int32, (HALF, 128), 1)
        first = jnp.where(projects, gain, 0.0)
        second = jnp.where(projects, bias, 0.0)
        tail = jnp.where(lane_at == 0, first, jnp.where(lane_at == 1, second, turned))
        made[rows, WIDTH:] = tail.astype(LOW)
        copies.append(start(made.at[rows, :], target, sems.at[13 + side]))
    for copy in copies:
        copy.wait()


def input_kernel(place, norms, tokens, hidden_grad, shares, other_shares, *refs):
    received, flows, made_out, scratch = refs[:6], refs[6:10], refs[10], refs[11:]
    tokens_in, grad_in, flow, weights, made, sems = scratch
    loads = []
    for index, pair in enumerate(as_sources(shares, other_shares, received)):
        loads.append([start(flows[index], flow.at[index], sems.at[4 + index])])
        for side, half in enumerate((place[0, 0], 1 - place[0, 0])):
            target = weights.at[index, lanes(half * HALF, HALF), :]
            loads[index].append(start(pair[side], target, sems.at[8 + 2 * index + side]))
    small = [start(tokens, tokens_in, sems.at[0]), start(hidden_grad, grad_in, sems.at[1])]
    upstream = jnp.zeros((TOK, WIDTH), FULL)
    for index in range(4):
        for load in loads[index]:
            load.wait()
        projects = lax.rem(place[0, 1] + index, 4) < 3
        pulled = dot_nt(flow[index], weights[index])
        upstream = upstream + jnp.where(projects, pulled, 0.0)
    for load in small:
        load.wait()
    unit, inverse = centered(tokens_in[...].astype(FULL))
    made[...] = grad_in[...] + norm_pull(upstream, unit, inverse, norms[0:1, :])
    start(made, made_out, sems.at[3]).wait()


def reduce_kernel(by_row, pieces, hidden, query, key, value, output, result, *refs):
    norms, held, hidden_in, sems = refs[:4], *refs[4:]
    hidden_load = start(hidden, hidden_in, sems.at[4])
    loads = []
    for part in range(4):
        rows = pl.ds(part * TOK, TOK)
        loads.append(start(pieces.at[rows, :], held.at[rows, :], sems.at[part]))
    sums = [jnp.zeros((8, WIDTH), FULL) for _ in range(4)]
    tail = jnp.zeros((8, 128), FULL)
    hidden_load.wait()
    made = hidden_in[...]
    for part in range(4):
        loads[part].wait()
        for pair in range(8):
            at = part * TOK + pair * 16
            rows = held[at : at + 16, :STAR].astype(FULL)
            for side in range(2):
                index = part * 16 + pair * 2 + side
                y, x, z = index // 16, index // 4 % 4, index % 4
                colour = (x + 2 * y - z) % 4
                piece = rows[side * 8 : (side + 1) * 8, :]
                sums[colour] = sums[colour] + piece[:, :WIDTH]
                tail = tail + piece[:, WIDTH:]
        at = slice(part * TOK, (part + 1) * TOK)
        made = made + dot(placed_rows(by_row[...], part), held[at, STAR:])
    result[...] = made.astype(LOW)
    for ref, total in zip((query, key, value, output), sums):
        ref[...] = total
    tail = jnp.concatenate([tail, jnp.zeros((TOK - 8, 128), FULL)], axis=0).T
    for index, norm in enumerate(norms):
        norm[...] = tail[index : index + 1, :8]


def tied(*values):
    return lax.optimization_barrier(values)


def per_device(
    tokens,
    hash_ids,
    doc_lengths,
    w_query,
    w_key,
    w_value,
    w_output,
    norm1_gain,
    norm1_bias,
    norm2_gain,
    norm2_bias,
    expert_in,
    expert_out,
    load_average,
    out_grad,
):
    experts = load_average.shape[0]
    groups = lax.axis_size("exp")
    devices = 2 * groups
    rep = lax.axis_index("rep")
    at = lax.axis_index("exp")
    y, x, z = lax.div(at, LINE * LINE), lax.rem(lax.div(at, LINE), LINE), lax.rem(at, LINE)
    colour = lax.rem(x + 2 * y + 3 * z, 4)
    place = jnp.stack([rep, colour]).astype(jnp.int32).reshape(1, 2)
    weight_in, weight_out = expert_in[0], expert_out[0]
    hidden = weight_in.shape[1]

    norm_params = jnp.concatenate([norm1_gain, norm1_bias, norm2_gain, norm2_bias]).reshape(1, 32)
    ids_row = hash_ids.reshape(1, TOK)
    (packed,) = kernel_call(
        pack_kernel,
        [VMEM] + [HBM] * 5,
        [((SLOTS, STAR), LOW, HBM)],
        scratch=[
            ((1, TOK), jnp.int32),
            ((4, 8, WIDTH), LOW),
            ((4, 32, STAR), LOW),
        ],
        copies=22,
        moved=3 << 20,
        name="pack",
    )(norm_params, ids_row, w_query, w_key, w_value, w_output)
    packed, ids_row = tied(packed, ids_row)
    laid, slot, by_row = kernel_call(
        grad_kernel,
        [HBM] * 2,
        [
            ((SLOTS, WIDTH), LOW, HBM),
            ((1, TOK), jnp.int32, VMEM),
            ((TOK, TOK), jnp.int32, VMEM),
        ],
        scratch=[((1, TOK), jnp.int32), ((TOK, WIDTH), LOW), ((SLOTS, WIDTH), LOW)],
        copies=6,
        flops=2 * SLOTS * TOK * WIDTH,
        moved=2 << 20,
        name="grad_rows",
    )(ids_row, out_grad)
    packed, first, second = tied(packed, weight_in, weight_out)
    shares = exchange(packed.reshape(groups, 8, STAR)).reshape(SLOTS, STAR)
    weight_in_other, weight_out_other = swap(first), swap(second)
    shares, place, weight_in_other, weight_out_other = tied(
        shares, place, weight_in_other, weight_out_other
    )
    received = [between(shares, ways, True) for ways in WAYS]
    other_shares = swap(shares)
    laid, *received = tied(laid, *received)
    grad_rows = exchange(laid.reshape(groups, CAPACITY, WIDTH)).reshape(SLOTS, WIDTH)
    received = [one for part in received for one in (part, swap(part))]

    def send(rows):
        return exchange(rows.reshape(groups, CAPACITY, WIDTH)).reshape(SLOTS, WIDTH)

    outgoing, hidden_one, qkv, probs, joined, normed, norms, extra = kernel_call(
        attend_kernel,
        [SMEM, VMEM, SMEM] + [HBM] * 9,
        [
            ((SLOTS, WIDTH), LOW, HBM),
            ((TOK, WIDTH), FULL, HBM),
            ((3, TOK, WIDTH), LOW, HBM),
            ((HEADS, TOK, TOK), LOW, HBM),
            ((TOK, WIDTH), LOW, HBM),
            ((TOK, WIDTH), LOW, HBM),
            ((8, WIDTH), FULL, HBM),
            ((WIDTH, 128), LOW, HBM),
        ],
        scratch=[
            ((TOK, WIDTH), LOW),
            ((WIDTH, 128), LOW),
            ((4, WIDTH, WIDTH), LOW),
            ((8, WIDTH), FULL),
            ((TOK, WIDTH), LOW),
            ((3, TOK, WIDTH), LOW),
            ((HEADS, TOK, TOK), FULL),
            ((HEADS, TOK, TOK), LOW),
            ((TOK, WIDTH), LOW),
            ((TOK, WIDTH), FULL),
            ((SLOTS, WIDTH), LOW),
        ],
        copies=32,
        flops=2 * TOK * WIDTH * 5000,
        moved=12 << 20,
        name="attend",
    )(place, slot, doc_lengths, shares, other_shares, *received, tokens)

    lefts = kernel_call(
        left_kernel,
        [SMEM] + [HBM] * 2,
        [((WIDTH, TOK), LOW, HBM)] * 4,
        scratch=[((2, TOK, WIDTH), LOW), ((2, WIDTH, TOK), LOW)],
        copies=6,
        moved=2 << 20,
        name="left",
    )(place, normed, joined)
    outgoing, *lefts = tied(outgoing, *lefts)

    up_own = dot_nt(grad_rows, weight_out).astype(LOW)
    up_other = dot_nt(grad_rows, weight_out_other).astype(LOW)
    rows, up_own, up_other = tied(send(outgoing), up_own, up_other)

    back_rows, *acts_flows = kernel_call(
        expert_kernel,
        [HBM] * 5,
        [
            ((SLOTS, WIDTH), LOW, HBM),
        ]
        + [((SLOTS, hidden), LOW, HBM)] * 4,
        scratch=[
            ((SLOTS, WIDTH), LOW),
            ((WIDTH, 2 * hidden), LOW),
            ((SLOTS, 2 * hidden), LOW),
            ((SLOTS, 2 * hidden), LOW),
            ((SLOTS, 2 * hidden), LOW),
            ((SLOTS, WIDTH), LOW),
        ],
        copies=3 + 8 * (hidden // 512),
        flops=8 * SLOTS * WIDTH * hidden,
        moved=24 << 20,
        name="expert",
    )(rows, weight_in, weight_in_other, up_own, up_other)
    act, act_theirs, flow, flow_theirs = acts_flows
    far_lefts = [between(left, ways, False) for left, ways in zip(lefts[1:], WAYS)]
    lefts = [lefts[0]] + far_lefts
    back = send(back_rows)
    (result,) = kernel_call(
        result_kernel,
        [HBM] * 4,
        [((SLOTS, LAST), LOW, HBM)],
        scratch=[
            ((2, SLOTS, hidden), LOW),
            ((2, hidden, WIDTH), LOW),
            ((SLOTS, WIDTH), FULL),
        ],
        copies=5,
        flops=4 * SLOTS * hidden * WIDTH,
        moved=14 << 20,
        name="result",
    )(act, act_theirs, weight_out, weight_out_other)
    act_other, flow_other = swap(act_theirs), swap(flow_theirs)
    back, result, act_other, flow_other, *lefts = tied(
        back, result, act_other, flow_other, *lefts
    )

    hidden_grad, *parts, gains = kernel_call(
        attend_back_kernel,
        [SMEM, VMEM, SMEM, VMEM] + [HBM] * 13,
        [
            ((TOK, WIDTH), FULL, HBM),
        ]
        + [((TOK, WIDTH), LOW, HBM)] * 4
        + [
            ((8, WIDTH), FULL, VMEM),
        ],
        scratch=[
            ((SLOTS, WIDTH), LOW),
            ((TOK, WIDTH), FULL),
            ((TOK, WIDTH), LOW),
            ((WIDTH, WIDTH), LOW),
            ((3, TOK, WIDTH), LOW),
            ((HEADS, TOK, TOK), LOW),
            ((TOK, WIDTH), FULL),
            ((TOK, WIDTH), LOW),
            ((TOK, ALL), LOW),
            ((HEADS, TOK, TOK), FULL),
            ((HEADS, TOK, TOK), FULL),
            ((HEADS, TOK, TOK), FULL),
            ((HEADS, TOK, TOK), LOW),
            ((HEADS, TOK, TOK), LOW),
            ((HEADS, TOK, TOK), LOW),
        ],
        copies=19,
        flops=2 * TOK * WIDTH * 3000,
        moved=8 << 20,
        name="attend_back",
    )(
        place,
        by_row,
        doc_lengths,
        norms,
        back,
        hidden_one,
        out_grad,
        shares,
        other_shares,
        *received,
        qkv,
        probs,
    )
    own_parts = parts
    parts = [parts[0]] + [between(part, ways, False) for part, ways in zip(parts[1:], WAYS)]
    mine, theirs = kernel_call(
        weights_kernel,
        [SMEM] + [HBM] * 11,
        [((HALF, STAR), LOW, HBM)] * 2,
        scratch=[
            ((WIDTH, 4 * TOK), LOW),
            ((4 * TOK, WIDTH), LOW),
            ((WIDTH, WIDTH), LOW),
            ((WIDTH, STAR), LOW),
            ((8, WIDTH), FULL),
        ],
        copies=15,
        flops=8 * TOK * WIDTH * WIDTH,
        moved=8 << 20,
        name="weights",
    )(place, *lefts, *parts, shares, other_shares, gains)
    summed = (mine.astype(FULL) + swap(theirs).astype(FULL)).astype(LOW)
    weight_part = lax.dynamic_update_slice(result, summed, (0, 0))
    pieces = exchange(weight_part.reshape(groups, 8, LAST)).reshape(SLOTS, LAST)

    act, flow, rows, grad_rows, *own_parts, _ = tied(
        act, flow, rows, grad_rows, *own_parts, weight_part
    )
    rows_other, grad_other = swap(rows), swap(grad_rows)
    out_weight_grad = weight_grad_call((grad_rows, grad_other), 0, (act, act_other), True)
    in_weight_grad = weight_grad_call((rows, rows_other), 0, (flow, flow_other), False)
    (input_grad,) = kernel_call(
        input_kernel,
        [SMEM, VMEM] + [HBM] * 14,
        [((TOK, WIDTH), FULL, HBM)],
        scratch=[
            ((TOK, WIDTH), LOW),
            ((TOK, WIDTH), FULL),
            ((4, TOK, WIDTH), LOW),
            ((4, WIDTH, WIDTH), LOW),
            ((TOK, WIDTH), FULL),
        ],
        copies=20,
        flops=2 * TOK * WIDTH * FLOW,
        moved=8 << 20,
        name="input_grad",
    )(place, norms, tokens, hidden_grad, shares, other_shares, *received, *own_parts)
    tails = extra[:, 64:].reshape(devices, 8, experts)[:, 0]
    counts = jnp.sum(tails.astype(FULL), axis=0)
    new_average = 0.7 * load_average + 0.3 * counts
    counts = counts.astype(jnp.int32)
    pieces, out_weight_grad, in_weight_grad, input_grad, counts, new_average = tied(
        pieces, out_weight_grad, in_weight_grad, input_grad, counts, new_average
    )
    *grads, output, gain_one, bias_one, gain_two, bias_two = kernel_call(
        reduce_kernel,
        [VMEM, HBM, HBM],
        [((8, WIDTH), FULL, VMEM)] * 4
        + [((TOK, WIDTH), LOW, VMEM)]
        + [((1, 8), FULL, VMEM)] * 4,
        scratch=[((SLOTS, LAST), LOW), ((TOK, WIDTH), FULL)],
        copies=5,
        moved=5 << 20,
        name="reduce",
    )(by_row, pieces, hidden_one)
    return (
        output,
        input_grad,
        *grads,
        gain_one.reshape(8),
        bias_one.reshape(8),
        gain_two.reshape(8),
        bias_two.reshape(8),
        in_weight_grad[None],
        out_weight_grad[None],
        counts,
        new_average,
    )


def solution(mesh):
    rows = P(("rep", "exp"), None)
    vector = P(("rep", "exp"))
    return jax.shard_map(
        per_device,
        mesh=mesh,
        in_specs=(rows,) * 7
        + (vector,) * 4
        + (P("exp", None, "rep"), P("exp", "rep", None), P(), rows),
        out_specs=(rows,) * 6
        + (vector,) * 4
        + (P("exp", None, "rep"), P("exp", "rep", None), P(), P()),
        check_vma=False,
    )
```

```python
import functools

import jax
import jax.numpy as jnp
from jax import lax
from jax.experimental import pallas as pl
from jax.experimental.pallas import tpu as pltpu
from jax.sharding import PartitionSpec as P

HEADS = 16
HEAD_DIM = 64
SCALE = HEAD_DIM ** (-0.5)
EPSILON = 1e-05
SWAP = [(0, 1), (1, 0)]
CAPACITY = 8
TOK = 128
WIDTH = 1024
HALF = WIDTH // 2
SLOTS = 512
FLOW = 3 * WIDTH
ALL = 4 * WIDTH
LENGTH = ALL + 128
STAR = WIDTH + 128
LAST = STAR + WIDTH
LINE = 4
VMEM_BYTES = 511 << 17
LOW = jnp.bfloat16
FULL = jnp.float32
VMEM = pl.BlockSpec(memory_space=pltpu.VMEM)
SMEM = pl.BlockSpec(memory_space=pltpu.SMEM)
HBM = pl.BlockSpec(memory_space=pltpu.HBM)


def swap(value):
    return lax.ppermute(value, "rep", SWAP)


def moved_on(index, stride, step):
    at = index // stride % LINE
    return index + ((at + step) % LINE - at) * stride


WAYS = (((LINE, 1), (1, -1)), ((LINE * LINE, 1), (LINE * LINE, -1)), ((LINE, -1), (1, 1)))


def between(value, ways, back):
    count = lax.axis_size("exp")
    pairs = []
    for rep, way in enumerate(ways):
        for index in range(count):
            near, far = rep * count + index, rep * count + moved_on(index, *way)
            pairs.append((far, near) if back else (near, far))
    return lax.ppermute(value, ("rep", "exp"), pairs)


def exchange(value):
    return lax.all_to_all(value, "exp", split_axis=0, concat_axis=0, tiled=True)


def dot(left, right):
    return jnp.dot(left, right, preferred_element_type=FULL)


def dot_nt(left, right):
    return lax.dot_general(left, right, (((1,), (1,)), ((), ())), preferred_element_type=FULL)


def dot_tn(left, right):
    return lax.dot_general(left, right, (((0,), (0,)), ((), ())), preferred_element_type=FULL)


def kernel_call(
    body, specs, outs, scratch=(), copies=0, flops=0, moved=0, name=None, aliases=None
):
    shapes = [pltpu.VMEM(shape, dtype) for shape, dtype in scratch]
    if copies:
        shapes.append(pltpu.SemaphoreType.DMA((copies,)))
    return pl.pallas_call(
        body,
        in_specs=specs,
        out_specs=[spec for _, _, spec in outs],
        out_shape=[jax.ShapeDtypeStruct(shape, dtype) for shape, dtype, _ in outs],
        scratch_shapes=shapes,
        input_output_aliases=aliases or {},
        compiler_params=pltpu.CompilerParams(vmem_limit_bytes=VMEM_BYTES),
        cost_estimate=pl.CostEstimate(flops=flops, bytes_accessed=moved, transcendentals=0),
        name=name,
    )


def start(source, target, sem):
    copy = pltpu.make_async_copy(source, target, sem)
    copy.start()
    return copy


def lanes(first, size):
    return pl.ds(pl.multiple_of(first, size), size)


def load_all(sources, place, weights, sems, first):
    loads = []
    for index, pair in enumerate(sources):
        for side, half in enumerate((place[0, 0], 1 - place[0, 0])):
            target = weights.at[index, lanes(half * HALF, HALF), :]
            loads.append(start(pair[side], target, sems.at[first + 2 * index + side]))
    return loads


def load_one(sources, place, matrix, weight, sems, first):
    loads = []
    for side, half in enumerate((place[0, 0], 1 - place[0, 0])):
        target, sem = weight.at[lanes(half * HALF, HALF), :], sems.at[first + side]
        for index, pair in enumerate(sources):

            @pl.when(lax.rem(place[0, 1] + index, 4) == matrix)
            def _(source=pair[side], target=target, sem=sem):
                pltpu.make_async_copy(source, target, sem).start()

        loads.append(pltpu.make_async_copy(sources[1][side], target, sem))
    return loads


def as_sources(shares, other_shares, received):
    at = pl.ds(0, WIDTH)
    pairs = [(shares, other_shares)]
    pairs += [(received[2 * index], received[2 * index + 1]) for index in range(3)]
    return [(own.at[:, at], other.at[:, at]) for own, other in pairs]


def centered(rows):
    center = rows - jnp.mean(rows, axis=-1, keepdims=True)
    spread = jnp.mean(center * center, axis=-1, keepdims=True)
    inverse = lax.rsqrt(spread + EPSILON)
    return center * inverse, inverse


def norm_pull(upstream, unit, inverse, gain):
    scaled = upstream * gain
    return inverse * (
        scaled
        - jnp.mean(scaled, axis=-1, keepdims=True)
        - unit * jnp.mean(scaled * unit, axis=-1, keepdims=True)
    )


def same_document(lengths, query_at, key_at):
    end = jnp.int32(0)
    query_doc = jnp.zeros((TOK, TOK), jnp.int32)
    key_doc = jnp.zeros((TOK, TOK), jnp.int32)
    for j in range(3):
        end = end + lengths[0, j]
        query_doc += (query_at >= end).astype(jnp.int32)
        key_doc += (key_at >= end).astype(jnp.int32)
    return query_doc == key_doc


def placed(slot, part):
    row_at = lax.broadcasted_iota(jnp.int32, (TOK, TOK), 0) + part * TOK
    return (row_at == slot).astype(LOW)


def pack_kernel(norms, ids, query, key, value, output, packed, *scratch):
    ids_in, rows, lined, sems = scratch
    loads = [start(ids, ids_in, sems.at[0])]
    for index, ref in enumerate((query, key, value, output)):
        loads.append(start(ref, rows.at[index], sems.at[1 + index]))
    row = jnp.concatenate([norms[...].astype(FULL), jnp.zeros((1, TOK - 32), FULL)], axis=1)
    tile = jnp.broadcast_to(row, (TOK, TOK)).T
    lane_at = lax.broadcasted_iota(jnp.int32, (8, TOK), 1)
    params = jnp.zeros((8, TOK), FULL)
    for index in range(4):
        params = params + jnp.where(lane_at == index, tile[index * 8 : (index + 1) * 8, :], 0.0)
    loads[0].wait()
    row_at = lax.broadcasted_iota(jnp.int32, (TOK, TOK), 0)
    chosen = (ids_in[...] == row_at - 64).astype(LOW)
    counts = dot_nt(jnp.ones((8, TOK), LOW), chosen)
    first = lax.broadcasted_iota(jnp.int32, (8, TOK), 0) == 0
    extra = params + jnp.where(first, counts, 0.0)
    for load in loads[1:]:
        load.wait()
    rows_full = [rows[index].astype(FULL) for index in range(4)]
    copies = []
    for base in range(4):
        made = [
            jnp.concatenate([rows_full[(base + 3 * z) % 4], extra], axis=1) for z in range(LINE)
        ]
        lined[base] = jnp.concatenate(made, axis=0).astype(LOW)
    for y in range(LINE):
        for x in range(LINE):
            index = y * LINE + x
            at = packed.at[pl.ds(index * 32, 32), :]
            copies.append(start(lined.at[(x + 2 * y) % 4], at, sems.at[6 + index]))
    for copy in copies:
        copy.wait()


def grad_kernel(ids, grad, laid, slot, by_row, ids_in, grad_in, rows_made, sems):
    loads = [start(ids, ids_in, sems.at[0]), start(grad, grad_in, sems.at[1])]
    row_at = lax.broadcasted_iota(jnp.int32, (TOK, TOK), 0)
    column_at = lax.broadcasted_iota(jnp.int32, (TOK, TOK), 1)
    loads[0].wait()
    by_column = jnp.broadcast_to(ids_in[...].astype(FULL), (TOK, TOK))
    before = (by_column.T == by_column) & (row_at < column_at)
    rank = jnp.sum(before.astype(FULL), axis=0, keepdims=True).astype(jnp.int32)
    target = ids_in[...] * CAPACITY + rank
    slot[...] = target
    by_row[...] = jnp.broadcast_to(target.astype(FULL), (TOK, TOK)).T.astype(jnp.int32)
    loads[1].wait()
    copies = []
    for part in range(4):
        at = pl.ds(part * TOK, TOK)
        rows_made[at, :] = dot(placed(target, part), grad_in[...]).astype(LOW)
        copies.append(start(rows_made.at[at, :], laid.at[at, :], sems.at[2 + part]))
    for copy in copies:
        copy.wait()


def placed_rows(by_row, part):
    lane_at = lax.broadcasted_iota(jnp.int32, (TOK, TOK), 1) + part * TOK
    return (lane_at == by_row).astype(LOW)


def attend_kernel(
    place, slot, lengths, shares, other_shares, *refs
):
    received, tokens, refs = refs[:6], refs[6], refs[7:]
    outgoing_out, hidden_out, qkv_out, probs_out, joined_out, normed_out = refs[:6]
    norms_out, extra_out, *scratch = refs[6:]
    tokens_in, extra, weights, norms, normed, qkv, raw, low, joined, hidden, outgoing, sems = scratch
    rep = place[0, 0]
    extra_loads = []
    for side, ref in enumerate((shares, other_shares)):
        rows = lanes((rep if side == 0 else 1 - rep) * HALF, HALF)
        source = ref.at[:, pl.ds(WIDTH, 128)]
        extra_loads.append(start(source, extra.at[rows, :], sems.at[18 + side]))
    tokens_load = start(tokens, tokens_in, sems.at[1])
    sources = as_sources(shares, other_shares, received)
    weight_loads = load_all(sources, place, weights, sems, 20)
    for load in extra_loads:
        load.wait()
    norms[...] = extra[...].astype(FULL).T[:8, :]
    copies = [start(norms, norms_out, sems.at[6]), start(extra, extra_out, sems.at[0])]
    tokens_load.wait()
    inputs = tokens_in[...].astype(FULL)
    unit, _ = centered(inputs)
    normed[...] = (unit * norms[0:1, :] + norms[1:2, :]).astype(LOW)
    copies.append(start(normed, normed_out, sems.at[7]))
    for index in range(4):
        for load in weight_loads[2 * index : 2 * index + 2]:
            load.wait()
        matrix = lax.rem(place[0, 1] + index, 4)
        qkv[matrix] = dot(normed[...], weights[index]).astype(LOW)
    copies.append(start(qkv.at[pl.ds(0, 3)], qkv_out, sems.at[8]))

    query_at = lax.broadcasted_iota(jnp.int32, (TOK, TOK), 0)
    key_at = lax.broadcasted_iota(jnp.int32, (TOK, TOK), 1)
    allowed = same_document(lengths, query_at, key_at) & (key_at <= query_at)
    for first in range(0, HEADS, 8):
        heads = range(first, first + 8)
        for head in heads:
            at = slice(head * HEAD_DIM, (head + 1) * HEAD_DIM)
            raw[head] = dot_nt(qkv[0, :, at], qkv[1, :, at])
        for head in heads:
            scores = jnp.where(allowed, raw[head] * SCALE, -1e30)
            raised = jnp.exp(scores - jnp.max(scores, axis=-1, keepdims=True))
            chance = raised / jnp.sum(raised, axis=-1, keepdims=True)
            low[head] = chance.astype(LOW)
        block = pl.ds(first, 8)
        copies.append(start(low.at[block], probs_out.at[block], sems.at[9 + first // 8]))
        for head in range(first, first + 8, 2):
            made = []
            for one in (head, head + 1):
                made.append(dot(low[one], qkv[2, :, one * HEAD_DIM : (one + 1) * HEAD_DIM]))
            at = slice(head * HEAD_DIM, (head + 2) * HEAD_DIM)
            joined[:, at] = jnp.concatenate(made, axis=1).astype(LOW)
    copies.append(start(joined, joined_out, sems.at[28]))
    made = inputs + dot(joined[...], weights[lax.rem(7 - place[0, 1], 4)])
    hidden[...] = made
    copies.append(start(hidden, hidden_out, sems.at[13]))
    unit, _ = centered(made)
    second = (unit * norms[2:3, :] + norms[3:4, :]).astype(LOW)
    for part in range(4):
        rows = pl.ds(part * TOK, TOK)
        outgoing[rows, :] = dot(placed(slot[...], part), second).astype(LOW)
        copies.append(start(outgoing.at[rows, :], outgoing_out.at[rows, :], sems.at[14 + part]))
    for copy in copies:
        copy.wait()


def left_kernel(place, normed, joined, *refs):
    targets, held, turned, sems = refs[:4], refs[4], refs[5], refs[6]
    loads = [start(ref, held.at[i], sems.at[i]) for i, ref in enumerate((normed, joined))]
    for index, load in enumerate(loads):
        load.wait()
        turned[index] = held[index].T
    copies = []
    for index, target in enumerate(targets):
        kind = lax.div(lax.rem(place[0, 1] + index, 4), 3)
        copies.append(start(turned.at[kind], target, sems.at[2 + index]))
    for copy in copies:
        copy.wait()


def gelu_parts(pre):
    square = pre * pre
    turn = jnp.tanh(pre * (0.7978845608028654 + 0.035677408136300125 * square))
    half = 0.5 + 0.5 * turn
    slope = half + (0.5 - 0.5 * turn * turn) * (
        pre * (0.7978845608028654 + 0.10703222440890037 * square)
    )
    return pre * half, slope


def expert_kernel(rows_in, weight_own, weight_other, up_own, up_other, out, *refs):
    acts, flows, scratch = refs[:2], refs[2:4], refs[4:]
    rows, weight, up, act, flow, back, sems = scratch
    hidden = weight.shape[1]
    half = hidden // 2
    chunk = 1024
    parts = hidden // chunk

    def load(j):
        cols = pl.ds(j * chunk, chunk)
        at = pl.ds(j * chunk % half, chunk)
        weight_in, up_in = (weight_own, up_own) if j * chunk < half else (weight_other, up_other)
        return (
            start(weight_in.at[:, at], weight.at[:, cols], sems.at[1 + j]),
            start(up_in.at[:, at], up.at[:, cols], sems.at[1 + parts + j]),
        )

    rows_load = start(rows_in, rows, sems.at[0])
    loads = [load(0), load(1)]
    rows_load.wait()
    copies = []
    for j in range(parts):
        cols = slice(j * chunk, (j + 1) * chunk)
        if j + 2 < parts:
            loads.append(load(j + 2))
        for copy in loads[j]:
            copy.wait()
        value, slope = gelu_parts(dot(rows[...], weight[:, cols]))
        act[:, cols] = value.astype(LOW)
        flow[:, cols] = (up[:, cols].astype(FULL) * slope).astype(LOW)
        at = pl.ds(j * chunk, chunk)
        side = j * chunk // half
        target_at = pl.ds(j * chunk % half, chunk)
        for index, (source, targets) in enumerate(((act, acts), (flow, flows))):
            sem = sems.at[1 + 2 * parts + 2 * j + index]
            copies.append(start(source.at[:, at], targets[side].at[:, target_at], sem))
    for index in range(2):
        block = slice(index * 256, (index + 1) * 256)
        back[block, :] = dot_nt(flow[block, :], weight[...]).astype(LOW)
        at = pl.ds(index * 256, 256)
        copies.append(start(back.at[at, :], out.at[at, :], sems.at[1 + 4 * parts + index]))
    for copy in copies:
        copy.wait()


def result_kernel(act_own, act_other, weight_own, weight_other, out, act, weight, made, sems):
    sides = []
    for side, (act_in, weight_in) in enumerate(((act_own, weight_own), (act_other, weight_other))):
        sides.append(
            [
                start(act_in, act.at[side], sems.at[2 * side]),
                start(weight_in, weight.at[side], sems.at[2 * side + 1]),
            ]
        )
        if side == 0:
            for load in sides[0]:
                load.wait()
    made[...] = dot(act[0], weight[0])
    for load in sides[1]:
        load.wait()
    act[0, :, :WIDTH] = (made[...] + dot(act[1], weight[1])).astype(LOW)
    source = act.at[0, :, pl.ds(0, WIDTH)]
    start(source, out.at[:, pl.ds(STAR, WIDTH)], sems.at[4]).wait()


def weight_grad_kernel(by_rows, at, first, second, streamed_first, streamed_second, made, held, sems):
    half = first.shape[0]
    cols = pl.ds(at, held.shape[1])

    @pl.when(pl.program_id(0) == 0)
    def _():
        loads = [
            start(first.at[:, cols], held.at[pl.ds(0, half), :], sems.at[0]),
            start(second.at[:, cols], held.at[pl.ds(half, half), :], sems.at[1]),
        ]
        for load in loads:
            load.wait()

    streamed = jnp.concatenate([streamed_first[...], streamed_second[...]], axis=0)
    made[...] = dot_tn(streamed, held[...]) if by_rows else dot_tn(held[...], streamed)


def weight_grad_call(held, at, streamed, by_rows, tile=1024):
    rows, wide = streamed[0].shape
    width = WIDTH
    shape = (wide, width) if by_rows else (width, wide)
    block = (tile, width) if by_rows else (width, tile)
    return pl.pallas_call(
        functools.partial(weight_grad_kernel, by_rows, at),
        grid=(wide // tile,),
        in_specs=[HBM, HBM] + [pl.BlockSpec((rows, tile), lambda i: (0, i))] * 2,
        out_specs=pl.BlockSpec(block, (lambda i: (i, 0)) if by_rows else (lambda i: (0, i))),
        out_shape=jax.ShapeDtypeStruct(shape, FULL),
        scratch_shapes=[pltpu.VMEM((2 * rows, width), LOW), pltpu.SemaphoreType.DMA((2,))],
        compiler_params=pltpu.CompilerParams(
            dimension_semantics=("arbitrary",), vmem_limit_bytes=VMEM_BYTES
        ),
        cost_estimate=pl.CostEstimate(
            flops=4 * rows * wide * width, bytes_accessed=14 << 20, transcendentals=0
        ),
        name="weight_grad",
    )(*held, *streamed)


def attend_back_kernel(
    place, by_row, lengths, norms, back, hidden, grad, shares, other_shares, *refs
):
    received, (qkv_in, probs_in, grad_out) = refs[:6], refs[6:9]
    parts_out, gains, scratch = refs[9:13], refs[13], refs[14:]
    back_in, hidden_in, grad_in, weight, qkv, probs, total, above, flow, *scratch = scratch
    raw, turned, pulled, low, low_turned, chance_turned, sems = scratch
    back_loads = []
    for part in range(2):
        at = pl.ds(part * 2 * TOK, 2 * TOK)
        back_loads.append(start(back.at[at, :], back_in.at[at, :], sems.at[part]))
    hidden_load = start(hidden, hidden_in, sems.at[4])
    grad_load = start(grad, grad_in, sems.at[5])
    sources = as_sources(shares, other_shares, received)
    weight_loads = load_one(sources, place, 3, weight, sems, 15)
    qkv_load = start(qkv_in, qkv, sems.at[7])
    probs_load = start(probs_in, probs, sems.at[8])
    upstream = jnp.zeros((TOK, WIDTH), FULL)
    for part in range(4):
        if part % 2 == 0:
            back_loads[part // 2].wait()
        rows = back_in[part * TOK : (part + 1) * TOK, :]
        upstream = upstream + dot(placed_rows(by_row[...], part), rows)
    hidden_load.wait()
    grad_load.wait()
    unit, inverse = centered(hidden_in[...])
    made = grad_in[...].astype(FULL) + norm_pull(upstream, unit, inverse, norms[2:3, :])
    total[...] = made
    copies = [start(total, grad_out, sems.at[9])]
    flow[:, FLOW:] = made.astype(LOW)
    gains[...] = jnp.zeros(gains.shape, FULL)
    gains[2:3, :] = jnp.sum(upstream * unit, axis=0, keepdims=True)
    gains[3:4, :] = jnp.sum(upstream, axis=0, keepdims=True)
    for load in weight_loads:
        load.wait()
    above[...] = dot_nt(flow[:, FLOW:], weight[...]).astype(LOW)
    qkv_load.wait()
    probs_load.wait()

    def head_of(part, head):
        return qkv[part, :, head * HEAD_DIM : (head + 1) * HEAD_DIM]

    def above_of(head):
        return above[:, head * HEAD_DIM : (head + 1) * HEAD_DIM]

    def store(part, first, pieces):
        at = part * WIDTH + first * HEAD_DIM
        flow[:, at : at + 2 * HEAD_DIM] = jnp.concatenate(pieces, axis=1).astype(LOW)

    key_at = lax.broadcasted_iota(jnp.int32, (TOK, TOK), 0)
    query_at = lax.broadcasted_iota(jnp.int32, (TOK, TOK), 1)
    allowed = same_document(lengths, query_at, key_at) & (key_at <= query_at)
    for first in range(0, HEADS, 8):
        heads = range(first, first + 8)
        pairs = range(first, first + 8, 2)
        for head in heads:
            raw[head] = dot_nt(above_of(head), head_of(2, head))
            turned[head] = dot_nt(head_of(1, head), head_of(0, head))
            pulled[head] = dot_nt(head_of(2, head), above_of(head))
        for head in heads:
            chance = probs[head].astype(FULL)
            taken = jnp.sum(chance * raw[head], axis=-1, keepdims=True)
            low[head] = (chance * (raw[head] - taken)).astype(LOW)
        for head in heads:
            scores = jnp.where(allowed, turned[head] * SCALE, -1e30)
            raised = jnp.exp(scores - jnp.max(scores, axis=0, keepdims=True))
            chance = raised / jnp.sum(raised, axis=0, keepdims=True)
            chance_turned[head] = chance.astype(LOW)
            taken = jnp.sum(chance * pulled[head], axis=0, keepdims=True)
            low_turned[head] = (chance * (pulled[head] - taken)).astype(LOW)
        for head in pairs:
            both = (head, head + 1)
            store(2, head, [dot(chance_turned[h], above_of(h)) for h in both])
            store(0, head, [dot(low[h], head_of(1, h)) * SCALE for h in both])
            store(1, head, [dot(low_turned[h], head_of(0, h)) * SCALE for h in both])
    for index, target in enumerate(parts_out):
        source = flow.at[:, lanes(lax.rem(place[0, 1] + index, 4) * WIDTH, WIDTH)]
        copies.append(start(source, target, sems.at[10 + index]))
    for copy in copies:
        copy.wait()


def weights_kernel(place, *refs):
    lefts, flows, shares, other_shares, gains_in = refs[:4], refs[4:8], *refs[8:11]
    mine, theirs, left, right, weight, made, gains, sems = refs[11:]
    rep, colour = place[0, 0], place[0, 1]
    loads = []
    for index in range(4):
        rows = pl.ds(index * TOK, TOK)
        loads.append(start(lefts[index], left.at[:, rows], sems.at[index]))
        loads.append(start(flows[index], right.at[rows, :], sems.at[4 + index]))
    small = [start(gains_in, gains, sems.at[8])]
    for side, ref in enumerate((shares, other_shares)):
        rows = lanes((rep if side == 0 else 1 - rep) * HALF, HALF)
        source = ref.at[:, pl.ds(0, WIDTH)]
        small.append(start(source, weight.at[rows, :], sems.at[9 + side]))
        source, target = ref.at[:, pl.ds(WIDTH, 128)], made.at[rows, pl.ds(WIDTH, 128)]
        small.append(start(source, target, sems.at[11 + side]))
    for load in loads:
        load.wait()
    total = jnp.sum(right[...].astype(FULL), axis=0, keepdims=True)
    projects = colour < 3
    copies = []
    for side, (half, target) in enumerate(((1 - rep, theirs), (rep, mine))):
        rows = lanes(half * HALF, HALF)
        value = dot(left[rows, :], right[...])
        made[rows, :WIDTH] = value.astype(LOW)
        if side == 0:
            for load in small:
                load.wait()
            columns = jnp.concatenate([gains[...], jnp.zeros((TOK - 8, WIDTH), FULL)], axis=0)
        weight_half = weight[rows, :].astype(FULL)
        params = made[rows, WIDTH:].astype(FULL)
        bias = jnp.sum(weight_half * total, axis=1, keepdims=True)
        gain = jnp.sum(weight_half * value, axis=1, keepdims=True)
        gain = (gain - params[:, 1:2] * bias) / params[:, 0:1]
        turned = jnp.where(half == 0, columns[:, :HALF], columns[:, HALF:]).T
        lane_at = lax.broadcasted_iota(jnp.int32, (HALF, 128), 1)
        first = jnp.where(projects, gain, 0.0)
        second = jnp.where(projects, bias, 0.0)
        tail = jnp.where(lane_at == 0, first, jnp.where(lane_at == 1, second, turned))
        made[rows, WIDTH:] = tail.astype(LOW)
        copies.append(start(made.at[rows, :], target, sems.at[13 + side]))
    for copy in copies:
        copy.wait()


def input_kernel(place, norms, tokens, hidden_grad, shares, other_shares, *refs):
    received, flows, made_out, scratch = refs[:6], refs[6:10], refs[10], refs[11:]
    tokens_in, grad_in, flow, weights, made, sems = scratch
    loads = []
    for index, pair in enumerate(as_sources(shares, other_shares, received)):
        loads.append([start(flows[index], flow.at[index], sems.at[4 + index])])
        for side, half in enumerate((place[0, 0], 1 - place[0, 0])):
            target = weights.at[index, lanes(half * HALF, HALF), :]
            loads[index].append(start(pair[side], target, sems.at[8 + 2 * index + side]))
    small = [start(tokens, tokens_in, sems.at[0]), start(hidden_grad, grad_in, sems.at[1])]
    upstream = jnp.zeros((TOK, WIDTH), FULL)
    for index in range(4):
        for load in loads[index]:
            load.wait()
        projects = lax.rem(place[0, 1] + index, 4) < 3
        pulled = dot_nt(flow[index], weights[index])
        upstream = upstream + jnp.where(projects, pulled, 0.0)
    for load in small:
        load.wait()
    unit, inverse = centered(tokens_in[...].astype(FULL))
    made[...] = grad_in[...] + norm_pull(upstream, unit, inverse, norms[0:1, :])
    start(made, made_out, sems.at[3]).wait()


def reduce_kernel(by_row, pieces, hidden, query, key, value, output, result, *refs):
    norms, held, hidden_in, sems = refs[:4], *refs[4:]
    hidden_load = start(hidden, hidden_in, sems.at[4])
    loads = []
    for part in range(4):
        rows = pl.ds(part * TOK, TOK)
        loads.append(start(pieces.at[rows, :], held.at[rows, :], sems.at[part]))
    sums = [jnp.zeros((8, WIDTH), FULL) for _ in range(4)]
    tail = jnp.zeros((8, 128), FULL)
    hidden_load.wait()
    made = hidden_in[...]
    for part in range(4):
        loads[part].wait()
        for pair in range(8):
            at = part * TOK + pair * 16
            rows = held[at : at + 16, :STAR].astype(FULL)
            for side in range(2):
                index = part * 16 + pair * 2 + side
                y, x, z = index // 16, index // 4 % 4, index % 4
                colour = (x + 2 * y - z) % 4
                piece = rows[side * 8 : (side + 1) * 8, :]
                sums[colour] = sums[colour] + piece[:, :WIDTH]
                tail = tail + piece[:, WIDTH:]
        at = slice(part * TOK, (part + 1) * TOK)
        made = made + dot(placed_rows(by_row[...], part), held[at, STAR:])
    result[...] = made.astype(LOW)
    for ref, total in zip((query, key, value, output), sums):
        ref[...] = total
    tail = jnp.concatenate([tail, jnp.zeros((TOK - 8, 128), FULL)], axis=0).T
    for index, norm in enumerate(norms):
        norm[...] = tail[index : index + 1, :8]


def tied(*values):
    return lax.optimization_barrier(values)


def per_device(
    tokens,
    hash_ids,
    doc_lengths,
    w_query,
    w_key,
    w_value,
    w_output,
    norm1_gain,
    norm1_bias,
    norm2_gain,
    norm2_bias,
    expert_in,
    expert_out,
    load_average,
    out_grad,
):
    experts = load_average.shape[0]
    groups = lax.axis_size("exp")
    devices = 2 * groups
    rep = lax.axis_index("rep")
    at = lax.axis_index("exp")
    y, x, z = lax.div(at, LINE * LINE), lax.rem(lax.div(at, LINE), LINE), lax.rem(at, LINE)
    colour = lax.rem(x + 2 * y + 3 * z, 4)
    place = jnp.stack([rep, colour]).astype(jnp.int32).reshape(1, 2)
    weight_in, weight_out = expert_in[0], expert_out[0]
    hidden = weight_in.shape[1]

    norm_params = jnp.concatenate([norm1_gain, norm1_bias, norm2_gain, norm2_bias]).reshape(1, 32)
    ids_row = hash_ids.reshape(1, TOK)
    (packed,) = kernel_call(
        pack_kernel,
        [VMEM] + [HBM] * 5,
        [((SLOTS, STAR), LOW, HBM)],
        scratch=[
            ((1, TOK), jnp.int32),
            ((4, 8, WIDTH), LOW),
            ((4, 32, STAR), LOW),
        ],
        copies=22,
        moved=3 << 20,
        name="pack",
    )(norm_params, ids_row, w_query, w_key, w_value, w_output)
    packed, ids_row = tied(packed, ids_row)
    laid, slot, by_row = kernel_call(
        grad_kernel,
        [HBM] * 2,
        [
            ((SLOTS, WIDTH), LOW, HBM),
            ((1, TOK), jnp.int32, VMEM),
            ((TOK, TOK), jnp.int32, VMEM),
        ],
        scratch=[((1, TOK), jnp.int32), ((TOK, WIDTH), LOW), ((SLOTS, WIDTH), LOW)],
        copies=6,
        flops=2 * SLOTS * TOK * WIDTH,
        moved=2 << 20,
        name="grad_rows",
    )(ids_row, out_grad)
    packed, first, second = tied(packed, weight_in, weight_out)
    shares = exchange(packed.reshape(groups, 8, STAR)).reshape(SLOTS, STAR)
    weight_in_other, weight_out_other = swap(first), swap(second)
    shares, place, weight_in_other, weight_out_other = tied(
        shares, place, weight_in_other, weight_out_other
    )
    received = [between(shares, ways, True) for ways in WAYS]
    other_shares = swap(shares)
    laid, *received = tied(laid, *received)
    grad_rows = exchange(laid.reshape(groups, CAPACITY, WIDTH)).reshape(SLOTS, WIDTH)
    received = [one for part in received for one in (part, swap(part))]

    def send(rows):
        return exchange(rows.reshape(groups, CAPACITY, WIDTH)).reshape(SLOTS, WIDTH)

    outgoing, hidden_one, qkv, probs, joined, normed, norms, extra = kernel_call(
        attend_kernel,
        [SMEM, VMEM, SMEM] + [HBM] * 9,
        [
            ((SLOTS, WIDTH), LOW, HBM),
            ((TOK, WIDTH), FULL, HBM),
            ((3, TOK, WIDTH), LOW, HBM),
            ((HEADS, TOK, TOK), LOW, HBM),
            ((TOK, WIDTH), LOW, HBM),
            ((TOK, WIDTH), LOW, HBM),
            ((8, WIDTH), FULL, HBM),
            ((WIDTH, 128), LOW, HBM),
        ],
        scratch=[
            ((TOK, WIDTH), LOW),
            ((WIDTH, 128), LOW),
            ((4, WIDTH, WIDTH), LOW),
            ((8, WIDTH), FULL),
            ((TOK, WIDTH), LOW),
            ((4, TOK, WIDTH), LOW),
            ((HEADS, TOK, TOK), FULL),
            ((HEADS, TOK, TOK), LOW),
            ((TOK, WIDTH), LOW),
            ((TOK, WIDTH), FULL),
            ((SLOTS, WIDTH), LOW),
        ],
        copies=32,
        flops=2 * TOK * WIDTH * 5000,
        moved=12 << 20,
        name="attend",
    )(place, slot, doc_lengths, shares, other_shares, *received, tokens)

    lefts = kernel_call(
        left_kernel,
        [SMEM] + [HBM] * 2,
        [((WIDTH, TOK), LOW, HBM)] * 4,
        scratch=[((2, TOK, WIDTH), LOW), ((2, WIDTH, TOK), LOW)],
        copies=6,
        moved=2 << 20,
        name="left",
    )(place, normed, joined)
    outgoing, *lefts = tied(outgoing, *lefts)

    up_own = dot_nt(grad_rows, weight_out).astype(LOW)
    up_other = dot_nt(grad_rows, weight_out_other).astype(LOW)
    rows, up_own, up_other = tied(send(outgoing), up_own, up_other)

    back_rows, *acts_flows = kernel_call(
        expert_kernel,
        [HBM] * 5,
        [
            ((SLOTS, WIDTH), LOW, HBM),
        ]
        + [((SLOTS, hidden), LOW, HBM)] * 4,
        scratch=[
            ((SLOTS, WIDTH), LOW),
            ((WIDTH, 2 * hidden), LOW),
            ((SLOTS, 2 * hidden), LOW),
            ((SLOTS, 2 * hidden), LOW),
            ((SLOTS, 2 * hidden), LOW),
            ((SLOTS, WIDTH), LOW),
        ],
        copies=3 + 8 * (hidden // 512),
        flops=8 * SLOTS * WIDTH * hidden,
        moved=24 << 20,
        name="expert",
    )(rows, weight_in, weight_in_other, up_own, up_other)
    act, act_theirs, flow, flow_theirs = acts_flows
    far_lefts = [between(left, ways, False) for left, ways in zip(lefts[1:], WAYS)]
    lefts = [lefts[0]] + far_lefts
    back = send(back_rows)
    (result,) = kernel_call(
        result_kernel,
        [HBM] * 4,
        [((SLOTS, LAST), LOW, HBM)],
        scratch=[
            ((2, SLOTS, hidden), LOW),
            ((2, hidden, WIDTH), LOW),
            ((SLOTS, WIDTH), FULL),
        ],
        copies=5,
        flops=4 * SLOTS * hidden * WIDTH,
        moved=14 << 20,
        name="result",
    )(act, act_theirs, weight_out, weight_out_other)
    act_other, flow_other = swap(act_theirs), swap(flow_theirs)
    back, result, act_other, flow_other, *lefts = tied(
        back, result, act_other, flow_other, *lefts
    )

    hidden_grad, *parts, gains = kernel_call(
        attend_back_kernel,
        [SMEM, VMEM, SMEM, VMEM] + [HBM] * 13,
        [
            ((TOK, WIDTH), FULL, HBM),
        ]
        + [((TOK, WIDTH), LOW, HBM)] * 4
        + [
            ((8, WIDTH), FULL, VMEM),
        ],
        scratch=[
            ((SLOTS, WIDTH), LOW),
            ((TOK, WIDTH), FULL),
            ((TOK, WIDTH), LOW),
            ((WIDTH, WIDTH), LOW),
            ((3, TOK, WIDTH), LOW),
            ((HEADS, TOK, TOK), LOW),
            ((TOK, WIDTH), FULL),
            ((TOK, WIDTH), LOW),
            ((TOK, ALL), LOW),
            ((HEADS, TOK, TOK), FULL),
            ((HEADS, TOK, TOK), FULL),
            ((HEADS, TOK, TOK), FULL),
            ((HEADS, TOK, TOK), LOW),
            ((HEADS, TOK, TOK), LOW),
            ((HEADS, TOK, TOK), LOW),
        ],
        copies=19,
        flops=2 * TOK * WIDTH * 3000,
        moved=8 << 20,
        name="attend_back",
    )(
        place,
        by_row,
        doc_lengths,
        norms,
        back,
        hidden_one,
        out_grad,
        shares,
        other_shares,
        *received,
        qkv,
        probs,
    )
    own_parts = parts
    parts = [parts[0]] + [between(part, ways, False) for part, ways in zip(parts[1:], WAYS)]
    mine, theirs = kernel_call(
        weights_kernel,
        [SMEM] + [HBM] * 11,
        [((HALF, STAR), LOW, HBM)] * 2,
        scratch=[
            ((WIDTH, 4 * TOK), LOW),
            ((4 * TOK, WIDTH), LOW),
            ((WIDTH, WIDTH), LOW),
            ((WIDTH, STAR), LOW),
            ((8, WIDTH), FULL),
        ],
        copies=15,
        flops=8 * TOK * WIDTH * WIDTH,
        moved=8 << 20,
        name="weights",
    )(place, *lefts, *parts, shares, other_shares, gains)
    summed = (mine.astype(FULL) + swap(theirs).astype(FULL)).astype(LOW)
    weight_part = lax.dynamic_update_slice(result, summed, (0, 0))
    pieces = exchange(weight_part.reshape(groups, 8, LAST)).reshape(SLOTS, LAST)

    act, flow, rows, grad_rows, *own_parts, _ = tied(
        act, flow, rows, grad_rows, *own_parts, weight_part
    )
    rows_other, grad_other = swap(rows), swap(grad_rows)
    out_weight_grad = weight_grad_call((grad_rows, grad_other), 0, (act, act_other), True)
    in_weight_grad = weight_grad_call((rows, rows_other), 0, (flow, flow_other), False)
    (input_grad,) = kernel_call(
        input_kernel,
        [SMEM, VMEM] + [HBM] * 14,
        [((TOK, WIDTH), FULL, HBM)],
        scratch=[
            ((TOK, WIDTH), LOW),
            ((TOK, WIDTH), FULL),
            ((4, TOK, WIDTH), LOW),
            ((4, WIDTH, WIDTH), LOW),
            ((TOK, WIDTH), FULL),
        ],
        copies=20,
        flops=2 * TOK * WIDTH * FLOW,
        moved=8 << 20,
        name="input_grad",
    )(place, norms, tokens, hidden_grad, shares, other_shares, *received, *own_parts)
    tails = extra[:, 64:].reshape(devices, 8, experts)[:, 0]
    counts = jnp.sum(tails.astype(FULL), axis=0)
    new_average = 0.7 * load_average + 0.3 * counts
    counts = counts.astype(jnp.int32)
    pieces, out_weight_grad, in_weight_grad, input_grad, counts, new_average = tied(
        pieces, out_weight_grad, in_weight_grad, input_grad, counts, new_average
    )
    *grads, output, gain_one, bias_one, gain_two, bias_two = kernel_call(
        reduce_kernel,
        [VMEM, HBM, HBM],
        [((8, WIDTH), FULL, VMEM)] * 4
        + [((TOK, WIDTH), LOW, VMEM)]
        + [((1, 8), FULL, VMEM)] * 4,
        scratch=[((SLOTS, LAST), LOW), ((TOK, WIDTH), FULL)],
        copies=5,
        moved=5 << 20,
        name="reduce",
    )(by_row, pieces, hidden_one)
    return (
        output,
        input_grad,
        *grads,
        gain_one.reshape(8),
        bias_one.reshape(8),
        gain_two.reshape(8),
        bias_two.reshape(8),
        in_weight_grad[None],
        out_weight_grad[None],
        counts,
        new_average,
    )


def solution(mesh):
    rows = P(("rep", "exp"), None)
    vector = P(("rep", "exp"))
    return jax.shard_map(
        per_device,
        mesh=mesh,
        in_specs=(rows,) * 7
        + (vector,) * 4
        + (P("exp", None, "rep"), P("exp", "rep", None), P(), rows),
        out_specs=(rows,) * 6
        + (vector,) * 4
        + (P("exp", None, "rep"), P("exp", "rep", None), P(), P()),
        check_vma=False,
    )
```
